128 devices in a mesh: slab: 8 (over y, core), patch: 16 (over x, z).
Axes of the slice: x: 4, y: 4, z: 4, core: 2. Of those that a mesh axis runs over, the one named last changes fastest.
Arguments:
- coarse: float32 [5, 128, 128, 128], P(None, 'slab', 'patch'), may hold values from -1.2 to 7.7, as said below
- fine: float32 [5, 256, 32, 1024], P(None, ('slab', 'patch')), may hold values from -1.2 to 7.7, as said below
- columns: int32 [32, 2], replicated, may hold values from 0 to 5, as said below
- patch_ids: int32 [8, 32], P('slab'), may hold values from 0 to 31, each once within a row
Outputs:
- coarse_out: float32 [5, 128, 128, 128], P(None, 'slab', 'patch')
- fine_out: float32 [5, 256, 32, 1024], P(None, ('slab', 'patch'))
The draws below stay inside these ranges and needn't reach their ends.
Inputs may be any that keep to these rules, and one draw needn't show every extreme that they name: `coarse`: conserved variables of states with density and pressure between 0.5 and 2 and velocity components between -0.6 and 1.4. `fine`: conserved variables of states with density and pressure between 0.5 and 2 and velocity components between -0.6 and 1.4. `columns`: 32 distinct pairs (gy, gz) with gy below 6 and gz below 6. `patch_ids`: each row is a permutation of the 32 patch numbers of a slab.
All inputs are finite; a program needn't handle non-finite values.
Results may differ from the reference program's by a relative error of at most 0.00005.
Values sent between devices are 32-bit elements; how exact they have to be, the bound alone decides.
A program may use at most 320 MiB of HBM per device.

```python
import math
import jax
import jax.numpy as jnp
from jax import lax

P_SIZE = 32
LX = 1
GY = 6
GZ = 6
PYZ = 32
H = 16
SLOTS = 32
PATCHES = 256
NXC = 128
NZC = 128
NYC = 128
N_SLAB = 8


def conserved(key, extents):
    keys = jax.random.split(key, 5)
    density = jnp.exp(jax.random.uniform(keys[0], extents, minval=math.log(0.5), maxval=math.log(2.0)))
    pressure = jnp.exp(jax.random.uniform(keys[1], extents, minval=math.log(0.5), maxval=math.log(2.0)))
    velocity_x = jax.random.uniform(keys[2], extents, minval=-0.6, maxval=0.6)
    velocity_y = jax.random.uniform(keys[3], extents, minval=-0.6, maxval=0.6)
    velocity_z = jax.random.uniform(keys[4], extents, minval=-0.6, maxval=0.6)
    energy = pressure / 0.4 + 0.5 * density * (velocity_x * velocity_x + velocity_y * velocity_y + velocity_z * velocity_z)
    return jnp.stack([density, density * velocity_x, density * velocity_y, density * velocity_z, energy]).astype(jnp.float32)


def draw_coarse(key, part):
    return conserved(jax.random.fold_in(key, 11), (NXC, NZC, NYC))


def draw_fine(key, part):
    return conserved(jax.random.fold_in(key, 23), (PATCHES, P_SIZE, P_SIZE * P_SIZE))


def draw_columns(key, part):
    chosen = jax.random.permutation(jax.random.fold_in(key, 37), GY * GZ)[:PYZ]
    return jnp.stack([chosen % GY, chosen // GY], axis=1).astype(jnp.int32)


def setup_inputs(seed: int = 0) -> dict:
    seeds = jax.random.split(jax.random.key(seed), 5)
    return {
        "coarse": draw_coarse(jax.random.fold_in(seeds[4], 71), 0),
        "fine": draw_fine(jax.random.fold_in(seeds[4], 71), 0),
        "columns": draw_columns(jax.random.fold_in(seeds[4], 71), 0),
        "patch_ids": jax.vmap(lambda own: jax.random.permutation(own, SLOTS))(jax.random.split(seeds[3], N_SLAB)).reshape((N_SLAB, SLOTS)).astype(jnp.int32),
    }


heat_ratio = 1.4
fine_rate = 0.1
coarse_rate = 0.05

def euler_flux(fields, normal_axis):
    density = fields[0]
    momentum = fields[1:4]
    energy = fields[4]
    velocity = momentum / density
    pressure = (heat_ratio - 1.0) * (energy - 0.5 * lax.optimization_barrier(jnp.sum(momentum * velocity, axis=0)))
    normal_speed = velocity[normal_axis]
    components = [momentum[normal_axis], momentum[0] * normal_speed, momentum[1] * normal_speed, momentum[2] * normal_speed, (energy + pressure) * normal_speed]
    components[1 + normal_axis] = components[1 + normal_axis] + pressure
    signal = jnp.abs(normal_speed) + jnp.sqrt(heat_ratio * pressure / density)
    return (jnp.stack(components), signal)

def rusanov(left_side, right_side, normal_axis):
    left_flux, left_signal = euler_flux(left_side, normal_axis)
    right_flux, right_signal = euler_flux(right_side, normal_axis)
    return 0.5 * (left_flux + right_flux) - 0.5 * jnp.maximum(left_signal, right_signal) * (right_side - left_side)

def advance(fields, ghosts):
    x_low, x_high, z_low, z_high, y_low, y_high = ghosts
    along_x = jnp.concatenate([x_low[:, :, None], fields, x_high[:, :, None]], axis=2)
    flux_x = rusanov(along_x[:, :, :-1], along_x[:, :, 1:], 0)
    along_z = jnp.concatenate([z_low[:, :, :, None], fields, z_high[:, :, :, None]], axis=3)
    flux_z = rusanov(along_z[:, :, :, :-1], along_z[:, :, :, 1:], 2)
    along_y = jnp.concatenate([y_low[..., None], fields, y_high[..., None]], axis=4)
    flux_y = rusanov(along_y[..., :-1], along_y[..., 1:], 1)
    change = flux_x[:, :, 1:] - flux_x[:, :, :-1] + (flux_z[:, :, :, 1:] - flux_z[:, :, :, :-1]) + (flux_y[..., 1:] - flux_y[..., :-1])
    updated = fields - fine_rate * change
    return (updated, (flux_y[..., 0], flux_y[..., -1], flux_z[:, :, :, 0], flux_z[:, :, :, -1]))

def pair_mean(face_cells):
    extents = face_cells.shape
    return face_cells.reshape(extents[0], extents[1], extents[2] // 2, 2, extents[3] // 2, 2).mean(axis=(3, 5))

def cell_mean(fields):
    extents = fields.shape
    return fields.reshape(extents[0], extents[1], extents[2] // 2, 2, extents[3] // 2, 2, extents[4] // 2, 2).mean(axis=(3, 5, 7))

def upsample(face_cells):
    return jnp.repeat(jnp.repeat(face_cells, 2, axis=-2), 2, axis=-1)

def onehot(indices, extent):
    return (indices[:, None] == jnp.arange(extent, dtype=jnp.int32)[None, :]).astype(jnp.float32)

def neighbours(columns, step_y, step_z):
    matches = (columns[None, :, 0] == columns[:, None, 0] + step_y) & (columns[None, :, 1] == columns[:, None, 1] + step_z)
    present = jnp.any(matches, axis=1)
    partner = lax.optimization_barrier(jnp.sum(jnp.where(matches, jnp.arange(columns.shape[0], dtype=jnp.int32)[None, :], 0), axis=1)).astype(jnp.int32)
    return (present, partner)

def block_targets(column_y, column_z):
    grid_width = GY + 2
    return ((column_z + 1) * grid_width + column_y + 1, (column_z + 1) * grid_width + column_y, (column_z + 1) * grid_width + column_y + 2, column_z * grid_width + column_y + 1, (column_z + 2) * grid_width + column_y + 1)

def cover_mask(columns):
    centre = block_targets(columns[:, 0], columns[:, 1])[0]
    occupied = lax.optimization_barrier(jnp.sum(onehot(centre, (GZ + 2) * (GY + 2)), axis=0))
    return jnp.repeat(jnp.repeat(occupied.reshape(GZ + 2, GY + 2), H, axis=0), H, axis=1)

def block_form(slab):
    layer_depth = slab.shape[1] // H
    shaped = slab.reshape(5, layer_depth, H, GZ + 2, H, GY + 2, H).transpose(0, 1, 2, 4, 6, 3, 5)
    return shaped.reshape(5, layer_depth, H, H, H, (GZ + 2) * (GY + 2))

def slab_form(blocks):
    layer_depth = blocks.shape[1]
    shaped = blocks.reshape(5, layer_depth, H, H, H, GZ + 2, GY + 2).transpose(0, 1, 2, 5, 3, 6, 4)
    return shaped.reshape(5, layer_depth * H, (GZ + 2) * H, (GY + 2) * H)

def reorder(slab_fields, order_index):
    return jnp.take(slab_fields, order_index, axis=1)

def arrange(values):
    return jnp.moveaxis(jnp.moveaxis(values, 0, 1), 2, -1)

def reference(coarse, fine, columns, patch_ids):
    layers = N_SLAB * LX
    slot_count = LX * PYZ
    slot_range = jnp.arange(slot_count, dtype=jnp.int32)
    inverse = lax.optimization_barrier(jnp.sum(jnp.where(patch_ids[:, :, None] == slot_range[None, None, :], slot_range[None, :, None], 0), axis=1)).astype(jnp.int32)
    grouped = fine.reshape(5, N_SLAB, slot_count, P_SIZE, P_SIZE, P_SIZE)
    ordered = jax.vmap(reorder, in_axes=(1, 0), out_axes=1)(grouped, inverse)
    fields_all = ordered.reshape(5, layers, PYZ, P_SIZE, P_SIZE, P_SIZE)
    x_lower = jnp.concatenate([fields_all[:, :1, :, 0], fields_all[:, :-1, :, P_SIZE - 1]], axis=1)
    x_upper = jnp.concatenate([fields_all[:, 1:, :, 0], fields_all[:, -1:, :, P_SIZE - 1]], axis=1)
    column_y = columns[:, 0]
    column_z = columns[:, 1]
    centre, below_y, above_y, below_z, above_z = block_targets(column_y, column_z)
    blocks = block_form(coarse)

    def inject(portion, target):
        return upsample(jnp.moveaxis(jnp.take(portion, target, axis=4), 4, 2))

    def blend_faces(step_y, step_z, neighbour_face, coarse_face):
        present, partner = neighbours(columns, step_y, step_z)
        return jnp.where(present[None, None, :, None, None], jnp.take(neighbour_face, partner, axis=2), coarse_face)
    y_lower_ghost = blend_faces(-1, 0, fields_all[..., P_SIZE - 1], inject(blocks[:, :, :, :, H - 1], below_y))
    y_upper_ghost = blend_faces(1, 0, fields_all[..., 0], inject(blocks[:, :, :, :, 0], above_y))
    z_lower_ghost = blend_faces(0, -1, fields_all[:, :, :, :, P_SIZE - 1], inject(blocks[:, :, :, H - 1], below_z))
    z_upper_ghost = blend_faces(0, 1, fields_all[:, :, :, :, 0], inject(blocks[:, :, :, 0], above_z))

    def layer_step(member):
        updated, boundary = advance(member[0], member[1:])
        return (updated, cell_mean(updated), tuple((pair_mean(face_cells) for face_cells in boundary)))
    members = tuple((jnp.moveaxis(source, 1, 0) for source in (fields_all, x_lower, x_upper, z_lower_ghost, z_upper_ghost, y_lower_ghost, y_upper_ghost)))
    updated, averaged, boundary = lax.map(layer_step, members)
    by_number = jnp.moveaxis(updated, 0, 1).reshape(5, N_SLAB, slot_count, P_SIZE, P_SIZE, P_SIZE)
    fine_out = jax.vmap(reorder, in_axes=(1, 0), out_axes=1)(by_number, patch_ids).reshape(5, N_SLAB * slot_count, P_SIZE, P_SIZE * P_SIZE)

    def absent_mask(step_y, step_z):
        return 1.0 - neighbours(columns, step_y, step_z)[0].astype(jnp.float32)
    y_lower = -coarse_rate * arrange(boundary[0]) * absent_mask(-1, 0)
    y_upper = coarse_rate * arrange(boundary[1]) * absent_mask(1, 0)
    z_lower = -coarse_rate * arrange(boundary[2]) * absent_mask(0, -1)
    z_upper = coarse_rate * arrange(boundary[3]) * absent_mask(0, 1)
    first_row = (jnp.arange(H) == 0).astype(jnp.float32)
    last_row = (jnp.arange(H) == H - 1).astype(jnp.float32)
    nblocks = (GZ + 2) * (GY + 2)
    totals = jnp.zeros((5, layers, H, H, H, nblocks), jnp.float32)
    totals = totals.at[..., centre].add(arrange(averaged))
    totals = totals.at[..., below_y].add(y_lower[:, :, :, :, None, :] * last_row[:, None])
    totals = totals.at[..., above_y].add(y_upper[:, :, :, :, None, :] * first_row[:, None])
    totals = totals.at[..., below_z].add(z_lower[:, :, :, None, :, :] * last_row[:, None, None])
    totals = totals.at[..., above_z].add(z_upper[:, :, :, None, :, :] * first_row[:, None, None])
    contrib = slab_form(totals)
    covered = cover_mask(columns)
    along_x = jnp.concatenate([coarse[:, :1], coarse, coarse[:, -1:]], axis=1)
    along_z = jnp.concatenate([coarse[:, :, :1], coarse, coarse[:, :, -1:]], axis=2)
    along_y = jnp.concatenate([coarse[..., :1], coarse, coarse[..., -1:]], axis=3)
    cover_z = jnp.pad(covered, ((1, 1), (0, 0)))
    cover_y = jnp.pad(covered, ((0, 0), (1, 1)))
    flux_x = rusanov(along_x[:, :-1], along_x[:, 1:], 0) * (1.0 - covered)
    flux_z = rusanov(along_z[:, :, :-1], along_z[:, :, 1:], 2) * ((1.0 - cover_z[:-1]) * (1.0 - cover_z[1:]))
    flux_y = rusanov(along_y[..., :-1], along_y[..., 1:], 1) * ((1.0 - cover_y[:, :-1]) * (1.0 - cover_y[:, 1:]))
    change = flux_x[:, 1:] - flux_x[:, :-1] + (flux_z[:, :, 1:] - flux_z[:, :, :-1]) + (flux_y[..., 1:] - flux_y[..., :-1])
    provisional = coarse - coarse_rate * change
    coarse_out = jnp.where(covered > 0, contrib, provisional + contrib)
    return (coarse_out, fine_out)
```

```python
import jax
import jax.numpy as jnp
from jax import lax
from jax.experimental import pallas as pl
from jax.experimental.pallas import tpu as pltpu
from jax.sharding import PartitionSpec as P

F32 = jnp.float32
BF16 = jnp.bfloat16
I32 = jnp.int32
MESH = pl.DeviceIdType.MESH
NS = 8
NP = 16
GOFF = 16


def iota(shape, dim):
    return lax.broadcasted_iota(I32, shape, dim)


def dot3(x, m):
    hi = x.astype(BF16)
    r = x - hi.astype(F32)
    mid = r.astype(BF16)
    lo = (r - mid.astype(F32)).astype(BF16)
    d = lambda a: jnp.dot(a, m, preferred_element_type=F32)
    return d(hi) + (d(mid) + d(lo))


def ones_where(c):
    return jnp.where(c, 1.0, 0.0).astype(BF16)


def state(q):
    r = 1.0 / q[0]
    p = 0.4 * (q[4] - 0.5 * ((q[1] * q[1] + q[2] * q[2] + q[3] * q[3]) * r))
    c = jnp.sqrt(1.4 * p * r)
    return r, p, c


def flux(q, s, d):
    r, p, c = s
    u = q[1 + d] * r
    f = [q[1 + d], q[1] * u, q[2] * u, q[3] * u, (q[4] + p) * u]
    f[1 + d] = f[1 + d] + p
    return f, jnp.abs(u) + c


def rusanov(ql, fl, al, qr, fr, ar):
    a = 0.5 * jnp.maximum(al, ar)
    return [0.5 * (fl[v] + fr[v]) - a * (qr[v] - ql[v]) for v in range(5)]


def pack_kernel(fine, coarse, ids, cols, yzp, xf, cp, rz, cx, tab, grid, ct):
    rank = lax.axis_index("patch")
    half = lax.rem(rank, 2)
    for i in range(96):
        grid[0, i] = jnp.int32(-1)

    def place(s, _):
        n = ids[0, s]
        gy = cols[n, 0]
        gz = cols[n, 1]
        tab[8, s] = gy
        tab[9, s] = gz
        grid[0, gy + 8 * gz + GOFF] = s
        return 0

    lax.fori_loop(0, 32, place, 0)

    def look(s, _):
        code = tab[8, s] + 8 * tab[9, s] + GOFF
        for g, step in enumerate((-1, 1, -8, 8)):
            q = grid[0, code + step]
            t = jnp.maximum(q, 0)
            tab[g, s] = (t >> 3) * 2 + (t & 1)
            tab[4 + g, s] = jnp.where(q < 0, -1, (t >> 1) & 3)
        return 0

    lax.fori_loop(0, 32, look, 0)
    k = iota((1024, 128), 0)
    c = iota((1024, 128), 1)
    g = c // 32
    i = lax.rem(c, 32)
    want = jnp.where(g == 0, 32 * i + 31, jnp.where(g == 1, 32 * i, jnp.where(g == 2, 992 + i, i)))
    sel = ones_where(k == want)
    for v in range(5):
        for p in range(2):
            yzp[p, v] = dot3(fine[v, p], sel)
    for d, row in ((0, 0), (1, 31)):
        for p in range(2):
            for v in range(5):
                for j in range(8):
                    xf[d, p * 5 + v, j : j + 1, :] = fine[v, p, row : row + 1, 128 * j : 128 * j + 128]
        sub = iota((8, 128), 0)
        tag = jnp.where(sub == 0, ids[0, 2 * rank], ids[0, 2 * rank + 1])
        xf[d, 10] = tag.astype(F32)
    for v in range(5):
        for z in range(8):
            ct[z, 16 * v : 16 * v + 16, :] = coarse[v, :, z, :]
    y = iota((128, 128), 0)
    k = iota((128, 128), 1) // 8
    plane = jnp.where(k < 6, 16 * (k + 1) - 1, jnp.where(k < 12, 16 * (k - 4), -1))
    sel = ones_where(y == plane)
    lane8 = lax.rem(iota((80, 128), 1), 8)
    acc = jnp.zeros((80, 128), F32)
    for z in range(8):
        acc = jnp.where(lane8 == z, dot3(ct[z], sel), acc)
    first = ct[0]
    last = ct[7]
    own = jnp.where(half == 0, first, last)
    for v in range(5):
        cut = slice(16 * v, 16 * v + 16)
        cp[v, 0] = acc[cut]
        cp[v, 1] = own[cut]
        rz[0, v] = first[cut]
        rz[1, v] = last[cut]
        cx[0, v] = coarse[v, 0]
        cx[1, v] = coarse[v, 15]


def ghost_kernel(yzp, xf, cp, cx, tab, ids, oyz, ox, oc, ocx, gx, bx, cz, syz, sx, sc, ss, rs, ls):
    s = lax.axis_index("slab")
    me = lax.axis_index("patch")
    x = me // 4
    z = lax.rem(me, 4)
    up = lax.rem(s + 1, NS)
    down = lax.rem(s + NS - 1, NS)
    xp = [lax.rem(x + d, 4) for d in range(4)]
    zp = [lax.rem(z + d, 4) for d in range(4)]
    barrier = pltpu.get_barrier_semaphore()
    for d in range(1, 4):
        pl.semaphore_signal(barrier, inc=1, device_id=(s, xp[d] * 4 + z), device_id_type=MESH)
        pl.semaphore_signal(barrier, inc=1, device_id=(s, x * 4 + zp[d]), device_id_type=MESH)
    for d in range(4):
        pl.semaphore_signal(barrier, inc=1, device_id=(up, x * 4 + zp[d]), device_id_type=MESH)
        pl.semaphore_signal(barrier, inc=1, device_id=(down, x * 4 + zp[d]), device_id_type=MESH)
    pl.semaphore_wait(barrier, 14)

    def send(k, src, dst, dev):
        c = pltpu.make_async_remote_copy(
            src_ref=src, dst_ref=dst, send_sem=ss.at[k], recv_sem=rs.at[k],
            device_id=dev, device_id_type=MESH,
        )
        c.start()
        return c

    one = []
    k = 0
    for d in range(1, 4):
        one.append(send(k, yzp, gx.at[pl.ds(2 * x, 2)], (s, xp[d] * 4 + z)))
        k += 1
    for d in range(4):
        one.append(send(k, xf.at[0], bx.at[1, z], (down, x * 4 + zp[d])))
        one.append(send(k + 1, xf.at[1], bx.at[0, z], (up, x * 4 + zp[d])))
        k += 2
    for d in range(1, 4):
        one.append(send(k, cp, cz.at[z], (s, x * 4 + zp[d])))
        k += 1
    one.append(send(k, cx.at[0], ocx.at[1], (down, me)))
    one.append(send(k + 1, cx.at[1], ocx.at[0], (up, me)))
    k += 2
    l0 = pltpu.make_async_copy(yzp, gx.at[pl.ds(2 * x, 2)], ls.at[0])
    l1 = pltpu.make_async_copy(cp, cz.at[z], ls.at[1])
    l0.start()
    l1.start()
    l0.wait()
    l1.wait()
    for c in one:
        c.wait()
    two = []
    lane = iota((5, 32, 128), 2) // 32
    for d in (1, 2, 3, 0):
        for p in range(2):
            slot = 2 * (x * 4 + zp[d]) + p
            got = [gx[tab[g, slot]] for g in range(4)]
            val = jnp.where(lane == 0, got[0], jnp.where(lane == 1, got[1], jnp.where(lane == 2, got[2], got[3])))
            if d:
                syz[d - 1, p] = val
            else:
                oyz[z, p] = val
        if d:
            two.append(send(k, syz.at[d - 1], oyz.at[z], (s, x * 4 + zp[d])))
            k += 1
    lane = iota((80, 128), 1)
    for d in (1, 2, 3, 0):
        for p in range(2):
            slot = 2 * (xp[d] * 4 + z) + p
            n = ids[0, slot].astype(F32)
            for way in range(2):
                acc = jnp.zeros((5, 8, 128), F32)
                for j in range(4):
                    for t in range(2):
                        hit = bx[way, j, 10, t : t + 1, :] == n
                        acc = jnp.where(hit[None], bx[way, j, 5 * t : 5 * t + 5], acc)
                if d:
                    sx[d - 1, p, way] = acc
                else:
                    ox[x, p, way] = acc
            gy = tab[8, slot]
            gz = tab[9, slot]
            a = 2 * ((gz + 1) & 1)
            b = 2 * (gz & 1)
            y0 = cz[a, :, 0].reshape(80, 128)
            y1 = cz[a + 1, :, 0].reshape(80, 128)
            z0 = cz[b + 1, :, 1].reshape(80, 128)
            z1 = cz[b, :, 1].reshape(80, 128)
            r0 = pltpu.roll(y0, (128 - 8 * gy) & 127, 1)
            r1 = pltpu.roll(y1, (136 - 8 * gy) & 127, 1)
            r2 = pltpu.roll(z0, (176 - 16 * gy) & 127, 1)
            r3 = pltpu.roll(z1, (192 - 16 * gy) & 127, 1)
            val = jnp.where(lane < 64, jnp.where((lane & 8) == 0, r0, r1), jnp.where(lane < 80, r2, r3))
            val = val.reshape(5, 16, 128)
            if d:
                sc[d - 1, p] = val
            else:
                oc[x, p] = val
        if d:
            two.append(send(k, sx.at[d - 1], ox.at[x], (s, xp[d] * 4 + z)))
            two.append(send(k + 1, sc.at[d - 1], oc.at[x], (s, xp[d] * 4 + z)))
            k += 2
    for c in two:
        c.wait()


def fine_kernel(fine, oyz, ox, oc, tab, out, av, ext, ghost, chg, fy, fz, xs, tmp):
    s = lax.axis_index("slab")
    me = lax.axis_index("patch")
    lane = iota((80, 128), 1)
    src = iota((128, 128), 0)
    dst = iota((128, 128), 1)
    g = dst // 32
    i = lax.rem(dst, 32) // 2
    base = jnp.where(g == 0, 0, jnp.where(g == 1, 48, jnp.where(g == 2, 64, 80)))
    spread = ones_where(src == base + i)
    src = iota((128, 1024), 0)
    dst = iota((128, 1024), 1)
    g = src // 32
    expand = ones_where(
        ((g == 0) & (dst == 32 * lax.rem(src, 32))) | ((g == 1) & (dst == 32 * lax.rem(src, 32) + 31))
    )
    src = iota((1024, 256), 0)
    dst = iota((1024, 256), 1)
    pair = ones_where((src // 64 == dst // 16) & (lax.rem(src, 32) // 2 == lax.rem(dst, 16)))
    src = iota((1024, 128), 0)
    dst = iota((1024, 128), 1)
    zz = (dst // 32) * 8 + lax.rem(dst, 8)
    side = lax.rem(dst, 32) // 8
    ypair = ones_where(
        (dst < 64) & (src // 64 == zz)
        & (((side == 0) & (lax.rem(src, 32) == 0)) | ((side == 1) & (lax.rem(src, 32) == 31)))
    )
    src = iota((128, 128), 0)
    dst = iota((128, 128), 1)
    zpair = ones_where(
        ((dst >= 48) & (dst < 64) & (src // 2 == dst - 48))
        | ((dst >= 16) & (dst < 32) & (src >= 96) & ((src - 96) // 2 == dst - 16))
    )
    l1 = iota((1, 128), 1)
    low = (lax.rem(l1, 32) < 8) | ((l1 >= 48) & (l1 < 64))
    coef = jnp.where(low, -0.05, 0.05).astype(F32)
    lg = iota((5, 32, 128), 2) // 32

    for p in range(2):
        slot = 2 * me + p
        gz = tab[9, slot]
        cy = oc[(gz + 1) >> 1, p].reshape(80, 128)
        cl = oc[gz >> 1, p].reshape(80, 128)
        ch = oc[(gz + 2) >> 1, p].reshape(80, 128)
        cg = jnp.where(lane < 64, cy, jnp.where(lane < 80, cl, ch))
        tmp[0:80, 0:128] = dot3(cg, spread)
        for v in range(5):
            for r in range(16):
                ghost[v, 2 * r : 2 * r + 2, :] = jnp.broadcast_to(tmp[16 * v + r : 16 * v + r + 1, 0:128], (2, 128))
        val = ghost[...]
        for g in range(4):
            q = tab[4 + g, slot]
            near = oyz[jnp.maximum(q, 0), p]
            val = jnp.where((lg == g) & (q >= 0), near, val)
        ghost[...] = val
        for way in range(2):
            edge = (s == 0) if way == 0 else (s == NS - 1)
            xs[...] = (ox[0, p, way] + ox[1, p, way]) + (ox[2, p, way] + ox[3, p, way])
            row = 7 if way == 0 else 40
            mine = 0 if way == 0 else 31
            for v in range(5):
                for j in range(8):
                    cut = slice(128 * j, 128 * j + 128)
                    ext[v, row : row + 1, cut] = jnp.where(edge, fine[v, p, mine : mine + 1, cut], xs[v, j : j + 1, :])
        for v in range(5):
            ext[v, 8:40, :] = fine[v, p]

        def along_x(j, _):
            cut = pl.ds(pl.multiple_of(128 * j, 128), 128)
            q = [ext[v, :, cut] for v in range(5)]
            f, a = flux(q, state(q), 0)
            nxt = lambda t: pltpu.roll(t, 47, 0)
            up = rusanov(q, f, a, [nxt(t) for t in q], [nxt(t) for t in f], nxt(a))
            for v in range(5):
                chg[v, :, cut] = (up[v] - pltpu.roll(up[v], 1, 0))[8:40]
            return 0

        lax.fori_loop(0, 8, along_x, 0)

        def rows(c, _):
            cut = pl.ds(pl.multiple_of(8 * c, 8), 8)
            q = [fine[v, p, cut, :] for v in range(5)]
            gh = [ghost[v, cut, :] for v in range(5)]
            gr = [pltpu.roll(t, 32, 1) for t in gh]
            qe = [jnp.concatenate([gr[v], q[v], gr[v]], axis=1) for v in range(5)]
            f, a = flux(qe, state(qe), 2)
            nxt = lambda t: pltpu.roll(t, 1280 - 32, 1)
            up = rusanov(qe, f, a, [nxt(t) for t in qe], [nxt(t) for t in f], nxt(a))
            lo = [pltpu.roll(t, 32, 1) for t in up]
            l8 = iota((8, 128), 1)
            for v in range(5):
                fz[v, cut, :] = jnp.where(l8 < 32, lo[v][:, 128:256], up[v][:, 1024:1152])
            change = [chg[v, cut, :] + (up[v] - lo[v])[:, 128:1152] for v in range(5)]
            eg = [dot3(t, expand) for t in gh]
            y = iota((8, 1024), 1) & 31
            qr = [jnp.where(y == 31, eg[v], pltpu.roll(q[v], 1023, 1)) for v in range(5)]
            ql = [jnp.where(y == 0, eg[v], pltpu.roll(q[v], 1, 1)) for v in range(5)]
            f, a = flux(q, state(q), 1)
            fr, ar = flux(qr, state(qr), 1)
            fl, al = flux(ql, state(ql), 1)
            up = rusanov(q, f, a, qr, fr, ar)
            lo = rusanov(ql, fl, al, q, f, a)
            for v in range(5):
                fy[v, cut, :] = jnp.where(y == 0, lo[v], up[v])
                out[v, p, cut, :] = q[v] - 0.1 * (change[v] + (up[v] - lo[v]))
            return 0

        lax.fori_loop(0, 4, rows, 0)
        l16 = iota((16, 128), 1) // 32
        for v in range(5):
            m = dot3(out[v, p], pair) * 0.125
            for h in range(2):
                tmp[0:32, 0:128] = m[:, 128 * h : 128 * h + 128]
                av[h, p, v] = tmp[pl.ds(0, 16, 2), :] + tmp[pl.ds(1, 16, 2), :]
            m = (dot3(fy[v], ypair) + dot3(fz[v], zpair)) * (0.25 * coef)
            tmp[0:32, 0:128] = m
            m = tmp[pl.ds(0, 16, 2), :] + tmp[pl.ds(1, 16, 2), :]
            t = 5 if v < 4 else 6
            gv = v % 4
            for h in range(2):
                r = pltpu.roll(m, (32 * gv - 32 * h) % 128, 1) if (32 * gv - 32 * h) % 128 else m
                if gv == 0:
                    av[h, p, t] = r
                else:
                    av[h, p, t] = jnp.where(l16 == gv, r, av[h, p, t])


def owner_kernel(av, rz, rb, oz, ss, rs, ls):
    s = lax.axis_index("slab")
    me = lax.axis_index("patch")
    peer = [lax.rem(me + d, NP) for d in range(NP)]
    barrier = pltpu.get_barrier_semaphore()
    for d in range(1, NP):
        pl.semaphore_signal(barrier, inc=1, device_id=(s, peer[d]), device_id_type=MESH)
    pl.semaphore_wait(barrier, NP - 1)
    own = pltpu.make_async_copy(av.at[lax.rem(me, 2)], rb.at[me], ls)
    own.start()
    copies = []

    def send(k, src, dst, to):
        c = pltpu.make_async_remote_copy(
            src_ref=src, dst_ref=dst, send_sem=ss.at[k], recv_sem=rs.at[k],
            device_id=(s, to), device_id_type=MESH,
        )
        c.start()
        copies.append(c)

    for d in range(1, NP):
        send(d, av.at[lax.rem(peer[d], 2)], rb.at[me], peer[d])
    send(0, rz.at[1], oz.at[0], peer[1])
    send(NP, rz.at[0], oz.at[1], peer[NP - 1])
    own.wait()
    for c in copies:
        c.wait()


def coarse_kernel(coarse, rb, oz, ocx, grid, out, ext, blk, zbl, res, sems):
    s = lax.axis_index("slab")
    me = lax.axis_index("patch")
    r = me // 2
    h = lax.rem(me, 2)
    rz = jnp.where(h == 0, r - 2, r)
    have = []
    havez = []
    cps = []
    for gy in range(6):
        a = grid[0, gy + 8 * (r - 1) + GOFF]
        b = grid[0, gy + 8 * rz + GOFF]
        have.append(a >= 0)
        havez.append(b >= 0)
        a = jnp.maximum(a, 0)
        b = jnp.maximum(b, 0)
        cps.append(pltpu.make_async_copy(rb.at[a >> 1, a & 1], blk.at[gy], sems.at[gy]))
        cps.append(pltpu.make_async_copy(rb.at[b >> 1, b & 1, pl.ds(5, 2)], zbl.at[gy], sems.at[6 + gy]))
    for c in cps:
        c.start()
    lane = iota((16, 128), 1)
    blocks = lane // 16

    def cover(row):
        m = jnp.zeros((16, 128), F32)
        for gy in range(6):
            m = jnp.where((blocks == gy + 1) & (grid[0, gy + 8 * (row - 1) + GOFF] >= 0), 1.0, m)
        return m

    mid = cover(r)
    below = jnp.where(h == 0, cover(r - 1), mid)
    above = jnp.where(h == 1, cover(r + 1), mid)
    free = 1.0 - mid
    fup = free * (1.0 - pltpu.roll(mid, 127, 1))
    flo = free * (1.0 - pltpu.roll(mid, 1, 1))
    zlo = free * (1.0 - below)
    zhi = free * (1.0 - above)
    for v in range(5):
        for k in range(8):
            ext[v, k + 1, 8:24, :] = coarse[v, :, k, :]
            ext[v, k + 1, 7:8, :] = jnp.where(s == 0, coarse[v, 0, k : k + 1, :], ocx[0, v, k : k + 1, :])
            ext[v, k + 1, 24:25, :] = jnp.where(s == NS - 1, coarse[v, 15, k : k + 1, :], ocx[1, v, k : k + 1, :])
        ext[v, 0, 8:24, :] = jnp.where(me == 0, coarse[v, :, 0, :], oz[0, v])
        ext[v, 9, 8:24, :] = jnp.where(me == NP - 1, coarse[v, :, 7, :], oz[1, v])
    for k in range(8):
        q = [ext[v, k + 1] for v in range(5)]
        st = state(q)
        f, a = flux(q, st, 0)
        nxt = lambda t: pltpu.roll(t, 31, 0)
        up = rusanov(q, f, a, [nxt(t) for t in q], [nxt(t) for t in f], nxt(a))
        change = [((up[v] - pltpu.roll(up[v], 1, 0))[8:24]) * free for v in range(5)]
        q = [t[8:24] for t in q]
        st = tuple(t[8:24] for t in st)
        f, a = flux(q, st, 2)
        qn = [ext[v, k + 2, 8:24, :] for v in range(5)]
        fn, an = flux(qn, state(qn), 2)
        qb = [ext[v, k, 8:24, :] for v in range(5)]
        fb, ab = flux(qb, state(qb), 2)
        up = rusanov(q, f, a, qn, fn, an)
        lo = rusanov(qb, fb, ab, q, f, a)
        mu = zhi if k == 7 else free
        ml = zlo if k == 0 else free
        change = [change[v] + (up[v] * mu - lo[v] * ml) for v in range(5)]
        f, a = flux(q, st, 1)
        nxt = lambda t: jnp.where(lane == 127, t, pltpu.roll(t, 127, 1))
        prv = lambda t: jnp.where(lane == 0, t, pltpu.roll(t, 1, 1))
        up = rusanov(q, f, a, [nxt(t) for t in q], [nxt(t) for t in f], nxt(a))
        lo = rusanov([prv(t) for t in q], [prv(t) for t in f], prv(a), q, f, a)
        for v in range(5):
            res[v, k] = q[v] - 0.05 * (change[v] + (up[v] * fup - lo[v] * flo))
    for c in cps:
        c.wait()
    src = iota((128, 1024), 0)
    dst = iota((128, 1024), 1)
    y = lax.rem(dst, 128)
    side = lax.rem(src, 16) // 8
    want = jnp.where(side == 0, 16 * (src // 16 + 1) - 1, 16 * (src // 16 + 2))
    place = ones_where((src < 96) & (dst // 128 == lax.rem(src, 8)) & (y == want))
    for v in range(5):
        t = 5 if v < 4 else 6
        gv = v % 4
        w = jnp.zeros((16, 128), F32)
        zf = jnp.zeros((16, 128), F32)
        for gy in range(6):
            sh = (16 * gy - 32 * gv) % 128
            fr = blk[gy, t]
            zr = zbl[gy, t - 5]
            if sh:
                fr = pltpu.roll(fr, sh, 1)
                zr = pltpu.roll(zr, sh, 1)
            w = jnp.where((blocks == gy) & have[gy], fr, w)
            zf = jnp.where((blocks == gy + 1) & havez[gy], zr, zf)
        yf = dot3(w, place)
        for k in range(8):
            val = res[v, k] + yf[:, 128 * k : 128 * k + 128]
            if k == 0:
                val = val + jnp.where(h == 0, zf, 0.0)
            if k == 7:
                val = val + jnp.where(h == 1, zf, 0.0)
            for gy in range(6):
                sh = (16 * (gy + 1 - k)) % 128
                t = blk[gy, v]
                if sh:
                    t = pltpu.roll(t, sh, 1)
                val = jnp.where((blocks == gy + 1) & have[gy], t, val)
            out[v, :, k, :] = val


def vm():
    return pl.BlockSpec(memory_space=pltpu.VMEM)


def sm():
    return pl.BlockSpec(memory_space=pltpu.SMEM)


def hb():
    return pl.BlockSpec(memory_space=pl.ANY)


def sds(*shape, dtype=F32):
    return jax.ShapeDtypeStruct(shape, dtype)


LIMIT = 48 << 20


def local(coarse, fine, columns, patch_ids):
    yzp, xf, cp, rz, cx, tab, grid = pl.pallas_call(
        pack_kernel,
        out_shape=(
            sds(2, 5, 32, 128), sds(2, 11, 8, 128), sds(5, 2, 16, 128), sds(2, 5, 16, 128), sds(2, 5, 8, 128),
            sds(10, 32, dtype=I32), sds(1, 96, dtype=I32),
        ),
        in_specs=[vm(), vm(), sm(), sm()],
        out_specs=(vm(), vm(), vm(), vm(), vm(), sm(), sm()),
        scratch_shapes=[pltpu.VMEM((8, 80, 128), F32)],
        compiler_params=pltpu.CompilerParams(vmem_limit_bytes=LIMIT),
        name="pack",
    )(fine, coarse, patch_ids, columns)
    nsem = 25
    oyz, ox, oc, ocx = pl.pallas_call(
        ghost_kernel,
        out_shape=(sds(4, 2, 5, 32, 128), sds(4, 2, 2, 5, 8, 128), sds(4, 2, 5, 16, 128), sds(2, 5, 8, 128)),
        in_specs=[vm(), vm(), vm(), vm(), sm(), sm()],
        out_specs=(vm(), vm(), vm(), vm()),
        scratch_shapes=[
            pltpu.VMEM((8, 5, 32, 128), F32),
            pltpu.VMEM((2, 4, 11, 8, 128), F32),
            pltpu.VMEM((4, 5, 2, 16, 128), F32),
            pltpu.VMEM((3, 2, 5, 32, 128), F32),
            pltpu.VMEM((3, 2, 2, 5, 8, 128), F32),
            pltpu.VMEM((3, 2, 5, 16, 128), F32),
            pltpu.SemaphoreType.DMA((nsem,)),
            pltpu.SemaphoreType.DMA((nsem,)),
            pltpu.SemaphoreType.DMA((2,)),
        ],
        compiler_params=pltpu.CompilerParams(collective_id=0, has_side_effects=True, vmem_limit_bytes=LIMIT),
        name="ghosts",
    )(yzp, xf, cp, cx, tab, patch_ids)
    fine_out, av = pl.pallas_call(
        fine_kernel,
        out_shape=(sds(5, 2, 32, 1024), sds(2, 2, 7, 16, 128)),
        in_specs=[vm(), vm(), vm(), vm(), sm()],
        out_specs=(vm(), vm()),
        scratch_shapes=[
            pltpu.VMEM((5, 48, 1024), F32),
            pltpu.VMEM((5, 32, 128), F32),
            pltpu.VMEM((5, 32, 1024), F32),
            pltpu.VMEM((5, 32, 1024), F32),
            pltpu.VMEM((5, 32, 128), F32),
            pltpu.VMEM((5, 8, 128), F32),
            pltpu.VMEM((80, 128), F32),
        ],
        compiler_params=pltpu.CompilerParams(vmem_limit_bytes=LIMIT),
        name="fine_step",
    )(fine, oyz, ox, oc, tab)
    rb, oz = pl.pallas_call(
        owner_kernel,
        out_shape=(sds(16, 2, 7, 16, 128), sds(2, 5, 16, 128)),
        in_specs=[vm(), vm()],
        out_specs=(hb(), hb()),
        scratch_shapes=[
            pltpu.SemaphoreType.DMA((NP + 1,)),
            pltpu.SemaphoreType.DMA((NP + 1,)),
            pltpu.SemaphoreType.DMA,
        ],
        compiler_params=pltpu.CompilerParams(collective_id=1, has_side_effects=True, vmem_limit_bytes=LIMIT),
        name="owners",
    )(av, rz)
    coarse_out = pl.pallas_call(
        coarse_kernel,
        out_shape=sds(5, 16, 8, 128),
        in_specs=[vm(), hb(), vm(), vm(), sm()],
        out_specs=vm(),
        scratch_shapes=[
            pltpu.VMEM((5, 10, 32, 128), F32),
            pltpu.VMEM((6, 7, 16, 128), F32),
            pltpu.VMEM((6, 2, 16, 128), F32),
            pltpu.VMEM((5, 8, 16, 128), F32),
            pltpu.SemaphoreType.DMA((12,)),
        ],
        compiler_params=pltpu.CompilerParams(vmem_limit_bytes=LIMIT),
        name="coarse_step",
    )(coarse, rb, oz, ocx, grid)
    return coarse_out, fine_out


def solution(mesh):
    return jax.shard_map(
        local,
        mesh=mesh,
        in_specs=(
            P(None, "slab", "patch", None),
            P(None, ("slab", "patch"), None, None),
            P(),
            P("slab", None),
        ),
        out_specs=(P(None, "slab", "patch", None), P(None, ("slab", "patch"), None, None)),
        check_vma=False,
    )
```

```python
import jax
import jax.numpy as jnp
from jax import lax
from jax.experimental import pallas as pl
from jax.experimental.pallas import tpu as pltpu
from jax.sharding import PartitionSpec as P

F32 = jnp.float32
BF16 = jnp.bfloat16
I32 = jnp.int32
MESH = pl.DeviceIdType.MESH
NS = 8
NP = 16
GOFF = 16


def iota(shape, dim):
    return lax.broadcasted_iota(I32, shape, dim)


def dot3(x, m):
    hi = x.astype(BF16)
    r = x - hi.astype(F32)
    mid = r.astype(BF16)
    lo = (r - mid.astype(F32)).astype(BF16)
    d = lambda a: jnp.dot(a, m, preferred_element_type=F32)
    return d(hi) + (d(mid) + d(lo))


def moved(x, k):
    return pltpu.roll(x, k % 128, 1) if k % 128 else x


def ones_where(c):
    return jnp.where(c, 1.0, 0.0).astype(BF16)


def state(q):
    r = 1.0 / q[0]
    p = 0.4 * (q[4] - 0.5 * ((q[1] * q[1] + q[2] * q[2] + q[3] * q[3]) * r))
    c = jnp.sqrt(1.4 * p * r)
    return r, p, c


def flux(q, s, d):
    r, p, c = s
    u = q[1 + d] * r
    f = [q[1 + d], q[1] * u, q[2] * u, q[3] * u, (q[4] + p) * u]
    f[1 + d] = f[1 + d] + p
    return f, jnp.abs(u) + c


def rusanov(ql, fl, al, qr, fr, ar):
    a = 0.5 * jnp.maximum(al, ar)
    return [0.5 * (fl[v] + fr[v]) - a * (qr[v] - ql[v]) for v in range(5)]


def pack_kernel(fine, coarse, ids, cols, a1, x1, rz, cx, nbr, grid, ct, fr):
    rank = lax.axis_index("patch")
    half = lax.rem(rank, 2)
    for i in range(96):
        grid[0, i] = jnp.int32(-1)

    def place(s, _):
        n = ids[0, s]
        gy = cols[n, 0]
        gz = cols[n, 1]
        nbr[4, s] = gy
        nbr[5, s] = gz
        grid[0, gy + 8 * gz + GOFF] = s
        return 0

    lax.fori_loop(0, 32, place, 0)

    def look(s, _):
        code = nbr[4, s] + 8 * nbr[5, s] + GOFF
        for g, step in enumerate((-1, 1, -8, 8)):
            nbr[g, s] = grid[0, code + step]
        return 0

    lax.fori_loop(0, 32, look, 0)
    k = iota((1024, 128), 0)
    c = iota((1024, 128), 1)
    g = c // 32
    i = lax.rem(c, 32)
    want = jnp.where(g == 0, 32 * i + 31, jnp.where(g == 1, 32 * i, jnp.where(g == 2, 992 + i, i)))
    sel = ones_where(k == want)
    for v in range(5):
        for p in range(2):
            fr[...] = dot3(fine[v, p], sel)
            for xr in range(2):
                a1[:, p, 5 * xr + v, :] = fr[pl.ds(xr, 16, 2), :]
    lane = iota((5, 128), 1)
    n0 = ids[0, 2 * rank]
    n1 = ids[0, 2 * rank + 1]
    tag = jnp.where(iota((3, 128), 1) < 64, n0, n1).astype(F32)
    for d, row in ((0, 0), (1, 31)):
        for j in range(8):
            t0 = fine[:, 0, row, 128 * j : 128 * j + 128]
            t1 = fine[:, 1, row, 128 * j : 128 * j + 128]
            x1[d, 2 * j, 0:5, :] = jnp.where(lane < 64, t0, pltpu.roll(t1, 64, 1))
            x1[d, 2 * j + 1, 0:5, :] = jnp.where(lane < 64, pltpu.roll(t0, 64, 1), t1)
            x1[d, 2 * j, 5:8, :] = tag
            x1[d, 2 * j + 1, 5:8, :] = tag
    for v in range(5):
        for z in range(8):
            ct[z, 16 * v : 16 * v + 16, :] = coarse[v, :, z, :]
    y = iota((128, 128), 0)
    k = iota((128, 128), 1) // 8
    plane = jnp.where(k < 6, 16 * (k + 1) - 1, jnp.where(k < 12, 16 * (k - 4), -1))
    sel = ones_where(y == plane)
    lane8 = lax.rem(iota((80, 128), 1), 8)
    acc = jnp.zeros((80, 128), F32)
    for z in range(8):
        acc = jnp.where(lane8 == z, dot3(ct[z], sel), acc)
    first = ct[0]
    last = ct[7]
    own = jnp.where(half == 0, first, last)
    for v in range(5):
        cut = slice(16 * v, 16 * v + 16)
        a1[:, 0, 10 + v, :] = acc[cut]
        a1[:, 1, 10 + v, :] = own[cut]
        rz[0, v] = first[cut]
        rz[1, v] = last[cut]
        cx[0, v] = coarse[v, 0]
        cx[1, v] = coarse[v, 15]
    a1[:, 0, 15, :] = jnp.zeros((16, 128), F32)
    a1[:, 1, 15, :] = jnp.zeros((16, 128), F32)


def ghost_kernel(a1, x1, rz, cx, nbr, ids, og, oz, ocx, ba, bx, tb, dd, ss, rs, ls):
    s = lax.axis_index("slab")
    me = lax.axis_index("patch")
    up = lax.rem(s + 1, NS)
    down = lax.rem(s + NS - 1, NS)
    peer = [lax.rem(me + d, NP) for d in range(NP)]
    barrier = pltpu.get_barrier_semaphore()
    for d in range(NP):
        if d:
            pl.semaphore_signal(barrier, inc=1, device_id=(s, peer[d]), device_id_type=MESH)
        pl.semaphore_signal(barrier, inc=1, device_id=(up, peer[d]), device_id_type=MESH)
        pl.semaphore_signal(barrier, inc=1, device_id=(down, peer[d]), device_id_type=MESH)
    pl.semaphore_wait(barrier, 3 * NP - 1)
    one = []
    two = []
    count = [0]

    def send(to, src, dst, dev):
        k = count[0]
        count[0] += 1
        c = pltpu.make_async_remote_copy(
            src_ref=src, dst_ref=dst, send_sem=ss.at[k], recv_sem=rs.at[k],
            device_id=dev, device_id_type=MESH,
        )
        c.start()
        to.append(c)

    for d in range(NP):
        j = peer[d]
        if d:
            send(one, a1.at[j], ba.at[pl.ds(2 * me, 2)], (s, j))
        send(one, x1.at[0, j], bx.at[1, me], (down, j))
        send(one, x1.at[1, j], bx.at[0, me], (up, j))
    send(two, cx.at[0], ocx.at[1], (down, me))
    send(two, cx.at[1], ocx.at[0], (up, me))
    send(two, rz.at[1], oz.at[0], (s, peer[1]))
    send(two, rz.at[0], oz.at[1], (s, peer[NP - 1]))
    own = pltpu.make_async_copy(a1.at[me], ba.at[pl.ds(2 * me, 2)], ls)
    own.start()
    own.wait()
    src = iota((128, 128), 0)
    dst = iota((128, 128), 1)
    g = dst // 32
    i = lax.rem(dst, 32) // 2
    base = jnp.where(g == 0, 0, jnp.where(g == 1, 48, jnp.where(g == 2, 64, 80)))
    spread = ones_where(src == base + i)
    for c in one:
        c.wait()

    def tags(i, _):
        for way in range(2):
            t = bx[way, i]
            r = pltpu.roll(t, 64, 1)
            tb[way, 2 * i] = t
            tb[way, 2 * i + 1] = r
        return 0

    lax.fori_loop(0, NP, tags, 0)
    lane = iota((8, 128), 1)
    group = iota((10, 128), 1) // 32

    def select(j, _):
        nn = jnp.where(iota((1, 128), 1) < 64, ids[0, 2 * j], ids[0, 2 * j + 1]).astype(F32)
        for p in range(2):
            slot = 2 * j + p
            gy = nbr[4, slot]
            gz = nbr[5, slot]
            a = 4 * (gz + 1)
            y0 = ba[a, 8:16, :]
            y1 = ba[a + 2, 8:16, :]
            z0 = ba[4 * gz + 3, 8:16, :]
            z1 = ba[4 * gz + 9, 8:16, :]
            r0 = pltpu.roll(y0, (128 - 8 * gy) & 127, 1)
            r1 = pltpu.roll(y1, (136 - 8 * gy) & 127, 1)
            r2 = pltpu.roll(z0, (176 - 16 * gy) & 127, 1)
            r3 = pltpu.roll(z1, (192 - 16 * gy) & 127, 1)
            c = jnp.where(lane < 64, jnp.where((lane & 8) == 0, r0, r1), jnp.where(lane < 80, r2, r3))
            c = dot3(c, spread)[2:7]
            val = jnp.concatenate([c, c], axis=0)
            for g in range(4):
                q = nbr[g, slot]
                val = jnp.where((group == g) & (q >= 0), ba[jnp.maximum(q, 0), 0:10, :], val)
            dd[j, p, 0:10, :] = val
            way = p
            acc = jnp.zeros((5, 128), F32)
            for i in range(2 * NP):
                acc = jnp.where(tb[way, i, 5:6, :] == nn, tb[way, i, 0:5, :], acc)
            dd[j, p, 10:15, :] = acc
            dd[j, p, 15:16, :] = jnp.zeros((1, 128), F32)
        return 0

    lax.fori_loop(0, NP, select, 0)
    for d in range(1, NP):
        send(two, dd.at[peer[d]], og.at[me], (s, peer[d]))
    own = pltpu.make_async_copy(dd.at[me], og.at[me], ls)
    own.start()
    own.wait()
    for c in two:
        c.wait()


def fine_kernel(fine, og, out, av, ext, ghost, chg, fy, fz, tmp):
    s = lax.axis_index("slab")
    src = iota((128, 1024), 0)
    dst = iota((128, 1024), 1)
    g = src // 32
    expand = ones_where(
        ((g == 0) & (dst == 32 * lax.rem(src, 32))) | ((g == 1) & (dst == 32 * lax.rem(src, 32) + 31))
    )
    src = iota((1024, 256), 0)
    dst = iota((1024, 256), 1)
    zz = 8 * (dst // 128) + 7 - lax.rem(dst, 128) // 16
    pair = ones_where((src // 64 == zz) & (lax.rem(src, 32) // 2 == lax.rem(dst, 16)))
    src = iota((1024, 128), 0)
    dst = iota((1024, 128), 1)
    d64 = dst & 63
    isl = d64 < 8
    ish = (d64 >= 17) & (d64 < 25)
    zz = (dst // 64) * 8 + 7 - jnp.where(isl, d64, d64 - 17)
    ypair = ones_where(
        (src // 64 == zz) & ((isl & (lax.rem(src, 32) == 0)) | (ish & (lax.rem(src, 32) == 31)))
    )
    src = iota((128, 128), 0)
    dst = iota((128, 128), 1)
    zpair = ones_where(
        ((dst >= 64) & (dst < 80) & (src < 32) & (src // 2 == dst - 64))
        | ((dst < 16) & (src >= 96) & ((src - 96) // 2 == dst))
    )
    l1 = iota((1, 128), 1)
    ycoef = jnp.where((l1 & 63) < 8, -0.05, 0.05).astype(F32) * 0.25
    zcoef = jnp.where(l1 >= 64, -0.05, 0.05).astype(F32) * 0.25
    l5 = iota((5, 128), 1)

    for p in range(2):
        for m in range(16):
            for xr in range(2):
                for v in range(5):
                    ghost[v, 2 * m + xr : 2 * m + xr + 1, :] = og[m, p, 5 * xr + v : 5 * xr + v + 1, :]
        for way in range(2):
            edge = (s == 0) if way == 0 else (s == NS - 1)
            row = 7 if way == 0 else 40
            mine = 0 if way == 0 else 31
            for j in range(8):
                cut = slice(128 * j, 128 * j + 128)
                e = og[2 * j, way, 10:15, :]
                o = og[2 * j + 1, way, 10:15, :]
                if p == 0:
                    o = pltpu.roll(o, 64, 1)
                else:
                    e = pltpu.roll(e, 64, 1)
                ext[:, row, cut] = jnp.where(edge, fine[:, p, mine, cut], jnp.where(l5 < 64, e, o))
        for v in range(5):
            ext[v, 8:40, :] = fine[v, p]

        def along_x(j, _):
            cut = pl.ds(pl.multiple_of(128 * j, 128), 128)
            q = [ext[v, :, cut] for v in range(5)]
            f, a = flux(q, state(q), 0)
            nxt = lambda t: pltpu.roll(t, 47, 0)
            up = rusanov(q, f, a, [nxt(t) for t in q], [nxt(t) for t in f], nxt(a))
            for v in range(5):
                chg[v, :, cut] = (up[v] - pltpu.roll(up[v], 1, 0))[8:40]
            return 0

        lax.fori_loop(0, 8, along_x, 0)

        def rows(c, _):
            cut = pl.ds(pl.multiple_of(8 * c, 8), 8)
            q = [fine[v, p, cut, :] for v in range(5)]
            gh = [ghost[v, cut, :] for v in range(5)]
            gr = [pltpu.roll(t, 32, 1) for t in gh]
            qe = [jnp.concatenate([gr[v], q[v], gr[v]], axis=1) for v in range(5)]
            f, a = flux(qe, state(qe), 2)
            nxt = lambda t: pltpu.roll(t, 1280 - 32, 1)
            up = rusanov(qe, f, a, [nxt(t) for t in qe], [nxt(t) for t in f], nxt(a))
            lo = [pltpu.roll(t, 32, 1) for t in up]
            l8 = iota((8, 128), 1)
            for v in range(5):
                fz[v, cut, :] = jnp.where(l8 < 32, lo[v][:, 128:256], up[v][:, 1024:1152])
            change = [chg[v, cut, :] + (up[v] - lo[v])[:, 128:1152] for v in range(5)]
            eg = [dot3(t, expand) for t in gh]
            y = iota((8, 1024), 1) & 31
            qr = [jnp.where(y == 31, eg[v], pltpu.roll(q[v], 1023, 1)) for v in range(5)]
            ql = [jnp.where(y == 0, eg[v], pltpu.roll(q[v], 1, 1)) for v in range(5)]
            f, a = flux(q, state(q), 1)
            fr, ar = flux(qr, state(qr), 1)
            fl, al = flux(ql, state(ql), 1)
            up = rusanov(q, f, a, qr, fr, ar)
            lo = rusanov(ql, fl, al, q, f, a)
            for v in range(5):
                fy[v, cut, :] = jnp.where(y == 0, lo[v], up[v])
                out[v, p, cut, :] = q[v] - 0.1 * (change[v] + (up[v] - lo[v]))
            return 0

        lax.fori_loop(0, 4, rows, 0)
        l16 = iota((16, 128), 1)
        yr = [jnp.zeros((16, 128), F32)] * 2
        zr = [jnp.zeros((16, 128), F32)] * 2

        def halve(m):
            tmp[...] = m
            return tmp[pl.ds(0, 16, 2), :] + tmp[pl.ds(1, 16, 2), :]

        for v in range(5):
            m = dot3(out[v, p], pair) * 0.125
            ym = halve(dot3(fy[v], ypair) * ycoef)
            zm = halve(dot3(fz[v], zpair) * zcoef)
            for h in range(2):
                av[:, h, p, v, :] = halve(m[:, 128 * h : 128 * h + 128])
                yr[h] = jnp.where((l16 >= 25 * v) & (l16 < 25 * v + 25), moved(ym, 25 * v - 64 * h), yr[h])
                zr[h] = jnp.where(l16 // 16 == v, moved(zm, 16 * v - 64 * h), zr[h])
        for h in range(2):
            av[:, h, p, 5, :] = yr[h]
            av[:, h, p, 6, :] = zr[h]
            av[:, h, p, 7, :] = jnp.zeros((16, 128), F32)


def owner_kernel(av, grid, oe, bb, ee, ss, rs, ls):
    s = lax.axis_index("slab")
    me = lax.axis_index("patch")
    peer = [lax.rem(me + d, NP) for d in range(NP)]
    barrier = pltpu.get_barrier_semaphore()
    for d in range(1, NP):
        pl.semaphore_signal(barrier, inc=1, device_id=(s, peer[d]), device_id_type=MESH)
    pl.semaphore_wait(barrier, NP - 1)
    one = []
    two = []

    def send(to, k, src, dst, j):
        c = pltpu.make_async_remote_copy(
            src_ref=src, dst_ref=dst, send_sem=ss.at[k], recv_sem=rs.at[k],
            device_id=(s, j), device_id_type=MESH,
        )
        c.start()
        to.append(c)

    for d in range(1, NP):
        send(one, d - 1, av.at[peer[d]], bb.at[me], peer[d])
    own = pltpu.make_async_copy(av.at[me], bb.at[me], ls)
    own.start()
    own.wait()
    lane = iota((8, 128), 1)
    sub = iota((8, 128), 0)
    block = lane // 16
    for c in one:
        c.wait()

    def expand(j, _):
        h = lax.rem(j, 2)
        r = j // 2
        far = jnp.where(h == 0, r - 2, r)
        edge = jnp.where(h == 0, 0, 7)
        val = [jnp.zeros((8, 128), F32)] * 5
        add = [jnp.zeros((8, 128), F32)] * 5
        for gy in range(6):
            a = grid[0, gy + 8 * (r - 1) + GOFF]
            b = grid[0, gy + 8 * far + GOFF]
            a0 = jnp.maximum(a, 0)
            b0 = jnp.maximum(b, 0)
            t = bb[a0 // 2, h, a0 & 1]
            zt = bb[b0 // 2, h, b0 & 1, 6:7, :]
            ina = (block == gy + 1) & (a >= 0)
            inb = (block == gy + 1) & (sub == edge) & (b >= 0)
            iny = ((lane == 16 * gy + 15) | (lane == 16 * gy + 32)) & (a >= 0)
            yt = pltpu.roll(jnp.broadcast_to(t[5:6], (8, 128)), 0, 1, stride=1, stride_axis=0)
            zt = jnp.broadcast_to(zt, (8, 128))
            for v in range(5):
                w = jnp.broadcast_to(t[v : v + 1], (8, 128))
                w = moved(pltpu.roll(w, 0, 1, stride=16, stride_axis=0), 16 * gy + 32)
                val[v] = jnp.where(ina, w, val[v])
                w = moved(yt, 16 * gy + 8 - 25 * v)
                add[v] = jnp.where(iny, add[v] + w, add[v])
                w = moved(zt, 16 * gy + 16 - 16 * v)
                add[v] = jnp.where(inb, add[v] + w, add[v])
        covered = jnp.zeros((8, 128), F32)
        for gy in range(6):
            covered = jnp.where((block == gy + 1) & (grid[0, gy + 8 * (r - 1) + GOFF] >= 0), 1.0, covered)
        for v in range(5):
            ee[j, v] = jnp.where(covered > 0, val[v], add[v])
        return 0

    lax.fori_loop(0, NP, expand, 0)
    for d in range(1, NP):
        send(two, NP - 2 + d, ee.at[peer[d]], oe.at[me], peer[d])
    own = pltpu.make_async_copy(ee.at[me], oe.at[me], ls)
    own.start()
    own.wait()
    for c in two:
        c.wait()


def coarse_kernel(coarse, oe, oz, ocx, grid, out):
    s = lax.axis_index("slab")
    me = lax.axis_index("patch")
    r = me // 2
    h = lax.rem(me, 2)
    lane = iota((8, 128), 1)
    sub = iota((8, 128), 0)
    blocks = lane // 16

    def cover(row):
        m = jnp.zeros((8, 128), F32)
        for gy in range(6):
            m = jnp.where((blocks == gy + 1) & (grid[0, gy + 8 * (row - 1) + GOFF] >= 0), 1.0, m)
        return m

    mid = cover(r)
    below = jnp.where(h == 0, cover(r - 1), mid)
    above = jnp.where(h == 1, cover(r + 1), mid)
    free = 1.0 - mid
    fup = free * (1.0 - pltpu.roll(mid, 127, 1))
    flo = free * (1.0 - pltpu.roll(mid, 1, 1))
    zlo = free * (1.0 - jnp.where(sub == 0, below, mid))
    zhi = free * (1.0 - jnp.where(sub == 7, above, mid))

    def cells(x):
        q = [coarse[v, x] for v in range(5)]
        st = state(q)
        return q, st, flux(q, st, 0)

    def face(a, b):
        return rusanov(a[0], a[2][0], a[2][1], b[0], b[2][0], b[2][1])

    first = cells(0)
    q = [jnp.where(s == 0, coarse[v, 0], ocx[0, v]) for v in range(5)]
    st = state(q)
    lower = face((q, st, flux(q, st, 0)), first)
    here = first
    for x in range(16):
        if x < 15:
            there = cells(x + 1)
        else:
            q = [jnp.where(s == NS - 1, coarse[v, 15], ocx[1, v]) for v in range(5)]
            st = state(q)
            there = (q, st, flux(q, st, 0))
        upper = face(here, there)
        q, st, _ = here
        change = [(upper[v] - lower[v]) * free for v in range(5)]
        row = slice(x, x + 1)
        zn = [jnp.where(sub == 7, jnp.where(me == NP - 1, q[v], oz[1, v, row, :]), pltpu.roll(q[v], 7, 0)) for v in range(5)]
        zb = [jnp.where(sub == 0, jnp.where(me == 0, q[v], oz[0, v, row, :]), pltpu.roll(q[v], 1, 0)) for v in range(5)]
        f, a = flux(q, st, 2)
        fn, an = flux(zn, state(zn), 2)
        fb, ab = flux(zb, state(zb), 2)
        up = rusanov(q, f, a, zn, fn, an)
        lo = rusanov(zb, fb, ab, q, f, a)
        change = [change[v] + (up[v] * zhi - lo[v] * zlo) for v in range(5)]
        f, a = flux(q, st, 1)
        nxt = lambda t: jnp.where(lane == 127, t, pltpu.roll(t, 127, 1))
        prv = lambda t: jnp.where(lane == 0, t, pltpu.roll(t, 1, 1))
        up = rusanov(q, f, a, [nxt(t) for t in q], [nxt(t) for t in f], nxt(a))
        lo = rusanov([prv(t) for t in q], [prv(t) for t in f], prv(a), q, f, a)
        for v in range(5):
            prov = q[v] - 0.05 * (change[v] + (up[v] * fup - lo[v] * flo))
            e = oe[x, v]
            out[v, x] = jnp.where(mid > 0, e, prov + e)
        here = there
        lower = upper


def vm():
    return pl.BlockSpec(memory_space=pltpu.VMEM)


def sm():
    return pl.BlockSpec(memory_space=pltpu.SMEM)


def sds(*shape, dtype=F32):
    return jax.ShapeDtypeStruct(shape, dtype)


LIMIT = 48 << 20


def params(**k):
    return pltpu.CompilerParams(vmem_limit_bytes=LIMIT, **k)


def local(coarse, fine, columns, patch_ids):
    a1, x1, rz, cx, nbr, grid = pl.pallas_call(
        pack_kernel,
        out_shape=(
            sds(16, 2, 16, 128), sds(2, 16, 8, 128), sds(2, 5, 16, 128), sds(2, 5, 8, 128),
            sds(6, 32, dtype=I32), sds(1, 96, dtype=I32),
        ),
        in_specs=[vm(), vm(), sm(), sm()],
        out_specs=(vm(), vm(), vm(), vm(), sm(), sm()),
        scratch_shapes=[pltpu.VMEM((8, 80, 128), F32), pltpu.VMEM((32, 128), F32)],
        compiler_params=params(),
        name="pack",
    )(fine, coarse, patch_ids, columns)
    nsem = 3 * NP - 1 + 4 + NP - 1
    og, oz, ocx = pl.pallas_call(
        ghost_kernel,
        out_shape=(sds(16, 2, 16, 128), sds(2, 5, 16, 128), sds(2, 5, 8, 128)),
        in_specs=[vm(), vm(), vm(), vm(), sm(), sm()],
        out_specs=(vm(), vm(), vm()),
        scratch_shapes=[
            pltpu.VMEM((32, 16, 128), F32),
            pltpu.VMEM((2, 16, 8, 128), F32),
            pltpu.VMEM((2, 32, 8, 128), F32),
            pltpu.VMEM((16, 2, 16, 128), F32),
            pltpu.SemaphoreType.DMA((nsem,)),
            pltpu.SemaphoreType.DMA((nsem,)),
            pltpu.SemaphoreType.DMA,
        ],
        compiler_params=params(collective_id=0, has_side_effects=True),
        name="ghosts",
    )(a1, x1, rz, cx, nbr, patch_ids)
    fine_out, av = pl.pallas_call(
        fine_kernel,
        out_shape=(sds(5, 2, 32, 1024), sds(16, 2, 2, 8, 128)),
        in_specs=[vm(), vm()],
        out_specs=(vm(), vm()),
        scratch_shapes=[
            pltpu.VMEM((5, 48, 1024), F32),
            pltpu.VMEM((5, 32, 128), F32),
            pltpu.VMEM((5, 32, 1024), F32),
            pltpu.VMEM((5, 32, 1024), F32),
            pltpu.VMEM((5, 32, 128), F32),
            pltpu.VMEM((32, 128), F32),
        ],
        compiler_params=params(),
        name="fine_step",
    )(fine, og)
    oe = pl.pallas_call(
        owner_kernel,
        out_shape=sds(16, 5, 8, 128),
        in_specs=[vm(), sm()],
        out_specs=vm(),
        scratch_shapes=[
            pltpu.VMEM((16, 2, 2, 8, 128), F32),
            pltpu.VMEM((16, 5, 8, 128), F32),
            pltpu.SemaphoreType.DMA((2 * NP - 2,)),
            pltpu.SemaphoreType.DMA((2 * NP - 2,)),
            pltpu.SemaphoreType.DMA,
        ],
        compiler_params=params(collective_id=1, has_side_effects=True),
        name="owners",
    )(av, grid)
    coarse_out = pl.pallas_call(
        coarse_kernel,
        out_shape=sds(5, 16, 8, 128),
        in_specs=[vm(), vm(), vm(), vm(), sm()],
        out_specs=vm(),
        compiler_params=params(),
        name="coarse_step",
    )(coarse, oe, oz, ocx, grid)
    return coarse_out, fine_out


def solution(mesh):
    return jax.shard_map(
        local,
        mesh=mesh,
        in_specs=(
            P(None, "slab", "patch", None),
            P(None, ("slab", "patch"), None, None),
            P(),
            P("slab", None),
        ),
        out_specs=(P(None, "slab", "patch", None), P(None, ("slab", "patch"), None, None)),
        check_vma=False,
    )
```

```python
import jax
import jax.numpy as jnp
from jax import lax
from jax.experimental import pallas as pl
from jax.experimental.pallas import tpu as pltpu
from jax.sharding import PartitionSpec as P

F32 = jnp.float32
BF16 = jnp.bfloat16
I32 = jnp.int32
MESH = pl.DeviceIdType.MESH
NS = 8
NP = 16
GOFF = 16


def iota(shape, dim):
    return lax.broadcasted_iota(I32, shape, dim)


def dot3(x, m):
    hi = x.astype(BF16)
    r = x - hi.astype(F32)
    mid = r.astype(BF16)
    lo = (r - mid.astype(F32)).astype(BF16)
    d = lambda a: jnp.dot(a, m, preferred_element_type=F32)
    return d(hi) + (d(mid) + d(lo))


def moved(x, k):
    return pltpu.roll(x, k % 128, 1) if k % 128 else x


def ones_where(c):
    return jnp.where(c, 1.0, 0.0).astype(BF16)


def state(q):
    r = 1.0 / q[0]
    p = 0.4 * (q[4] - 0.5 * ((q[1] * q[1] + q[2] * q[2] + q[3] * q[3]) * r))
    c = jnp.sqrt(1.4 * p * r)
    return r, p, c


def flux(q, s, d):
    r, p, c = s
    u = q[1 + d] * r
    f = [q[1 + d], q[1] * u, q[2] * u, q[3] * u, (q[4] + p) * u]
    f[1 + d] = f[1 + d] + p
    return f, jnp.abs(u) + c


def rusanov(ql, fl, al, qr, fr, ar):
    a = 0.5 * jnp.maximum(al, ar)
    return [0.5 * (fl[v] + fr[v]) - a * (qr[v] - ql[v]) for v in range(5)]


N1 = NP - 1
S_X = N1
S_H = S_X + 2 * NP
S_G = S_H + 4
S_A = S_G + N1
S_E = S_A + N1
N_SEM = S_E + N1


def step_kernel(
    fine, coarse, ids, cols, fo, oe, oz, ocx, grid,
    nbr, fb, cb, a1, x1, rz, ct, pk, ba, bx, tb, dd, og, gh, bf, xg, xo, avs, av, bb, ee, big, chg, ss, rs, ls,
):
    s = lax.axis_index("slab")
    me = lax.axis_index("patch")
    half = lax.rem(me, 2)
    up = lax.rem(s + 1, NS)
    down = lax.rem(s + NS - 1, NS)
    peer = [lax.rem(me + d, NP) for d in range(NP)]
    loads = [pltpu.make_async_copy(fine.at[v], fb.at[v], ls.at[v]) for v in range(5)]
    loads.append(pltpu.make_async_copy(coarse, cb, ls.at[5]))
    barrier = pltpu.get_barrier_semaphore()
    for c in loads:
        c.start()
    for d in range(NP):
        if d:
            pl.semaphore_signal(barrier, inc=1, device_id=(s, peer[d]), device_id_type=MESH)
        pl.semaphore_signal(barrier, inc=1, device_id=(up, peer[d]), device_id_type=MESH)
        pl.semaphore_signal(barrier, inc=1, device_id=(down, peer[d]), device_id_type=MESH)

    def copy(k, src, dst, dev):
        return pltpu.make_async_remote_copy(
            src_ref=src, dst_ref=dst, send_sem=ss.at[k], recv_sem=rs.at[k],
            device_id=dev, device_id_type=MESH,
        )

    def place(t, _):
        n = ids[0, t]
        gy = cols[0, n]
        gz = cols[1, n]
        nbr[4, t] = gy
        nbr[5, t] = gz
        nbr[6, t] = gy + 8 * gz + GOFF
        return 0

    lax.fori_loop(0, 32, place, 0)
    for i in range(GOFF):
        grid[0, i] = jnp.int32(-1)

    def find(k, _):
        q = jnp.int32(-1)
        for t in range(32):
            q = jnp.where(nbr[6, t] == k, t, q)
        grid[0, k] = q
        return 0

    lax.fori_loop(GOFF, GOFF + 48, find, 0)
    for i in range(GOFF + 48, 96):
        grid[0, i] = jnp.int32(-1)

    def look(t, _):
        for g, step in enumerate((-1, 1, -8, 8)):
            nbr[g, t] = grid[0, nbr[6, t] + step]
        return 0

    lax.fori_loop(0, 32, look, 0)

    k = iota((1024, 128), 0)
    c = iota((1024, 128), 1)
    g = c // 32
    i = lax.rem(c, 32)
    want = jnp.where(g == 0, 32 * i + 31, jnp.where(g == 1, 32 * i, jnp.where(g == 2, 992 + i, i)))
    sel = ones_where(k == want)
    for v in range(5):
        loads[v].wait()
        for p in range(2):
            pk[p, v] = dot3(fb[v, p], sel)
            for xr in range(2):
                a1[:, p, 5 * xr + v, :] = pk[p, v, pl.ds(xr, 16, 2), :]
    lane = iota((5, 128), 1)
    tag = jnp.where(iota((3, 128), 1) < 64, ids[0, 2 * me], ids[0, 2 * me + 1]).astype(F32)
    for d, row in ((0, 0), (1, 31)):
        for j in range(8):
            t0 = fb[:, 0, row, 128 * j : 128 * j + 128]
            t1 = fb[:, 1, row, 128 * j : 128 * j + 128]
            xo[:, d, 128 * j : 128 * j + 128] = t0
            xo[:, 2 + d, 128 * j : 128 * j + 128] = t1
            x1[d, 2 * j, 0:5, :] = jnp.where(lane < 64, t0, pltpu.roll(t1, 64, 1))
            x1[d, 2 * j + 1, 0:5, :] = jnp.where(lane < 64, pltpu.roll(t0, 64, 1), t1)
            x1[d, 2 * j, 5:8, :] = tag
            x1[d, 2 * j + 1, 5:8, :] = tag
    loads[5].wait()
    for v in range(5):
        for z in range(8):
            ct[z, 16 * v : 16 * v + 16, :] = cb[v, :, z, :]
    y = iota((128, 128), 0)
    k = iota((128, 128), 1) // 8
    plane = jnp.where(k < 6, 16 * (k + 1) - 1, jnp.where(k < 12, 16 * (k - 4), -1))
    sel = ones_where(y == plane)
    lane8 = lax.rem(iota((80, 128), 1), 8)
    acc = jnp.zeros((80, 128), F32)
    for z in range(8):
        acc = jnp.where(lane8 == z, dot3(ct[z], sel), acc)
    first = ct[0]
    last = ct[7]
    own = jnp.where(half == 0, first, last)
    for v in range(5):
        cut = slice(16 * v, 16 * v + 16)
        a1[:, 0, 10 + v, :] = acc[cut]
        a1[:, 1, 10 + v, :] = own[cut]
        rz[0, v] = first[cut]
        rz[1, v] = last[cut]
    a1[:, 0, 15, :] = jnp.zeros((16, 128), F32)
    a1[:, 1, 15, :] = jnp.zeros((16, 128), F32)

    pl.semaphore_wait(barrier, 3 * NP - 1)
    one = []
    two = []
    for d in range(NP):
        j = peer[d]
        if d:
            one.append(copy(d - 1, a1.at[j], ba.at[pl.ds(2 * me, 2)], (s, j)))
            one[-1].start()
        for c in (
            copy(S_X + 2 * d, x1.at[0, j], bx.at[1, me], (down, j)),
            copy(S_X + 2 * d + 1, x1.at[1, j], bx.at[0, me], (up, j)),
        ):
            c.start()
            one.append(c)
    two = [
        copy(S_H, cb.at[:, 0], ocx.at[1], (down, me)),
        copy(S_H + 1, cb.at[:, 15], ocx.at[0], (up, me)),
        copy(S_H + 2, rz.at[1], oz.at[0], (s, peer[1])),
        copy(S_H + 3, rz.at[0], oz.at[1], (s, peer[N1])),
    ]
    for c in two:
        c.start()
    own = pltpu.make_async_copy(a1.at[me], ba.at[pl.ds(2 * me, 2)], ls.at[6])
    own.start()

    src = iota((1024, 256), 0)
    dst = iota((1024, 256), 1)
    zz = 8 * (dst // 128) + 7 - lax.rem(dst, 128) // 16
    pair = ones_where((src // 64 == zz) & (lax.rem(src, 32) // 2 == lax.rem(dst, 16)))

    def interior(p):
        def along_x(j, _):
            cut = pl.ds(pl.multiple_of(128 * j, 128), 128)
            q = [fb[v, p, :, cut] for v in range(5)]
            f, a = flux(q, state(q), 0)
            nxt = lambda t: pltpu.roll(t, 31, 0)
            hi = rusanov(q, f, a, [nxt(t) for t in q], [nxt(t) for t in f], nxt(a))
            inner = iota((32, 128), 0) < 31
            for v in range(5):
                t = jnp.where(inner, hi[v], 0.0)
                chg[v, :, cut] = t - pltpu.roll(t, 1, 0)
            return 0

        lax.fori_loop(0, 8, along_x, 0)

        def rows(c, _):
            cut = pl.ds(pl.multiple_of(8 * c, 8), 8)
            q = [fb[v, p, cut, :] for v in range(5)]
            st = state(q)
            l8 = iota((8, 1024), 1)
            change = [chg[v, cut, :] for v in range(5)]
            for way, shift, inner in ((2, 32, l8 < 992), (1, 1, (l8 & 31) < 31)):
                f, a = flux(q, st, way)
                nxt = lambda t: pltpu.roll(t, 1024 - shift, 1)
                hi = rusanov(q, f, a, [nxt(t) for t in q], [nxt(t) for t in f], nxt(a))
                for v in range(5):
                    t = jnp.where(inner, hi[v], 0.0)
                    change[v] = change[v] + (t - pltpu.roll(t, shift, 1))
            for v in range(5):
                fo[v, p, cut, :] = q[v] - 0.1 * change[v]
            return 0

        lax.fori_loop(0, 4, rows, 0)
        for v in range(5):
            m = dot3(fo[v, p], pair)
            for h in range(2):
                big[h, 0:32, :] = m[:, 128 * h : 128 * h + 128]
                avs[p, v, h] = 0.125 * (big[h, pl.ds(0, 16, 2), :] + big[h, pl.ds(1, 16, 2), :])

    interior(0)
    src = iota((128, 128), 0)
    dst = iota((128, 128), 1)
    g = dst // 32
    i = lax.rem(dst, 32) // 2
    base = jnp.where(g == 0, 0, jnp.where(g == 1, 48, jnp.where(g == 2, 64, 80)))
    spread = ones_where(src == base + i)
    own.wait()
    for c in one:
        c.wait()

    def tags(i, _):
        for way in range(2):
            t = bx[way, i]
            tb[way, 2 * i] = t
            tb[way, 2 * i + 1] = pltpu.roll(t, 64, 1)
        return 0

    lax.fori_loop(0, NP, tags, 0)
    lane = iota((8, 128), 1)
    group = iota((10, 128), 1) // 32

    def select(j):
        nn = jnp.where(iota((1, 128), 1) < 64, ids[0, 2 * j], ids[0, 2 * j + 1]).astype(F32)
        for p in range(2):
            slot = 2 * j + p
            gy = nbr[4, slot]
            gz = nbr[5, slot]
            a = 4 * (gz + 1)
            r0 = pltpu.roll(ba[a, 8:16, :], (128 - 8 * gy) & 127, 1)
            r1 = pltpu.roll(ba[a + 2, 8:16, :], (136 - 8 * gy) & 127, 1)
            r2 = pltpu.roll(ba[4 * gz + 3, 8:16, :], (176 - 16 * gy) & 127, 1)
            r3 = pltpu.roll(ba[4 * gz + 9, 8:16, :], (192 - 16 * gy) & 127, 1)
            c = jnp.where(lane < 64, jnp.where((lane & 8) == 0, r0, r1), jnp.where(lane < 80, r2, r3))
            c = dot3(c, spread)[2:7]
            val = jnp.concatenate([c, c], axis=0)
            for g in range(4):
                q = nbr[g, slot]
                val = jnp.where((group == g) & (q >= 0), ba[jnp.maximum(q, 0), 0:10, :], val)
            dd[j, p, 0:10, :] = val
            acc = jnp.zeros((5, 128), F32)
            for i in range(2 * NP):
                acc = jnp.where(tb[p, i, 5:6, :] == nn, tb[p, i, 0:5, :], acc)
            dd[j, p, 10:15, :] = acc
            dd[j, p, 15:16, :] = jnp.zeros((1, 128), F32)

    def selected(d):
        j = lax.rem(me + d, NP)
        return copy(S_G + d - 1, dd.at[j], og.at[me], (s, j))

    def select_send(d, _):
        select(lax.rem(me + d, NP))
        selected(d).start()
        return 0

    lax.fori_loop(1, NP, select_send, 0)
    select(me)
    own = pltpu.make_async_copy(dd.at[me], og.at[me], ls.at[6])
    own.start()
    interior(1)

    src = iota((128, 256), 0)
    dst = iota((128, 256), 1)
    g = src // 32
    i = lax.rem(src, 32) // 2
    zz = 8 * (dst // 128) + 7 - lax.rem(dst, 128) // 16
    yy = lax.rem(dst, 16)
    far = 15 * (g & 1)
    hit = (zz == jnp.where(g < 2, i, far)) & (yy == jnp.where(g < 2, far, i))
    sign = jnp.where((g & 1) == 0, -1.0, 1.0)
    mean_of = jnp.where(hit, sign, 0.0).astype(BF16)
    src = iota((128, 128), 0)
    dst = iota((128, 128), 1)
    g = src // 32
    i = lax.rem(src, 32) // 2
    z_at = 64 * (i // 8) + 7 - lax.rem(i, 8)
    at = jnp.where(g == 0, z_at, jnp.where(g == 1, z_at + 17, jnp.where(g == 2, 96 + i, 32 + i)))
    reflux = ones_where(dst == at)
    l1 = iota((1, 128), 1)
    low = ((l1 & 63) < 8) | (l1 >= 96)
    coef = jnp.where(low, -0.05, 0.05).astype(F32) * 0.25
    src = iota((128, 1024), 0)
    dst = iota((128, 1024), 1)
    g = src // 32
    i = lax.rem(src, 32)
    at = jnp.where(g == 0, 32 * i, jnp.where(g == 1, 32 * i + 31, jnp.where(g == 2, i, 992 + i)))
    sign = jnp.where((g & 1) == 0, -1.0, 1.0)
    expand = jnp.where(dst == at, sign, 0.0).astype(BF16)
    own.wait()
    for d in range(1, NP):
        two.append(selected(d))
    for c in two:
        c.wait()

    g1 = iota((32, 128), 1)
    low = ((g1 // 32) & 1) == 0
    isy = g1 < 64

    def face_flux(q):
        r, pr, c = state(q)
        mn = jnp.where(isy, q[2], q[3])
        u = mn * r
        py = jnp.where(isy, pr, 0.0)
        f = [mn, q[1] * u, q[2] * u + py, q[3] * u + (pr - py), (q[4] + pr) * u]
        return f, jnp.abs(u) + c

    for p in range(2):
        for v in range(5):
            for xr in range(2):
                gh[v, pl.ds(xr, 16, 2), :] = og[:, p, 5 * xr + v, :]
        theirs = [gh[v] for v in range(5)]
        mine = [jnp.where(low, pltpu.roll(pk[p, v], 96, 1), pltpu.roll(pk[p, v], 32, 1)) for v in range(5)]
        ql = [jnp.where(low, theirs[v], mine[v]) for v in range(5)]
        qr = [jnp.where(low, mine[v], theirs[v]) for v in range(5)]
        fl, al = face_flux(ql)
        fr, ar = face_flux(qr)
        f = rusanov(ql, fl, al, qr, fr, ar)
        for v in range(5):
            bf[160 * p + 32 * v : 160 * p + 32 * v + 32, :] = f[v]
    l5 = iota((5, 128), 1)
    for way in range(2):
        for j in range(8):
            e = og[2 * j, way, 10:15, :]
            o = og[2 * j + 1, way, 10:15, :]
            cut = slice(128 * j, 128 * j + 128)
            xg[:, way, cut] = jnp.where(l5 < 64, e, pltpu.roll(o, 64, 1))
            xg[:, 2 + way, cut] = jnp.where(l5 < 64, pltpu.roll(e, 64, 1), o)
    row = iota((4, 1024), 0)
    low = (row & 1) == 0
    edge = (row & 1) == jnp.where(s == 0, 0, jnp.where(s == NS - 1, 1, 2))
    mine = [xo[v] for v in range(5)]
    theirs = [jnp.where(edge, mine[v], xg[v]) for v in range(5)]
    ql = [jnp.where(low, theirs[v], mine[v]) for v in range(5)]
    qr = [jnp.where(low, mine[v], theirs[v]) for v in range(5)]
    fl, al = flux(ql, state(ql), 0)
    fr, ar = flux(qr, state(qr), 0)
    f = rusanov(ql, fl, al, qr, fr, ar)
    for v in range(5):
        xg[v] = jnp.where(low, -f[v], f[v])
    fluxes = bf[...]
    m = dot3(fluxes, mean_of)
    big[0] = m[:, 0:128]
    big[1] = m[:, 128:256]
    big[2] = dot3(fluxes, reflux)
    l16 = iota((16, 128), 1)
    for p in range(2):
        yr = [jnp.zeros((16, 128), F32)] * 2
        zr = [jnp.zeros((16, 128), F32)] * 2
        for v in range(5):
            a = 160 * p + 32 * v
            t = [big[h, pl.ds(a, 16, 2), :] + big[h, pl.ds(a + 1, 16, 2), :] for h in range(3)]
            xm = dot3(xg[v, 2 * p : 2 * p + 2, :], pair)
            sub = iota((16, 128), 0)
            w = t[2] * coef
            for h in range(2):
                xh = xm[:, 128 * h : 128 * h + 128]
                fix = t[h] + jnp.where(sub == 0, xh[0:1], jnp.where(sub == 15, xh[1:2], 0.0))
                av[:, h, p, v, :] = avs[p, v, h] - 0.0125 * fix
                yr[h] = jnp.where((l16 >= 25 * v) & (l16 < 25 * v + 25), moved(w, 25 * v - 64 * h), yr[h])
                zr[h] = jnp.where(l16 // 16 == v, moved(w, 16 * v - 64 * h - 32), zr[h])
        for h in range(2):
            av[:, h, p, 5, :] = yr[h]
            av[:, h, p, 6, :] = zr[h]
            av[:, h, p, 7, :] = jnp.zeros((16, 128), F32)
    one = []
    for d in range(1, NP):
        one.append(copy(S_A + d - 1, av.at[peer[d]], bb.at[me], (s, peer[d])))
        one[-1].start()
    own = pltpu.make_async_copy(av.at[me], bb.at[me], ls.at[6])
    own.start()
    for p in range(2):
        for v in range(5):
            a = 160 * p + 32 * v
            fo[v, p] = fo[v, p] - 0.1 * dot3(bf[a : a + 32, :], expand)
            for way, x in ((0, 0), (1, 31)):
                fo[v, p, x : x + 1, :] = fo[v, p, x : x + 1, :] - 0.1 * xg[v, 2 * p + way : 2 * p + way + 1, :]
    lane = iota((8, 128), 1)
    sub = iota((8, 128), 0)
    block = lane // 16
    own.wait()
    for c in one:
        c.wait()

    def expand_to(j):
        h = lax.rem(j, 2)
        r = j // 2
        far = r - 2 + 2 * h
        val = [jnp.zeros((8, 128), F32)] * 5
        add = [jnp.zeros((8, 128), F32)] * 5
        covered = jnp.zeros((8, 128), F32)
        for gy in range(6):
            a = grid[0, gy + 8 * (r - 1) + GOFF]
            b = grid[0, gy + 8 * far + GOFF]
            a0 = jnp.maximum(a, 0)
            b0 = jnp.maximum(b, 0)
            t = bb[a0 // 2, h, a0 & 1]
            zt = bb[b0 // 2, h, b0 & 1, 6:7, :]
            ina = (block == gy + 1) & (a >= 0)
            inb = (block == gy + 1) & (sub == 7 * h) & (b >= 0)
            iny = ((lane == 16 * gy + 15) | (lane == 16 * gy + 32)) & (a >= 0)
            covered = jnp.where(ina, 1.0, covered)
            yt = pltpu.roll(jnp.broadcast_to(t[5:6], (8, 128)), 0, 1, stride=1, stride_axis=0)
            zt = jnp.broadcast_to(zt, (8, 128))
            for v in range(5):
                w = jnp.broadcast_to(t[v : v + 1], (8, 128))
                w = moved(pltpu.roll(w, 0, 1, stride=16, stride_axis=0), 16 * gy + 32)
                val[v] = jnp.where(ina, w, val[v])
                add[v] = jnp.where(iny, add[v] + moved(yt, 16 * gy + 8 - 25 * v), add[v])
                add[v] = jnp.where(inb, add[v] + moved(zt, 16 * gy + 16 - 16 * v), add[v])
        for v in range(5):
            ee[j, v] = jnp.where(covered > 0, val[v], add[v])

    def expanded(d):
        j = lax.rem(me + d, NP)
        return copy(S_E + d - 1, ee.at[j], oe.at[me], (s, j))

    def expand_send(d, _):
        expand_to(lax.rem(me + d, NP))
        expanded(d).start()
        return 0

    lax.fori_loop(1, NP, expand_send, 0)
    expand_to(me)
    own = pltpu.make_async_copy(ee.at[me], oe.at[me], ls.at[6])
    own.start()
    own.wait()
    for d in range(1, NP):
        expanded(d).wait()


def coarse_kernel(coarse, oe, oz, ocx, grid, fo, out, fine_out, sem):
    done = pltpu.make_async_copy(fo, fine_out, sem)
    done.start()
    s = lax.axis_index("slab")
    me = lax.axis_index("patch")
    r = me // 2
    h = lax.rem(me, 2)
    lane = iota((8, 128), 1)
    sub = iota((8, 128), 0)
    blocks = lane // 16

    def cover(row):
        m = jnp.zeros((8, 128), F32)
        for gy in range(6):
            m = jnp.where((blocks == gy + 1) & (grid[0, gy + 8 * (row - 1) + GOFF] >= 0), 1.0, m)
        return m

    mid = cover(r)
    below = jnp.where(h == 0, cover(r - 1), mid)
    above = jnp.where(h == 1, cover(r + 1), mid)
    free = 1.0 - mid
    fup = free * (1.0 - pltpu.roll(mid, 127, 1))
    flo = free * (1.0 - pltpu.roll(mid, 1, 1))
    zlo = free * (1.0 - jnp.where(sub == 0, below, mid))
    zhi = free * (1.0 - jnp.where(sub == 7, above, mid))

    def cells(x):
        q = [coarse[v, x] for v in range(5)]
        st = state(q)
        return q, st, flux(q, st, 0)

    def face(a, b):
        return rusanov(a[0], a[2][0], a[2][1], b[0], b[2][0], b[2][1])

    first = cells(0)
    q = [jnp.where(s == 0, coarse[v, 0], ocx[0, v]) for v in range(5)]
    st = state(q)
    lower = face((q, st, flux(q, st, 0)), first)
    here = first
    for x in range(16):
        if x < 15:
            there = cells(x + 1)
        else:
            q = [jnp.where(s == NS - 1, coarse[v, 15], ocx[1, v]) for v in range(5)]
            st = state(q)
            there = (q, st, flux(q, st, 0))
        upper = face(here, there)
        q, st, _ = here
        change = [(upper[v] - lower[v]) * free for v in range(5)]
        row = slice(x, x + 1)
        zn = [jnp.where(sub == 7, jnp.where(me == NP - 1, q[v], oz[1, v, row, :]), pltpu.roll(q[v], 7, 0)) for v in range(5)]
        zb = [jnp.where(sub == 0, jnp.where(me == 0, q[v], oz[0, v, row, :]), pltpu.roll(q[v], 1, 0)) for v in range(5)]
        f, a = flux(q, st, 2)
        fn, an = flux(zn, state(zn), 2)
        fb, ab = flux(zb, state(zb), 2)
        up = rusanov(q, f, a, zn, fn, an)
        lo = rusanov(zb, fb, ab, q, f, a)
        change = [change[v] + (up[v] * zhi - lo[v] * zlo) for v in range(5)]
        f, a = flux(q, st, 1)
        nxt = lambda t: jnp.where(lane == 127, t, pltpu.roll(t, 127, 1))
        prv = lambda t: jnp.where(lane == 0, t, pltpu.roll(t, 1, 1))
        up = rusanov(q, f, a, [nxt(t) for t in q], [nxt(t) for t in f], nxt(a))
        lo = rusanov([prv(t) for t in q], [prv(t) for t in f], prv(a), q, f, a)
        for v in range(5):
            prov = q[v] - 0.05 * (change[v] + (up[v] * fup - lo[v] * flo))
            e = oe[x, v]
            out[v, x] = jnp.where(mid > 0, e, prov + e)
        here = there
        lower = upper
    done.wait()


def vm():
    return pl.BlockSpec(memory_space=pltpu.VMEM)


def sm():
    return pl.BlockSpec(memory_space=pltpu.SMEM)


def hb():
    return pl.BlockSpec(memory_space=pltpu.HBM)


def sds(*shape, dtype=F32):
    return jax.ShapeDtypeStruct(shape, dtype)


def buf(*shape):
    return pltpu.VMEM(shape, F32)


LIMIT = 48 << 20


def local(coarse, fine, columns, patch_ids):
    fo, oe, oz, ocx, grid = pl.pallas_call(
        step_kernel,
        out_shape=(
            sds(5, 2, 32, 1024), sds(16, 5, 8, 128), sds(2, 5, 16, 128), sds(2, 5, 8, 128), sds(1, 96, dtype=I32),
        ),
        in_specs=[hb(), hb(), sm(), sm()],
        out_specs=(vm(), vm(), vm(), vm(), sm()),
        scratch_shapes=[
            pltpu.SMEM((7, 32), I32),
            buf(5, 2, 32, 1024),
            buf(5, 16, 8, 128),
            buf(16, 2, 16, 128),
            buf(2, 16, 8, 128),
            buf(2, 5, 16, 128),
            buf(8, 80, 128),
            buf(2, 5, 32, 128),
            buf(32, 16, 128),
            buf(2, 16, 8, 128),
            buf(2, 32, 8, 128),
            buf(16, 2, 16, 128),
            buf(16, 2, 16, 128),
            buf(5, 32, 128),
            buf(320, 128),
            buf(5, 4, 1024),
            buf(5, 4, 1024),
            buf(2, 5, 2, 16, 128),
            buf(16, 2, 2, 8, 128),
            buf(16, 2, 2, 8, 128),
            buf(16, 5, 8, 128),
            buf(3, 320, 128),
            buf(5, 32, 1024),
            pltpu.SemaphoreType.DMA((N_SEM,)),
            pltpu.SemaphoreType.DMA((N_SEM,)),
            pltpu.SemaphoreType.DMA((7,)),
        ],
        compiler_params=pltpu.CompilerParams(collective_id=0, has_side_effects=True, vmem_limit_bytes=LIMIT),
        name="step",
    )(fine, coarse, patch_ids, columns.T)
    return pl.pallas_call(
        coarse_kernel,
        out_shape=(sds(5, 16, 8, 128), sds(5, 2, 32, 1024)),
        in_specs=[vm(), vm(), vm(), vm(), sm(), pl.BlockSpec(memory_space=pl.ANY)],
        out_specs=(vm(), hb()),
        scratch_shapes=[pltpu.SemaphoreType.DMA],
        compiler_params=pltpu.CompilerParams(vmem_limit_bytes=LIMIT),
        name="coarse_step",
    )(coarse, oe, oz, ocx, grid, fo)


def solution(mesh):
    return jax.shard_map(
        local,
        mesh=mesh,
        in_specs=(
            P(None, "slab", "patch", None),
            P(None, ("slab", "patch"), None, None),
            P(),
            P("slab", None),
        ),
        out_specs=(P(None, "slab", "patch", None), P(None, ("slab", "patch"), None, None)),
        check_vma=False,
    )
```

```python
import jax
import jax.numpy as jnp
from jax import lax
from jax.experimental import pallas as pl
from jax.experimental.pallas import tpu as pltpu
from jax.sharding import PartitionSpec as P

F32 = jnp.float32
BF16 = jnp.bfloat16
I32 = jnp.int32
MESH = pl.DeviceIdType.MESH
NS = 8
NP = 16
GOFF = 16


def iota(shape, dim):
    return lax.broadcasted_iota(I32, shape, dim)


def dot3(x, m):
    hi = x.astype(BF16)
    r = x - hi.astype(F32)
    mid = r.astype(BF16)
    lo = (r - mid.astype(F32)).astype(BF16)
    d = lambda a: jnp.dot(a, m, preferred_element_type=F32)
    return d(hi) + (d(mid) + d(lo))


def dot3_left(m, x):
    hi = x.astype(BF16)
    r = x - hi.astype(F32)
    mid = r.astype(BF16)
    lo = (r - mid.astype(F32)).astype(BF16)
    d = lambda a: jnp.dot(m, a, preferred_element_type=F32)
    return d(hi) + (d(mid) + d(lo))


def moved(x, k):
    return pltpu.roll(x, k % 128, 1) if k % 128 else x


def ones_where(c):
    return jnp.where(c, 1.0, 0.0).astype(BF16)


def state(q):
    r = 1.0 / q[0]
    p = 0.4 * (q[4] - 0.5 * ((q[1] * q[1] + q[2] * q[2] + q[3] * q[3]) * r))
    c = jnp.sqrt(1.4 * p * r)
    return r, p, c


def flux(q, s, d):
    r, p, c = s
    u = q[1 + d] * r
    f = [q[1 + d], q[1] * u, q[2] * u, q[3] * u, (q[4] + p) * u]
    f[1 + d] = f[1 + d] + p
    return f, jnp.abs(u) + c


def rusanov(ql, fl, al, qr, fr, ar):
    a = 0.5 * jnp.maximum(al, ar)
    return [0.5 * (fl[v] + fr[v]) - a * (qr[v] - ql[v]) for v in range(5)]


def provisional(s, me, coarse, oz, ocx, grid, prov):
    r = me // 2
    h = lax.rem(me, 2)
    lane = iota((8, 128), 1)
    sub = iota((8, 128), 0)
    blocks = lane // 16

    def cover(row):
        m = jnp.zeros((8, 128), F32)
        for gy in range(6):
            m = jnp.where((blocks == gy + 1) & (grid[0, gy + 8 * (row - 1) + GOFF] >= 0), 1.0, m)
        return m

    mid = cover(r)
    below = jnp.where(h == 0, cover(r - 1), mid)
    above = jnp.where(h == 1, cover(r + 1), mid)
    free = 1.0 - mid
    fup = free * (1.0 - pltpu.roll(mid, 127, 1))
    flo = free * (1.0 - pltpu.roll(mid, 1, 1))
    zlo = free * (1.0 - jnp.where(sub == 0, below, mid))
    zhi = free * (1.0 - jnp.where(sub == 7, above, mid))

    def cells(x):
        q = [coarse[v, x] for v in range(5)]
        st = state(q)
        return q, st, flux(q, st, 0)

    def face(a, b):
        return rusanov(a[0], a[2][0], a[2][1], b[0], b[2][0], b[2][1])

    first = cells(0)
    q = [jnp.where(s == 0, coarse[v, 0], ocx[0, v]) for v in range(5)]
    st = state(q)
    lower = face((q, st, flux(q, st, 0)), first)
    here = first
    for x in range(16):
        if x < 15:
            there = cells(x + 1)
        else:
            q = [jnp.where(s == NS - 1, coarse[v, 15], ocx[1, v]) for v in range(5)]
            st = state(q)
            there = (q, st, flux(q, st, 0))
        upper = face(here, there)
        q, st, _ = here
        change = [(upper[v] - lower[v]) * free for v in range(5)]
        row = slice(x, x + 1)
        zn = [jnp.where(sub == 7, jnp.where(me == NP - 1, q[v], oz[1, v, row, :]), pltpu.roll(q[v], 7, 0)) for v in range(5)]
        zb = [jnp.where(sub == 0, jnp.where(me == 0, q[v], oz[0, v, row, :]), pltpu.roll(q[v], 1, 0)) for v in range(5)]
        f, a = flux(q, st, 2)
        fn, an = flux(zn, state(zn), 2)
        fb, ab = flux(zb, state(zb), 2)
        up = rusanov(q, f, a, zn, fn, an)
        lo = rusanov(zb, fb, ab, q, f, a)
        change = [change[v] + (up[v] * zhi - lo[v] * zlo) for v in range(5)]
        f, a = flux(q, st, 1)
        nxt = lambda t: jnp.where(lane == 127, t, pltpu.roll(t, 127, 1))
        prv = lambda t: jnp.where(lane == 0, t, pltpu.roll(t, 1, 1))
        up = rusanov(q, f, a, [nxt(t) for t in q], [nxt(t) for t in f], nxt(a))
        lo = rusanov([prv(t) for t in q], [prv(t) for t in f], prv(a), q, f, a)
        for v in range(5):
            prov[v, x] = q[v] - 0.05 * (change[v] + (up[v] * fup - lo[v] * flo))
        here = there
        lower = upper
    return mid


N1 = NP - 1
S_X = N1
S_H = S_X + 2 * NP
S_G = S_H + 4
S_A = S_G + N1
S_E = S_A + N1
N_SEM = S_E + N1


def step_kernel(
    fine, coarse, ids, cols, fo, co,
    nbr, grid, fb, cb, fs, a1, x1, rz, ct, pk, ba, bx, cg, dd, og, oz, ocx,
    gh, bf, xg, xo, avs, av, bb, ee, oe, big, chg, prov, ss, rs, ls,
):
    s = lax.axis_index("slab")
    me = lax.axis_index("patch")
    half = lax.rem(me, 2)
    up = lax.rem(s + 1, NS)
    down = lax.rem(s + NS - 1, NS)
    peer = [lax.rem(me + d, NP) for d in range(NP)]
    loads = [pltpu.make_async_copy(fine.at[v], fb.at[v], ls.at[v]) for v in range(5)]
    loads.append(pltpu.make_async_copy(coarse, cb, ls.at[5]))
    barrier = pltpu.get_barrier_semaphore()
    for c in loads:
        c.start()
    for d in range(NP):
        if d:
            pl.semaphore_signal(barrier, inc=1, device_id=(s, peer[d]), device_id_type=MESH)
        pl.semaphore_signal(barrier, inc=1, device_id=(up, peer[d]), device_id_type=MESH)
        pl.semaphore_signal(barrier, inc=1, device_id=(down, peer[d]), device_id_type=MESH)

    def copy(k, src, dst, dev):
        return pltpu.make_async_remote_copy(
            src_ref=src, dst_ref=dst, send_sem=ss.at[k], recv_sem=rs.at[k],
            device_id=dev, device_id_type=MESH,
        )

    k = iota((1024, 128), 0)
    c = iota((1024, 128), 1)
    g = c // 32
    i = lax.rem(c, 32)
    want = jnp.where(g == 0, 32 * i + 31, jnp.where(g == 1, 32 * i, jnp.where(g == 2, 992 + i, i)))
    sel = ones_where(k == want)
    for v in range(5):
        loads[v].wait()
        for p in range(2):
            pk[p, v] = dot3(fb[v, p], sel)
            for xr in range(2):
                a1[:, p, 5 * xr + v, :] = pk[p, v, pl.ds(xr, 16, 2), :]
    lane = iota((5, 128), 1)
    tag = jnp.where(iota((3, 128), 1) < 64, ids[0, 2 * me], ids[0, 2 * me + 1]).astype(F32)
    for d, row in ((0, 0), (1, 31)):
        for j in range(8):
            t0 = fb[:, 0, row, 128 * j : 128 * j + 128]
            t1 = fb[:, 1, row, 128 * j : 128 * j + 128]
            xo[:, d, 128 * j : 128 * j + 128] = t0
            xo[:, 2 + d, 128 * j : 128 * j + 128] = t1
            x1[d, 2 * j, 0:5, :] = jnp.where(lane < 64, t0, pltpu.roll(t1, 64, 1))
            x1[d, 2 * j + 1, 0:5, :] = jnp.where(lane < 64, pltpu.roll(t0, 64, 1), t1)
            x1[d, 2 * j, 5:8, :] = tag
            x1[d, 2 * j + 1, 5:8, :] = tag
    loads[5].wait()
    for v in range(5):
        for z in range(8):
            ct[z, 16 * v : 16 * v + 16, :] = cb[v, :, z, :]
    y = iota((128, 128), 0)
    k = iota((128, 128), 1) // 8
    plane = jnp.where(k < 6, 16 * (k + 1) - 1, jnp.where(k < 12, 16 * (k - 4), -1))
    sel = ones_where(y == plane)
    lane8 = lax.rem(iota((80, 128), 1), 8)
    acc = jnp.zeros((80, 128), F32)
    for z in range(8):
        acc = jnp.where(lane8 == z, dot3(ct[z], sel), acc)
    first = ct[0]
    last = ct[7]
    own = jnp.where(half == 0, first, last)
    for v in range(5):
        cut = slice(16 * v, 16 * v + 16)
        a1[:, 0, 10 + v, :] = acc[cut]
        a1[:, 1, 10 + v, :] = own[cut]
        rz[0, v] = first[cut]
        rz[1, v] = last[cut]
    a1[:, 0, 15, :] = jnp.zeros((16, 128), F32)
    a1[:, 1, 15, :] = jnp.zeros((16, 128), F32)

    pl.semaphore_wait(barrier, 3 * NP - 1)
    one = []
    two = []
    for d in range(NP):
        j = peer[d]
        if d:
            one.append(copy(d - 1, a1.at[j], ba.at[pl.ds(2 * me, 2)], (s, j)))
            one[-1].start()
        for c in (
            copy(S_X + 2 * d, x1.at[0, j], bx.at[1, me], (down, j)),
            copy(S_X + 2 * d + 1, x1.at[1, j], bx.at[0, me], (up, j)),
        ):
            c.start()
            one.append(c)
    two = [
        copy(S_H, cb.at[:, 0], ocx.at[1], (down, me)),
        copy(S_H + 1, cb.at[:, 15], ocx.at[0], (up, me)),
        copy(S_H + 2, rz.at[1], oz.at[0], (s, peer[1])),
        copy(S_H + 3, rz.at[0], oz.at[1], (s, peer[N1])),
    ]
    for c in two:
        c.start()
    own = pltpu.make_async_copy(a1.at[me], ba.at[pl.ds(2 * me, 2)], ls.at[6])
    own.start()

    def place(t, _):
        n = ids[0, t]
        gy = cols[0, n]
        gz = cols[1, n]
        nbr[4, t] = gy
        nbr[5, t] = gz
        nbr[6, t] = gy + 8 * gz + GOFF
        return 0

    lax.fori_loop(0, 32, place, 0)
    for i in range(GOFF):
        grid[0, i] = jnp.int32(-1)

    def find(k, _):
        q = jnp.int32(-1)
        for t in range(32):
            q = jnp.where(nbr[6, t] == k, t, q)
        grid[0, k] = q
        return 0

    lax.fori_loop(GOFF, GOFF + 48, find, 0)
    for i in range(GOFF + 48, 96):
        grid[0, i] = jnp.int32(-1)

    def look(t, _):
        for g, step in enumerate((-1, 1, -8, 8)):
            nbr[g, t] = grid[0, nbr[6, t] + step]
        return 0

    lax.fori_loop(0, 32, look, 0)

    src = iota((1024, 256), 0)
    dst = iota((1024, 256), 1)
    zz = 8 * (dst // 128) + 7 - lax.rem(dst, 128) // 16
    pair = ones_where((src // 64 == zz) & (lax.rem(src, 32) // 2 == lax.rem(dst, 16)))

    def interior(p):
        def along_x(j, _):
            cut = pl.ds(pl.multiple_of(128 * j, 128), 128)
            q = [fb[v, p, :, cut] for v in range(5)]
            f, a = flux(q, state(q), 0)
            nxt = lambda t: pltpu.roll(t, 31, 0)
            hi = rusanov(q, f, a, [nxt(t) for t in q], [nxt(t) for t in f], nxt(a))
            inner = iota((32, 128), 0) < 31
            for v in range(5):
                t = jnp.where(inner, hi[v], 0.0)
                chg[v, :, cut] = t - pltpu.roll(t, 1, 0)
            return 0

        lax.fori_loop(0, 8, along_x, 0)

        def rows(c, _):
            cut = pl.ds(pl.multiple_of(8 * c, 8), 8)
            q = [fb[v, p, cut, :] for v in range(5)]
            st = state(q)
            l8 = iota((8, 1024), 1)
            change = [chg[v, cut, :] for v in range(5)]
            for way, shift, inner in ((2, 32, l8 < 992), (1, 1, (l8 & 31) < 31)):
                f, a = flux(q, st, way)
                nxt = lambda t: pltpu.roll(t, 1024 - shift, 1)
                hi = rusanov(q, f, a, [nxt(t) for t in q], [nxt(t) for t in f], nxt(a))
                for v in range(5):
                    t = jnp.where(inner, hi[v], 0.0)
                    change[v] = change[v] + (t - pltpu.roll(t, shift, 1))
            for v in range(5):
                fs[v, p, cut, :] = q[v] - 0.1 * change[v]
            return 0

        lax.fori_loop(0, 4, rows, 0)
        for v in range(5):
            m = dot3(fs[v, p], pair)
            for h in range(2):
                big[h, 0:32, :] = m[:, 128 * h : 128 * h + 128]
                avs[p, v, h] = 0.125 * (big[h, pl.ds(0, 16, 2), :] + big[h, pl.ds(1, 16, 2), :])

    interior(0)
    src = iota((128, 128), 0)
    dst = iota((128, 128), 1)
    g = dst // 32
    i = lax.rem(dst, 32) // 2
    base = jnp.where(g == 0, 0, jnp.where(g == 1, 48, jnp.where(g == 2, 64, 80)))
    spread = ones_where(src == base + i)
    own.wait()
    for c in one:
        c.wait()

    lane = iota((8, 128), 1)

    def place_coarse(j, _):
        for p in range(2):
            slot = 2 * j + p
            gy = nbr[4, slot]
            gz = nbr[5, slot]
            a = 4 * (gz + 1)
            r0 = pltpu.roll(ba[a, 8:16, :], (128 - 8 * gy) & 127, 1)
            r1 = pltpu.roll(ba[a + 2, 8:16, :], (136 - 8 * gy) & 127, 1)
            r2 = pltpu.roll(ba[4 * gz + 3, 8:16, :], (176 - 16 * gy) & 127, 1)
            r3 = pltpu.roll(ba[4 * gz + 9, 8:16, :], (192 - 16 * gy) & 127, 1)
            cg[slot] = jnp.where(lane < 64, jnp.where((lane & 8) == 0, r0, r1), jnp.where(lane < 80, r2, r3))
        return 0

    lax.fori_loop(0, NP, place_coarse, 0, unroll=2)
    cg[...] = dot3(cg[...].reshape(256, 128), spread).reshape(32, 8, 128)
    sub = iota((32, 128), 0)
    want = jnp.zeros((32, 128), I32)
    for j in range(NP):
        for p in range(2):
            want = jnp.where(sub == NP * p + j, ids[0, 2 * j + p], want)
    want = want.astype(F32)
    l16 = iota((16, 128), 1)
    diagonal = l16 == iota((16, 128), 0)
    for way in range(2):
        tag = bx[way, :, 5, :]
        data = jnp.concatenate([bx[way, :, v, :] for v in range(5)], axis=1)
        got = []
        for t in range(2):
            tt = pltpu.roll(tag, 64, 1) if t else tag
            row = jnp.sum(jnp.where(diagonal, tt, 0.0), axis=0, keepdims=True)
            got.append(dot3_left(ones_where(want == row)[:, 0:16], data))
        for v in range(5):
            g0 = got[0][:, 128 * v : 128 * v + 128]
            g1 = got[1][:, 128 * v : 128 * v + 128]
            lo = g0[0:16] + pltpu.roll(g1[0:16], 64, 1)
            hi = pltpu.roll(g0[16:32], 64, 1) + g1[16:32]
            dd[:, way, 10 + v, :] = jnp.where(l16 < 64, lo, hi)
        dd[:, way, 15, :] = jnp.zeros((16, 128), F32)
    group = iota((10, 128), 1) // 32

    def select(j):
        for p in range(2):
            slot = 2 * j + p
            c = cg[slot, 2:7, :]
            val = jnp.concatenate([c, c], axis=0)
            for g in range(4):
                q = nbr[g, slot]
                val = jnp.where((group == g) & (q >= 0), ba[jnp.maximum(q, 0), 0:10, :], val)
            dd[j, p, 0:10, :] = val

    def selected(d):
        j = lax.rem(me + d, NP)
        return copy(S_G + d - 1, dd.at[j], og.at[me], (s, j))

    def select_send(d, _):
        select(lax.rem(me + d, NP))
        selected(d).start()
        return 0

    lax.fori_loop(1, NP, select_send, 0)
    select(me)
    own = pltpu.make_async_copy(dd.at[me], og.at[me], ls.at[6])
    own.start()
    interior(1)

    src = iota((128, 256), 0)
    dst = iota((128, 256), 1)
    g = src // 32
    i = lax.rem(src, 32) // 2
    zz = 8 * (dst // 128) + 7 - lax.rem(dst, 128) // 16
    yy = lax.rem(dst, 16)
    far = 15 * (g & 1)
    hit = (zz == jnp.where(g < 2, i, far)) & (yy == jnp.where(g < 2, far, i))
    sign = jnp.where((g & 1) == 0, -1.0, 1.0)
    mean_of = jnp.where(hit, sign, 0.0).astype(BF16)
    src = iota((128, 128), 0)
    dst = iota((128, 128), 1)
    g = src // 32
    i = lax.rem(src, 32) // 2
    z_at = 64 * (i // 8) + 7 - lax.rem(i, 8)
    at = jnp.where(g == 0, z_at, jnp.where(g == 1, z_at + 17, jnp.where(g == 2, 96 + i, 32 + i)))
    reflux = ones_where(dst == at)
    l1 = iota((1, 128), 1)
    low = ((l1 & 63) < 8) | (l1 >= 96)
    coef = jnp.where(low, -0.05, 0.05).astype(F32) * 0.25
    src = iota((128, 1024), 0)
    dst = iota((128, 1024), 1)
    g = src // 32
    i = lax.rem(src, 32)
    at = jnp.where(g == 0, 32 * i, jnp.where(g == 1, 32 * i + 31, jnp.where(g == 2, i, 992 + i)))
    sign = jnp.where((g & 1) == 0, -1.0, 1.0)
    expand = jnp.where(dst == at, sign, 0.0).astype(BF16)
    own.wait()
    for d in range(1, NP):
        two.append(selected(d))
    for c in two:
        c.wait()

    g1 = iota((32, 128), 1)
    low = ((g1 // 32) & 1) == 0
    isy = g1 < 64

    def face_flux(q):
        r, pr, c = state(q)
        mn = jnp.where(isy, q[2], q[3])
        u = mn * r
        py = jnp.where(isy, pr, 0.0)
        f = [mn, q[1] * u, q[2] * u + py, q[3] * u + (pr - py), (q[4] + pr) * u]
        return f, jnp.abs(u) + c

    for p in range(2):
        for v in range(5):
            for xr in range(2):
                gh[v, pl.ds(xr, 16, 2), :] = og[:, p, 5 * xr + v, :]
        theirs = [gh[v] for v in range(5)]
        mine = [jnp.where(low, pltpu.roll(pk[p, v], 96, 1), pltpu.roll(pk[p, v], 32, 1)) for v in range(5)]
        ql = [jnp.where(low, theirs[v], mine[v]) for v in range(5)]
        qr = [jnp.where(low, mine[v], theirs[v]) for v in range(5)]
        fl, al = face_flux(ql)
        fr, ar = face_flux(qr)
        f = rusanov(ql, fl, al, qr, fr, ar)
        for v in range(5):
            bf[160 * p + 32 * v : 160 * p + 32 * v + 32, :] = f[v]
    l5 = iota((5, 128), 1)
    for way in range(2):
        for j in range(8):
            e = og[2 * j, way, 10:15, :]
            o = og[2 * j + 1, way, 10:15, :]
            cut = slice(128 * j, 128 * j + 128)
            xg[:, way, cut] = jnp.where(l5 < 64, e, pltpu.roll(o, 64, 1))
            xg[:, 2 + way, cut] = jnp.where(l5 < 64, pltpu.roll(e, 64, 1), o)
    row = iota((4, 1024), 0)
    low = (row & 1) == 0
    edge = (row & 1) == jnp.where(s == 0, 0, jnp.where(s == NS - 1, 1, 2))
    mine = [xo[v] for v in range(5)]
    theirs = [jnp.where(edge, mine[v], xg[v]) for v in range(5)]
    ql = [jnp.where(low, theirs[v], mine[v]) for v in range(5)]
    qr = [jnp.where(low, mine[v], theirs[v]) for v in range(5)]
    fl, al = flux(ql, state(ql), 0)
    fr, ar = flux(qr, state(qr), 0)
    f = rusanov(ql, fl, al, qr, fr, ar)
    for v in range(5):
        xg[v] = jnp.where(low, -f[v], f[v])
    fluxes = bf[...]
    m = dot3(fluxes, mean_of)
    big[0] = m[:, 0:128]
    big[1] = m[:, 128:256]
    big[2] = dot3(fluxes, reflux)
    l16 = iota((16, 128), 1)
    for p in range(2):
        gy = nbr[4, 2 * me + p]
        turn_a = (16 * gy + 32) & 127
        turn_y = 16 * gy
        turn_z = (16 * gy + 80) & 127
        yr = [jnp.zeros((16, 128), F32)] * 2
        zr = [jnp.zeros((16, 128), F32)] * 2
        for v in range(5):
            a = 160 * p + 32 * v
            t = [big[h, pl.ds(a, 16, 2), :] + big[h, pl.ds(a + 1, 16, 2), :] for h in range(3)]
            xm = dot3(xg[v, 2 * p : 2 * p + 2, :], pair)
            sub = iota((16, 128), 0)
            w = t[2] * coef
            for h in range(2):
                xh = xm[:, 128 * h : 128 * h + 128]
                fix = t[h] + jnp.where(sub == 0, xh[0:1], jnp.where(sub == 15, xh[1:2], 0.0))
                av[:, h, p, v, :] = pltpu.roll(avs[p, v, h] - 0.0125 * fix, turn_a, 1)
                yr[h] = jnp.where((l16 >= 25 * v) & (l16 < 25 * v + 25), moved(w, 25 * v - 64 * h), yr[h])
                zr[h] = jnp.where(l16 // 16 == 4 - v, moved(w, 16 * (4 - v) - 64 * h - 32), zr[h])
        for h in range(2):
            av[:, h, p, 5, :] = pltpu.roll(yr[h], turn_y, 1)
            av[:, h, p, 6, :] = pltpu.roll(zr[h], turn_z, 1)
            av[:, h, p, 7, :] = jnp.zeros((16, 128), F32)
    one = []
    for d in range(1, NP):
        one.append(copy(S_A + d - 1, av.at[peer[d]], bb.at[me], (s, peer[d])))
        one[-1].start()
    own = pltpu.make_async_copy(av.at[me], bb.at[me], ls.at[6])
    own.start()
    for p in range(2):
        for v in range(5):
            a = 160 * p + 32 * v
            fs[v, p] = fs[v, p] - 0.1 * dot3(bf[a : a + 32, :], expand)
            for way, x in ((0, 0), (1, 31)):
                fs[v, p, x : x + 1, :] = fs[v, p, x : x + 1, :] - 0.1 * xg[v, 2 * p + way : 2 * p + way + 1, :]
    stores = [pltpu.make_async_copy(fs.at[v], fo.at[v], ls.at[v]) for v in range(5)]
    for c in stores:
        c.start()
    lane = iota((8, 128), 1)
    sub = iota((8, 128), 0)
    block = lane // 16
    ring = (block + sub) & 7
    slope = lane + sub - 7
    own.wait()
    for c in one:
        c.wait()

    def expand_to(j):
        h = lax.rem(j, 2)
        r = j // 2
        far = r - 2 + 2 * h
        acc = [jnp.zeros((8, 128), F32)] * 5
        accy = [jnp.zeros((8, 128), F32)] * 5
        accz = jnp.zeros((8, 128), F32)
        covered = jnp.zeros((8, 128), F32)
        for gy in range(6):
            a = grid[0, gy + 8 * (r - 1) + GOFF]
            b = grid[0, gy + 8 * far + GOFF]
            a0 = jnp.maximum(a, 0)
            b0 = jnp.maximum(b, 0)
            t = bb[a0 // 2, h, a0 & 1]
            zt = bb[b0 // 2, h, b0 & 1, 6:7, :]
            covered = jnp.where((block == gy + 1) & (a >= 0), 1.0, covered)
            ina = (ring == gy + 1) & (a >= 0)
            accz = jnp.where((ring == gy + 1) & (b >= 0), zt, accz)
            for v in range(5):
                acc[v] = jnp.where(ina, t[v : v + 1], acc[v])
                off = (slope - 16 * gy - 25 * v) & 127
                accy[v] = jnp.where(((off == 0) | (off == 17)) & (a >= 0), t[5:6], accy[v])
        accz = pltpu.roll(accz, 0, 1, stride=16, stride_axis=0)
        for v in range(5):
            val = pltpu.roll(acc[v], 0, 1, stride=16, stride_axis=0)
            add = moved(pltpu.roll(accy[v], 0, 1, stride=1, stride_axis=0), 8 - 25 * v)
            add = add + jnp.where(sub == 7 * h, accz[v : v + 1], 0.0)
            ee[j, v] = jnp.where(covered > 0, val, add)

    def expanded(d):
        j = lax.rem(me + d, NP)
        return copy(S_E + d - 1, ee.at[j], oe.at[me], (s, j))

    def expand_send(d, _):
        expand_to(lax.rem(me + d, NP))
        expanded(d).start()
        return 0

    lax.fori_loop(1, NP, expand_send, 0)
    expand_to(me)
    own = pltpu.make_async_copy(ee.at[me], oe.at[me], ls.at[6])
    own.start()
    mid = provisional(s, me, cb, oz, ocx, grid, prov)
    own.wait()
    for d in range(1, NP):
        expanded(d).wait()
    for x in range(16):
        for v in range(5):
            e = oe[x, v]
            prov[v, x] = jnp.where(mid > 0, e, prov[v, x] + e)
    done = pltpu.make_async_copy(prov, co, ls.at[5])
    done.start()
    for c in stores:
        c.wait()
    done.wait()


def copy_kernel(a, b, a_out, b_out, sems):
    n = a.shape[0]
    copies = []
    for v in range(n):
        copies.append(pltpu.make_async_copy(b.at[v, 0], b_out.at[v, 0], sems.at[n + v]))
        copies.append(pltpu.make_async_copy(b.at[v, 1], b_out.at[v, 1], sems.at[2 * n + v]))
        copies.append(pltpu.make_async_copy(a.at[v], a_out.at[v], sems.at[v]))
    for c in copies:
        c.start()
    for c in copies:
        c.wait()


def sm():
    return pl.BlockSpec(memory_space=pltpu.SMEM)


def hb():
    return pl.BlockSpec(memory_space=pltpu.HBM)


def sds(*shape, dtype=F32):
    return jax.ShapeDtypeStruct(shape, dtype)


def buf(*shape):
    return pltpu.VMEM(shape, F32)


LIMIT = 60 << 20


def local(coarse, fine, columns, patch_ids):
    fo, co = pl.pallas_call(
        step_kernel,
        out_shape=(sds(5, 2, 32, 1024), sds(5, 16, 8, 128)),
        in_specs=[hb(), hb(), sm(), sm()],
        out_specs=(hb(), hb()),
        scratch_shapes=[
            pltpu.SMEM((7, 32), I32),
            pltpu.SMEM((1, 96), I32),
            buf(5, 2, 32, 1024),
            buf(5, 16, 8, 128),
            buf(5, 2, 32, 1024),
            buf(16, 2, 16, 128),
            buf(2, 16, 8, 128),
            buf(2, 5, 16, 128),
            buf(8, 80, 128),
            buf(2, 5, 32, 128),
            buf(32, 16, 128),
            buf(2, 16, 8, 128),
            buf(32, 8, 128),
            buf(16, 2, 16, 128),
            buf(16, 2, 16, 128),
            buf(2, 5, 16, 128),
            buf(2, 5, 8, 128),
            buf(5, 32, 128),
            buf(320, 128),
            buf(5, 4, 1024),
            buf(5, 4, 1024),
            buf(2, 5, 2, 16, 128),
            buf(16, 2, 2, 8, 128),
            buf(16, 2, 2, 8, 128),
            buf(16, 5, 8, 128),
            buf(16, 5, 8, 128),
            buf(3, 320, 128),
            buf(5, 32, 1024),
            buf(5, 16, 8, 128),
            pltpu.SemaphoreType.DMA((N_SEM,)),
            pltpu.SemaphoreType.DMA((N_SEM,)),
            pltpu.SemaphoreType.DMA((7,)),
        ],
        compiler_params=pltpu.CompilerParams(collective_id=0, has_side_effects=True, vmem_limit_bytes=LIMIT),
        name="step",
    )(fine, coarse, patch_ids, columns.T)
    return pl.pallas_call(
        copy_kernel,
        out_shape=(sds(5, 16, 8, 128), sds(5, 2, 32, 1024)),
        in_specs=[hb(), hb()],
        out_specs=(hb(), hb()),
        scratch_shapes=[pltpu.SemaphoreType.DMA((15,))],
        compiler_params=pltpu.CompilerParams(vmem_limit_bytes=LIMIT),
        name="copy_out",
    )(co, fo)


def solution(mesh):
    return jax.shard_map(
        local,
        mesh=mesh,
        in_specs=(
            P(None, "slab", "patch", None),
            P(None, ("slab", "patch"), None, None),
            P(),
            P("slab", None),
        ),
        out_specs=(P(None, "slab", "patch", None), P(None, ("slab", "patch"), None, None)),
        check_vma=False,
    )
```

```python
import jax
import jax.numpy as jnp
from jax import lax
from jax.experimental import pallas as pl
from jax.experimental.pallas import tpu as pltpu
from jax.sharding import PartitionSpec as P

F32 = jnp.float32
BF16 = jnp.bfloat16
I32 = jnp.int32
MESH = pl.DeviceIdType.MESH
NS = 8
NP = 16
GOFF = 16


def iota(shape, dim):
    return lax.broadcasted_iota(I32, shape, dim)


def dot3(x, m):
    hi = x.astype(BF16)
    r = x - hi.astype(F32)
    mid = r.astype(BF16)
    lo = (r - mid.astype(F32)).astype(BF16)
    d = lambda a: jnp.dot(a, m, preferred_element_type=F32)
    return d(hi) + (d(mid) + d(lo))


def dot3_left(m, x):
    hi = x.astype(BF16)
    r = x - hi.astype(F32)
    mid = r.astype(BF16)
    lo = (r - mid.astype(F32)).astype(BF16)
    d = lambda a: jnp.dot(m, a, preferred_element_type=F32)
    return d(hi) + (d(mid) + d(lo))


def moved(x, k):
    return pltpu.roll(x, k % 128, 1) if k % 128 else x


def ones_where(c):
    return jnp.where(c, 1.0, 0.0).astype(BF16)


def state(q):
    r = 1.0 / q[0]
    p = 0.4 * (q[4] - 0.5 * ((q[1] * q[1] + q[2] * q[2] + q[3] * q[3]) * r))
    c = jnp.sqrt(1.4 * p * r)
    return r, p, c


def flux(q, s, d):
    r, p, c = s
    u = q[1 + d] * r
    f = [q[1 + d], q[1] * u, q[2] * u, q[3] * u, (q[4] + p) * u]
    f[1 + d] = f[1 + d] + p
    return f, jnp.abs(u) + c


def rusanov(ql, fl, al, qr, fr, ar):
    a = 0.5 * jnp.maximum(al, ar)
    return [0.5 * (fl[v] + fr[v]) - a * (qr[v] - ql[v]) for v in range(5)]


def provisional(s, me, coarse, oz, ocx, grid, prov):
    r = me // 2
    h = lax.rem(me, 2)
    lane = iota((8, 128), 1)
    sub = iota((8, 128), 0)
    blocks = lane // 16

    def cover(row):
        m = jnp.zeros((8, 128), F32)
        for gy in range(6):
            m = jnp.where((blocks == gy + 1) & (grid[0, gy + 8 * (row - 1) + GOFF] >= 0), 1.0, m)
        return m

    mid = cover(r)
    below = jnp.where(h == 0, cover(r - 1), mid)
    above = jnp.where(h == 1, cover(r + 1), mid)
    free = 1.0 - mid
    fup = free * (1.0 - pltpu.roll(mid, 127, 1))
    flo = free * (1.0 - pltpu.roll(mid, 1, 1))
    zlo = free * (1.0 - jnp.where(sub == 0, below, mid))
    zhi = free * (1.0 - jnp.where(sub == 7, above, mid))

    def cells(x):
        q = [coarse[v, x] for v in range(5)]
        st = state(q)
        return q, st, flux(q, st, 0)

    def face(a, b):
        return rusanov(a[0], a[2][0], a[2][1], b[0], b[2][0], b[2][1])

    first = cells(0)
    q = [jnp.where(s == 0, coarse[v, 0], ocx[0, v]) for v in range(5)]
    st = state(q)
    lower = face((q, st, flux(q, st, 0)), first)
    here = first
    for x in range(16):
        if x < 15:
            there = cells(x + 1)
        else:
            q = [jnp.where(s == NS - 1, coarse[v, 15], ocx[1, v]) for v in range(5)]
            st = state(q)
            there = (q, st, flux(q, st, 0))
        upper = face(here, there)
        q, st, _ = here
        change = [(upper[v] - lower[v]) * free for v in range(5)]
        row = slice(x, x + 1)
        zn = [jnp.where(sub == 7, jnp.where(me == NP - 1, q[v], oz[1, v, row, :]), pltpu.roll(q[v], 7, 0)) for v in range(5)]
        zb = [jnp.where(sub == 0, jnp.where(me == 0, q[v], oz[0, v, row, :]), pltpu.roll(q[v], 1, 0)) for v in range(5)]
        f, a = flux(q, st, 2)
        fn, an = flux(zn, state(zn), 2)
        fb, ab = flux(zb, state(zb), 2)
        up = rusanov(q, f, a, zn, fn, an)
        lo = rusanov(zb, fb, ab, q, f, a)
        change = [change[v] + (up[v] * zhi - lo[v] * zlo) for v in range(5)]
        f, a = flux(q, st, 1)
        nxt = lambda t: jnp.where(lane == 127, t, pltpu.roll(t, 127, 1))
        prv = lambda t: jnp.where(lane == 0, t, pltpu.roll(t, 1, 1))
        up = rusanov(q, f, a, [nxt(t) for t in q], [nxt(t) for t in f], nxt(a))
        lo = rusanov([prv(t) for t in q], [prv(t) for t in f], prv(a), q, f, a)
        for v in range(5):
            prov[v, x] = q[v] - 0.05 * (change[v] + (up[v] * fup - lo[v] * flo))
        here = there
        lower = upper
    return mid


N1 = NP - 1
S_X = N1
S_H = S_X + 2 * NP
S_G = S_H + 4
S_A = S_G + N1
S_E = S_A + N1
N_SEM = S_E + N1


def step_kernel(
    fine, coarse, ids_in, cols_in, fs, prov,
    ids, cols, nbr, grid, fb, cb, a1, x1, rz, ct, pk, ba, bx, cg, dd, og, oz, ocx,
    gh, bf, xg, xo, avs, av, bb, ee, oe, big, chg, ss, rs, ls,
):
    s = lax.axis_index("slab")
    me = lax.axis_index("patch")
    half = lax.rem(me, 2)
    up = lax.rem(s + 1, NS)
    down = lax.rem(s + NS - 1, NS)
    peer = [lax.rem(me + d, NP) for d in range(NP)]
    loads = [pltpu.make_async_copy(fine.at[v], fb.at[v], ls.at[v]) for v in range(5)]
    loads.append(pltpu.make_async_copy(coarse, cb, ls.at[5]))
    loads.append(pltpu.make_async_copy(ids_in, ids, ls.at[6]))
    loads.append(pltpu.make_async_copy(cols_in, cols, ls.at[7]))
    barrier = pltpu.get_barrier_semaphore()
    for c in loads:
        c.start()
    for d in range(NP):
        if d:
            pl.semaphore_signal(barrier, inc=1, device_id=(s, peer[d]), device_id_type=MESH)
        pl.semaphore_signal(barrier, inc=1, device_id=(up, peer[d]), device_id_type=MESH)
        pl.semaphore_signal(barrier, inc=1, device_id=(down, peer[d]), device_id_type=MESH)

    def copy(k, src, dst, dev):
        return pltpu.make_async_remote_copy(
            src_ref=src, dst_ref=dst, send_sem=ss.at[k], recv_sem=rs.at[k],
            device_id=dev, device_id_type=MESH,
        )

    k = iota((1024, 128), 0)
    c = iota((1024, 128), 1)
    g = c // 32
    i = lax.rem(c, 32)
    want = jnp.where(g == 0, 32 * i + 31, jnp.where(g == 1, 32 * i, jnp.where(g == 2, 992 + i, i)))
    sel = ones_where(k == want)
    for v in range(5):
        loads[v].wait()
        for p in range(2):
            pk[p, v] = dot3(fb[v, p], sel)
            for xr in range(2):
                a1[:, p, 5 * xr + v, :] = pk[p, v, pl.ds(xr, 16, 2), :]
    loads[6].wait()
    loads[7].wait()
    lane = iota((5, 128), 1)
    tag = jnp.where(iota((3, 128), 1) < 64, ids[0, 2 * me], ids[0, 2 * me + 1]).astype(F32)
    for d, row in ((0, 0), (1, 31)):
        for j in range(8):
            t0 = fb[:, 0, row, 128 * j : 128 * j + 128]
            t1 = fb[:, 1, row, 128 * j : 128 * j + 128]
            xo[:, d, 128 * j : 128 * j + 128] = t0
            xo[:, 2 + d, 128 * j : 128 * j + 128] = t1
            x1[d, 2 * j, 0:5, :] = jnp.where(lane < 64, t0, pltpu.roll(t1, 64, 1))
            x1[d, 2 * j + 1, 0:5, :] = jnp.where(lane < 64, pltpu.roll(t0, 64, 1), t1)
            x1[d, 2 * j, 5:8, :] = tag
            x1[d, 2 * j + 1, 5:8, :] = tag
    loads[5].wait()
    for v in range(5):
        for z in range(8):
            ct[z, 16 * v : 16 * v + 16, :] = cb[v, :, z, :]
    y = iota((128, 128), 0)
    k = iota((128, 128), 1) // 8
    plane = jnp.where(k < 6, 16 * (k + 1) - 1, jnp.where(k < 12, 16 * (k - 4), -1))
    sel = ones_where(y == plane)
    lane8 = lax.rem(iota((80, 128), 1), 8)
    acc = jnp.zeros((80, 128), F32)
    for z in range(8):
        acc = jnp.where(lane8 == z, dot3(ct[z], sel), acc)
    first = ct[0]
    last = ct[7]
    own = jnp.where(half == 0, first, last)
    for v in range(5):
        cut = slice(16 * v, 16 * v + 16)
        a1[:, 0, 10 + v, :] = acc[cut]
        a1[:, 1, 10 + v, :] = own[cut]
        rz[0, v] = first[cut]
        rz[1, v] = last[cut]
    a1[:, 0, 15, :] = jnp.zeros((16, 128), F32)
    a1[:, 1, 15, :] = jnp.zeros((16, 128), F32)

    pl.semaphore_wait(barrier, 3 * NP - 1)
    one = []
    two = []
    for d in range(NP):
        j = peer[d]
        if d:
            one.append(copy(d - 1, a1.at[j], ba.at[pl.ds(2 * me, 2)], (s, j)))
            one[-1].start()
        for c in (
            copy(S_X + 2 * d, x1.at[0, j], bx.at[1, me], (down, j)),
            copy(S_X + 2 * d + 1, x1.at[1, j], bx.at[0, me], (up, j)),
        ):
            c.start()
            one.append(c)
    two = [
        copy(S_H, cb.at[:, 0], ocx.at[1], (down, me)),
        copy(S_H + 1, cb.at[:, 15], ocx.at[0], (up, me)),
        copy(S_H + 2, rz.at[1], oz.at[0], (s, peer[1])),
        copy(S_H + 3, rz.at[0], oz.at[1], (s, peer[N1])),
    ]
    for c in two:
        c.start()
    own = pltpu.make_async_copy(a1.at[me], ba.at[pl.ds(2 * me, 2)], ls.at[6])
    own.start()

    def place(t, _):
        n = ids[0, t]
        gy = cols[0, n]
        gz = cols[1, n]
        nbr[4, t] = gy
        nbr[5, t] = gz
        nbr[6, t] = gy + 8 * gz + GOFF
        return 0

    lax.fori_loop(0, 32, place, 0)
    for i in range(GOFF):
        grid[0, i] = jnp.int32(-1)

    def find(k, _):
        q = jnp.int32(-1)
        for t in range(32):
            q = jnp.where(nbr[6, t] == k, t, q)
        grid[0, k] = q
        return 0

    lax.fori_loop(GOFF, GOFF + 48, find, 0)
    for i in range(GOFF + 48, 96):
        grid[0, i] = jnp.int32(-1)

    def look(t, _):
        for g, step in enumerate((-1, 1, -8, 8)):
            nbr[g, t] = grid[0, nbr[6, t] + step]
        return 0

    lax.fori_loop(0, 32, look, 0)

    src = iota((1024, 256), 0)
    dst = iota((1024, 256), 1)
    zz = 8 * (dst // 128) + 7 - lax.rem(dst, 128) // 16
    pair = ones_where((src // 64 == zz) & (lax.rem(src, 32) // 2 == lax.rem(dst, 16)))

    def interior(p):
        def along_x(j, _):
            cut = pl.ds(pl.multiple_of(128 * j, 128), 128)
            q = [fb[v, p, :, cut] for v in range(5)]
            f, a = flux(q, state(q), 0)
            nxt = lambda t: pltpu.roll(t, 31, 0)
            hi = rusanov(q, f, a, [nxt(t) for t in q], [nxt(t) for t in f], nxt(a))
            inner = iota((32, 128), 0) < 31
            for v in range(5):
                t = jnp.where(inner, hi[v], 0.0)
                chg[v, :, cut] = t - pltpu.roll(t, 1, 0)
            return 0

        lax.fori_loop(0, 8, along_x, 0)

        def rows(c, _):
            cut = pl.ds(pl.multiple_of(8 * c, 8), 8)
            q = [fb[v, p, cut, :] for v in range(5)]
            st = state(q)
            l8 = iota((8, 1024), 1)
            change = [chg[v, cut, :] for v in range(5)]
            for way, shift, inner in ((2, 32, l8 < 992), (1, 1, (l8 & 31) < 31)):
                f, a = flux(q, st, way)
                nxt = lambda t: pltpu.roll(t, 1024 - shift, 1)
                hi = rusanov(q, f, a, [nxt(t) for t in q], [nxt(t) for t in f], nxt(a))
                for v in range(5):
                    t = jnp.where(inner, hi[v], 0.0)
                    change[v] = change[v] + (t - pltpu.roll(t, shift, 1))
            for v in range(5):
                fs[v, p, cut, :] = q[v] - 0.1 * change[v]
            return 0

        lax.fori_loop(0, 4, rows, 0)
        for v in range(5):
            m = dot3(fs[v, p], pair)
            for h in range(2):
                big[h, 0:32, :] = m[:, 128 * h : 128 * h + 128]
                avs[p, v, h] = 0.125 * (big[h, pl.ds(0, 16, 2), :] + big[h, pl.ds(1, 16, 2), :])

    interior(0)
    src = iota((128, 128), 0)
    dst = iota((128, 128), 1)
    g = dst // 32
    i = lax.rem(dst, 32) // 2
    base = jnp.where(g == 0, 0, jnp.where(g == 1, 48, jnp.where(g == 2, 64, 80)))
    spread = ones_where(src == base + i)
    own.wait()
    for c in one:
        c.wait()

    lane = iota((8, 128), 1)

    def place_coarse(j, _):
        for p in range(2):
            slot = 2 * j + p
            gy = nbr[4, slot]
            gz = nbr[5, slot]
            a = 4 * (gz + 1)
            r0 = pltpu.roll(ba[a, 8:16, :], (128 - 8 * gy) & 127, 1)
            r1 = pltpu.roll(ba[a + 2, 8:16, :], (136 - 8 * gy) & 127, 1)
            r2 = pltpu.roll(ba[4 * gz + 3, 8:16, :], (176 - 16 * gy) & 127, 1)
            r3 = pltpu.roll(ba[4 * gz + 9, 8:16, :], (192 - 16 * gy) & 127, 1)
            cg[slot] = jnp.where(lane < 64, jnp.where((lane & 8) == 0, r0, r1), jnp.where(lane < 80, r2, r3))
        return 0

    lax.fori_loop(0, NP, place_coarse, 0, unroll=2)
    cg[...] = dot3(cg[...].reshape(256, 128), spread).reshape(32, 8, 128)
    sub = iota((32, 128), 0)
    want = jnp.zeros((32, 128), I32)
    for j in range(NP):
        for p in range(2):
            want = jnp.where(sub == NP * p + j, ids[0, 2 * j + p], want)
    want = want.astype(F32)
    l16 = iota((16, 128), 1)
    diagonal = l16 == iota((16, 128), 0)
    for way in range(2):
        tag = bx[way, :, 5, :]
        data = jnp.concatenate([bx[way, :, v, :] for v in range(5)], axis=1)
        got = []
        for t in range(2):
            tt = pltpu.roll(tag, 64, 1) if t else tag
            row = jnp.sum(jnp.where(diagonal, tt, 0.0), axis=0, keepdims=True)
            got.append(dot3_left(ones_where(want == row)[:, 0:16], data))
        for v in range(5):
            g0 = got[0][:, 128 * v : 128 * v + 128]
            g1 = got[1][:, 128 * v : 128 * v + 128]
            lo = g0[0:16] + pltpu.roll(g1[0:16], 64, 1)
            hi = pltpu.roll(g0[16:32], 64, 1) + g1[16:32]
            dd[:, way, 10 + v, :] = jnp.where(l16 < 64, lo, hi)
        dd[:, way, 15, :] = jnp.zeros((16, 128), F32)
    group = iota((10, 128), 1) // 32

    def select(j):
        for p in range(2):
            slot = 2 * j + p
            c = cg[slot, 2:7, :]
            val = jnp.concatenate([c, c], axis=0)
            for g in range(4):
                q = nbr[g, slot]
                val = jnp.where((group == g) & (q >= 0), ba[jnp.maximum(q, 0), 0:10, :], val)
            dd[j, p, 0:10, :] = val

    def selected(d):
        j = lax.rem(me + d, NP)
        return copy(S_G + d - 1, dd.at[j], og.at[me], (s, j))

    def select_send(d, _):
        select(lax.rem(me + d, NP))
        selected(d).start()
        return 0

    lax.fori_loop(1, NP, select_send, 0)
    select(me)
    own = pltpu.make_async_copy(dd.at[me], og.at[me], ls.at[6])
    own.start()
    interior(1)

    src = iota((128, 256), 0)
    dst = iota((128, 256), 1)
    g = src // 32
    i = lax.rem(src, 32) // 2
    zz = 8 * (dst // 128) + 7 - lax.rem(dst, 128) // 16
    yy = lax.rem(dst, 16)
    far = 15 * (g & 1)
    hit = (zz == jnp.where(g < 2, i, far)) & (yy == jnp.where(g < 2, far, i))
    sign = jnp.where((g & 1) == 0, -1.0, 1.0)
    mean_of = jnp.where(hit, sign, 0.0).astype(BF16)
    src = iota((128, 128), 0)
    dst = iota((128, 128), 1)
    g = src // 32
    i = lax.rem(src, 32) // 2
    z_at = 64 * (i // 8) + 7 - lax.rem(i, 8)
    at = jnp.where(g == 0, z_at, jnp.where(g == 1, z_at + 17, jnp.where(g == 2, 96 + i, 32 + i)))
    reflux = ones_where(dst == at)
    l1 = iota((1, 128), 1)
    low = ((l1 & 63) < 8) | (l1 >= 96)
    coef = jnp.where(low, -0.05, 0.05).astype(F32) * 0.25
    src = iota((128, 1024), 0)
    dst = iota((128, 1024), 1)
    g = src // 32
    i = lax.rem(src, 32)
    at = jnp.where(g == 0, 32 * i, jnp.where(g == 1, 32 * i + 31, jnp.where(g == 2, i, 992 + i)))
    sign = jnp.where((g & 1) == 0, -1.0, 1.0)
    expand = jnp.where(dst == at, sign, 0.0).astype(BF16)
    own.wait()
    for d in range(1, NP):
        two.append(selected(d))
    for c in two:
        c.wait()

    g1 = iota((32, 128), 1)
    low = ((g1 // 32) & 1) == 0
    isy = g1 < 64

    def face_flux(q):
        r, pr, c = state(q)
        mn = jnp.where(isy, q[2], q[3])
        u = mn * r
        py = jnp.where(isy, pr, 0.0)
        f = [mn, q[1] * u, q[2] * u + py, q[3] * u + (pr - py), (q[4] + pr) * u]
        return f, jnp.abs(u) + c

    for p in range(2):
        for v in range(5):
            for xr in range(2):
                gh[v, pl.ds(xr, 16, 2), :] = og[:, p, 5 * xr + v, :]
        theirs = [gh[v] for v in range(5)]
        mine = [jnp.where(low, pltpu.roll(pk[p, v], 96, 1), pltpu.roll(pk[p, v], 32, 1)) for v in range(5)]
        ql = [jnp.where(low, theirs[v], mine[v]) for v in range(5)]
        qr = [jnp.where(low, mine[v], theirs[v]) for v in range(5)]
        fl, al = face_flux(ql)
        fr, ar = face_flux(qr)
        f = rusanov(ql, fl, al, qr, fr, ar)
        for v in range(5):
            bf[160 * p + 32 * v : 160 * p + 32 * v + 32, :] = f[v]
    l5 = iota((5, 128), 1)
    for way in range(2):
        for j in range(8):
            e = og[2 * j, way, 10:15, :]
            o = og[2 * j + 1, way, 10:15, :]
            cut = slice(128 * j, 128 * j + 128)
            xg[:, way, cut] = jnp.where(l5 < 64, e, pltpu.roll(o, 64, 1))
            xg[:, 2 + way, cut] = jnp.where(l5 < 64, pltpu.roll(e, 64, 1), o)
    row = iota((4, 1024), 0)
    low = (row & 1) == 0
    edge = (row & 1) == jnp.where(s == 0, 0, jnp.where(s == NS - 1, 1, 2))
    mine = [xo[v] for v in range(5)]
    theirs = [jnp.where(edge, mine[v], xg[v]) for v in range(5)]
    ql = [jnp.where(low, theirs[v], mine[v]) for v in range(5)]
    qr = [jnp.where(low, mine[v], theirs[v]) for v in range(5)]
    fl, al = flux(ql, state(ql), 0)
    fr, ar = flux(qr, state(qr), 0)
    f = rusanov(ql, fl, al, qr, fr, ar)
    for v in range(5):
        xg[v] = jnp.where(low, -f[v], f[v])
    fluxes = bf[...]
    m = dot3(fluxes, mean_of)
    big[0] = m[:, 0:128]
    big[1] = m[:, 128:256]
    big[2] = dot3(fluxes, reflux)
    l16 = iota((16, 128), 1)
    for p in range(2):
        gy = nbr[4, 2 * me + p]
        turn_a = (16 * gy + 32) & 127
        turn_y = 16 * gy
        turn_z = (16 * gy + 80) & 127
        yr = [jnp.zeros((16, 128), F32)] * 2
        zr = [jnp.zeros((16, 128), F32)] * 2
        for v in range(5):
            a = 160 * p + 32 * v
            t = [big[h, pl.ds(a, 16, 2), :] + big[h, pl.ds(a + 1, 16, 2), :] for h in range(3)]
            xm = dot3(xg[v, 2 * p : 2 * p + 2, :], pair)
            sub = iota((16, 128), 0)
            w = t[2] * coef
            for h in range(2):
                xh = xm[:, 128 * h : 128 * h + 128]
                fix = t[h] + jnp.where(sub == 0, xh[0:1], jnp.where(sub == 15, xh[1:2], 0.0))
                av[:, h, p, v, :] = pltpu.roll(avs[p, v, h] - 0.0125 * fix, turn_a, 1)
                yr[h] = jnp.where((l16 >= 25 * v) & (l16 < 25 * v + 25), moved(w, 25 * v - 64 * h), yr[h])
                zr[h] = jnp.where(l16 // 16 == 4 - v, moved(w, 16 * (4 - v) - 64 * h - 32), zr[h])
        for h in range(2):
            av[:, h, p, 5, :] = pltpu.roll(yr[h], turn_y, 1)
            av[:, h, p, 6, :] = pltpu.roll(zr[h], turn_z, 1)
            av[:, h, p, 7, :] = jnp.zeros((16, 128), F32)
    one = []
    for d in range(1, NP):
        one.append(copy(S_A + d - 1, av.at[peer[d]], bb.at[me], (s, peer[d])))
        one[-1].start()
    own = pltpu.make_async_copy(av.at[me], bb.at[me], ls.at[6])
    own.start()
    for p in range(2):
        for v in range(5):
            a = 160 * p + 32 * v
            fs[v, p] = fs[v, p] - 0.1 * dot3(bf[a : a + 32, :], expand)
            for way, x in ((0, 0), (1, 31)):
                fs[v, p, x : x + 1, :] = fs[v, p, x : x + 1, :] - 0.1 * xg[v, 2 * p + way : 2 * p + way + 1, :]
    lane = iota((8, 128), 1)
    sub = iota((8, 128), 0)
    block = lane // 16
    ring = (block + sub) & 7
    slope = lane + sub - 7
    own.wait()
    for c in one:
        c.wait()

    def expand_to(j):
        h = lax.rem(j, 2)
        r = j // 2
        far = r - 2 + 2 * h
        acc = [jnp.zeros((8, 128), F32)] * 5
        accy = [jnp.zeros((8, 128), F32)] * 5
        accz = jnp.zeros((8, 128), F32)
        covered = jnp.zeros((8, 128), F32)
        for gy in range(6):
            a = grid[0, gy + 8 * (r - 1) + GOFF]
            b = grid[0, gy + 8 * far + GOFF]
            a0 = jnp.maximum(a, 0)
            b0 = jnp.maximum(b, 0)
            t = bb[a0 // 2, h, a0 & 1]
            zt = bb[b0 // 2, h, b0 & 1, 6:7, :]
            covered = jnp.where((block == gy + 1) & (a >= 0), 1.0, covered)
            ina = (ring == gy + 1) & (a >= 0)
            accz = jnp.where((ring == gy + 1) & (b >= 0), zt, accz)
            for v in range(5):
                acc[v] = jnp.where(ina, t[v : v + 1], acc[v])
                off = (slope - 16 * gy - 25 * v) & 127
                accy[v] = jnp.where(((off == 0) | (off == 17)) & (a >= 0), t[5:6], accy[v])
        accz = pltpu.roll(accz, 0, 1, stride=16, stride_axis=0)
        for v in range(5):
            val = pltpu.roll(acc[v], 0, 1, stride=16, stride_axis=0)
            add = moved(pltpu.roll(accy[v], 0, 1, stride=1, stride_axis=0), 8 - 25 * v)
            add = add + jnp.where(sub == 7 * h, accz[v : v + 1], 0.0)
            ee[j, v] = jnp.where(covered > 0, val, add)

    def expanded(d):
        j = lax.rem(me + d, NP)
        return copy(S_E + d - 1, ee.at[j], oe.at[me], (s, j))

    def expand_send(d, _):
        expand_to(lax.rem(me + d, NP))
        expanded(d).start()
        return 0

    lax.fori_loop(1, NP, expand_send, 0)
    expand_to(me)
    own = pltpu.make_async_copy(ee.at[me], oe.at[me], ls.at[6])
    own.start()
    mid = provisional(s, me, cb, oz, ocx, grid, prov)
    own.wait()
    for d in range(1, NP):
        expanded(d).wait()
    for x in range(16):
        for v in range(5):
            e = oe[x, v]
            prov[v, x] = jnp.where(mid > 0, e, prov[v, x] + e)


def copy_kernel(a, b, a_out, b_out, sems):
    n = a.shape[0]
    copies = []
    for v in range(n):
        copies.append(pltpu.make_async_copy(b.at[v, 0], b_out.at[v, 0], sems.at[n + v]))
        copies.append(pltpu.make_async_copy(b.at[v, 1], b_out.at[v, 1], sems.at[2 * n + v]))
        copies.append(pltpu.make_async_copy(a.at[v], a_out.at[v], sems.at[v]))
    for c in copies:
        c.start()
    for c in copies:
        c.wait()


def vm():
    return pl.BlockSpec(memory_space=pltpu.VMEM)


def hb():
    return pl.BlockSpec(memory_space=pltpu.HBM)


def sds(*shape, dtype=F32):
    return jax.ShapeDtypeStruct(shape, dtype)


def buf(*shape):
    return pltpu.VMEM(shape, F32)


LIMIT = 48 << 20


def pin(x):
    return pltpu.with_memory_space_constraint(x, pltpu.HBM)


def local(coarse, fine, columns, patch_ids):
    fo, co = pl.pallas_call(
        step_kernel,
        out_shape=(sds(5, 2, 32, 1024), sds(5, 16, 8, 128)),
        in_specs=[hb()] * 4,
        out_specs=(vm(), vm()),
        scratch_shapes=[
            pltpu.SMEM((1, 32), I32),
            pltpu.SMEM((2, 32), I32),
            pltpu.SMEM((7, 32), I32),
            pltpu.SMEM((1, 96), I32),
            buf(5, 2, 32, 1024),
            buf(5, 16, 8, 128),
            buf(16, 2, 16, 128),
            buf(2, 16, 8, 128),
            buf(2, 5, 16, 128),
            buf(8, 80, 128),
            buf(2, 5, 32, 128),
            buf(32, 16, 128),
            buf(2, 16, 8, 128),
            buf(32, 8, 128),
            buf(16, 2, 16, 128),
            buf(16, 2, 16, 128),
            buf(2, 5, 16, 128),
            buf(2, 5, 8, 128),
            buf(5, 32, 128),
            buf(320, 128),
            buf(5, 4, 1024),
            buf(5, 4, 1024),
            buf(2, 5, 2, 16, 128),
            buf(16, 2, 2, 8, 128),
            buf(16, 2, 2, 8, 128),
            buf(16, 5, 8, 128),
            buf(16, 5, 8, 128),
            buf(3, 320, 128),
            buf(5, 32, 1024),
            pltpu.SemaphoreType.DMA((N_SEM,)),
            pltpu.SemaphoreType.DMA((N_SEM,)),
            pltpu.SemaphoreType.DMA((8,)),
        ],
        compiler_params=pltpu.CompilerParams(collective_id=0, has_side_effects=True, vmem_limit_bytes=LIMIT),
        name="step",
    )(pin(fine), pin(coarse), pin(patch_ids), pin(columns.T))
    return pl.pallas_call(
        copy_kernel,
        out_shape=(sds(5, 16, 8, 128), sds(5, 2, 32, 1024)),
        in_specs=[pl.BlockSpec(memory_space=pl.ANY)] * 2,
        out_specs=(hb(), hb()),
        scratch_shapes=[pltpu.SemaphoreType.DMA((15,))],
        compiler_params=pltpu.CompilerParams(vmem_limit_bytes=LIMIT),
        name="copy_out",
    )(co, fo)


def solution(mesh):
    return jax.shard_map(
        local,
        mesh=mesh,
        in_specs=(
            P(None, "slab", "patch", None),
            P(None, ("slab", "patch"), None, None),
            P(),
            P("slab", None),
        ),
        out_specs=(P(None, "slab", "patch", None), P(None, ("slab", "patch"), None, None)),
        check_vma=False,
    )
```

```python
import jax
import jax.numpy as jnp
from jax import lax
from jax.experimental import pallas as pl
from jax.experimental.pallas import tpu as pltpu
from jax.sharding import PartitionSpec as P

F32 = jnp.float32
BF16 = jnp.bfloat16
I32 = jnp.int32
MESH = pl.DeviceIdType.MESH
NS = 8
NP = 16
GOFF = 16


def iota(shape, dim):
    return lax.broadcasted_iota(I32, shape, dim)


def dot3(x, m):
    hi = x.astype(BF16)
    r = x - hi.astype(F32)
    mid = r.astype(BF16)
    lo = (r - mid.astype(F32)).astype(BF16)
    d = lambda a: jnp.dot(a, m, preferred_element_type=F32)
    return d(hi) + (d(mid) + d(lo))


def dot3_left(m, x):
    hi = x.astype(BF16)
    r = x - hi.astype(F32)
    mid = r.astype(BF16)
    lo = (r - mid.astype(F32)).astype(BF16)
    d = lambda a: jnp.dot(m, a, preferred_element_type=F32)
    return d(hi) + (d(mid) + d(lo))


def moved(x, k):
    return pltpu.roll(x, k % 128, 1) if k % 128 else x


def ones_where(c):
    return jnp.where(c, 1.0, 0.0).astype(BF16)


def state(q):
    r = 1.0 / q[0]
    p = 0.4 * (q[4] - 0.5 * ((q[1] * q[1] + q[2] * q[2] + q[3] * q[3]) * r))
    c = jnp.sqrt(1.4 * p * r)
    return r, p, c


def flux(q, s, d):
    r, p, c = s
    u = q[1 + d] * r
    f = [q[1 + d], q[1] * u, q[2] * u, q[3] * u, (q[4] + p) * u]
    f[1 + d] = f[1 + d] + p
    return f, jnp.abs(u) + c


def rusanov(ql, fl, al, qr, fr, ar):
    a = 0.5 * jnp.maximum(al, ar)
    return [0.5 * (fl[v] + fr[v]) - a * (qr[v] - ql[v]) for v in range(5)]


def provisional(s, me, coarse, oz, ocx, grid, prov):
    r = me // 2
    h = lax.rem(me, 2)
    lane = iota((8, 128), 1)
    sub = iota((8, 128), 0)
    blocks = lane // 16

    def cover(row):
        m = jnp.zeros((8, 128), F32)
        for gy in range(6):
            m = jnp.where((blocks == gy + 1) & (grid[0, gy + 8 * (row - 1) + GOFF] >= 0), 1.0, m)
        return m

    mid = cover(r)
    below = jnp.where(h == 0, cover(r - 1), mid)
    above = jnp.where(h == 1, cover(r + 1), mid)
    free = 1.0 - mid
    fup = free * (1.0 - pltpu.roll(mid, 127, 1))
    flo = free * (1.0 - pltpu.roll(mid, 1, 1))
    zlo = free * (1.0 - jnp.where(sub == 0, below, mid))
    zhi = free * (1.0 - jnp.where(sub == 7, above, mid))

    def cells(x):
        q = [coarse[v, x] for v in range(5)]
        st = state(q)
        return q, st, flux(q, st, 0)

    def face(a, b):
        return rusanov(a[0], a[2][0], a[2][1], b[0], b[2][0], b[2][1])

    first = cells(0)
    q = [jnp.where(s == 0, coarse[v, 0], ocx[0, v]) for v in range(5)]
    st = state(q)
    lower = face((q, st, flux(q, st, 0)), first)
    here = first
    for x in range(16):
        if x < 15:
            there = cells(x + 1)
        else:
            q = [jnp.where(s == NS - 1, coarse[v, 15], ocx[1, v]) for v in range(5)]
            st = state(q)
            there = (q, st, flux(q, st, 0))
        upper = face(here, there)
        q, st, _ = here
        change = [(upper[v] - lower[v]) * free for v in range(5)]
        row = slice(x, x + 1)
        zn = [jnp.where(sub == 7, jnp.where(me == NP - 1, q[v], oz[1, v, row, :]), pltpu.roll(q[v], 7, 0)) for v in range(5)]
        zb = [jnp.where(sub == 0, jnp.where(me == 0, q[v], oz[0, v, row, :]), pltpu.roll(q[v], 1, 0)) for v in range(5)]
        f, a = flux(q, st, 2)
        fn, an = flux(zn, state(zn), 2)
        fb, ab = flux(zb, state(zb), 2)
        up = rusanov(q, f, a, zn, fn, an)
        lo = rusanov(zb, fb, ab, q, f, a)
        change = [change[v] + (up[v] * zhi - lo[v] * zlo) for v in range(5)]
        f, a = flux(q, st, 1)
        nxt = lambda t: jnp.where(lane == 127, t, pltpu.roll(t, 127, 1))
        prv = lambda t: jnp.where(lane == 0, t, pltpu.roll(t, 1, 1))
        up = rusanov(q, f, a, [nxt(t) for t in q], [nxt(t) for t in f], nxt(a))
        lo = rusanov([prv(t) for t in q], [prv(t) for t in f], prv(a), q, f, a)
        for v in range(5):
            prov[v, x] = q[v] - 0.05 * (change[v] + (up[v] * fup - lo[v] * flo))
        here = there
        lower = upper
    return mid


N1 = NP - 1
S_X = N1
S_H = S_X + 2 * NP
S_G = S_H + 4
S_A = S_G + N1
S_E = S_A + N1
N_SEM = S_E + N1


def step_kernel(
    fine, coarse, ids_in, cols_in, fs, prov,
    ids, cols, nbr, grid, fb, cb, a1, x1, rz, ct, pk, ba, bx, cg, dd, og, oz, ocx,
    bf, xg, av, bb, cc, xt, tt, ee, oe, big, chg, ss, rs, ls,
):
    s = lax.axis_index("slab")
    me = lax.axis_index("patch")
    half = lax.rem(me, 2)
    up = lax.rem(s + 1, NS)
    down = lax.rem(s + NS - 1, NS)
    peer = [lax.rem(me + d, NP) for d in range(NP)]
    loads = [pltpu.make_async_copy(fine.at[v], fb.at[v], ls.at[v]) for v in range(5)]
    loads.append(pltpu.make_async_copy(coarse, cb, ls.at[5]))
    loads.append(pltpu.make_async_copy(ids_in, ids, ls.at[6]))
    loads.append(pltpu.make_async_copy(cols_in, cols, ls.at[7]))
    barrier = pltpu.get_barrier_semaphore()
    for c in loads:
        c.start()
    for d in range(NP):
        if d:
            pl.semaphore_signal(barrier, inc=1, device_id=(s, peer[d]), device_id_type=MESH)
        pl.semaphore_signal(barrier, inc=1, device_id=(up, peer[d]), device_id_type=MESH)
        pl.semaphore_signal(barrier, inc=1, device_id=(down, peer[d]), device_id_type=MESH)

    def copy(k, src, dst, dev):
        return pltpu.make_async_remote_copy(
            src_ref=src, dst_ref=dst, send_sem=ss.at[k], recv_sem=rs.at[k],
            device_id=dev, device_id_type=MESH,
        )

    k = iota((1024, 128), 0)
    c = iota((1024, 128), 1)
    g = c // 32
    i = lax.rem(c, 32)
    want = jnp.where(g == 0, 32 * i + 31, jnp.where(g == 1, 32 * i, jnp.where(g == 2, 992 + i, i)))
    sel = ones_where(k == want)
    for v in range(5):
        loads[v].wait()
        for p in range(2):
            pk[...] = dot3(fb[v, p], sel)
            for xr in range(2):
                a1[:, p, 5 * xr + v, :] = pk[pl.ds(xr, 16, 2), :]
    loads[6].wait()
    loads[7].wait()
    lane = iota((5, 128), 1)
    tag = jnp.where(iota((3, 128), 1) < 64, ids[0, 2 * me], ids[0, 2 * me + 1]).astype(F32)
    for d, row in ((0, 0), (1, 31)):
        for j in range(8):
            t0 = fb[:, 0, row, 128 * j : 128 * j + 128]
            t1 = fb[:, 1, row, 128 * j : 128 * j + 128]
            for o, t in (
                (0, jnp.where(lane < 64, t0, pltpu.roll(t1, 64, 1))),
                (1, jnp.where(lane < 64, pltpu.roll(t0, 64, 1), t1)),
            ):
                x1[d, 2 * j + o, 0:5, :] = t
                a1[2 * j + o, 2, 8 * d : 8 * d + 5, :] = t
            x1[d, 2 * j, 5:8, :] = tag
            x1[d, 2 * j + 1, 5:8, :] = tag
    loads[5].wait()
    for v in range(5):
        for z in range(8):
            ct[z, 16 * v : 16 * v + 16, :] = cb[v, :, z, :]
    y = iota((128, 128), 0)
    k = iota((128, 128), 1) // 8
    plane = jnp.where(k < 6, 16 * (k + 1) - 1, jnp.where(k < 12, 16 * (k - 4), -1))
    sel = ones_where(y == plane)
    lane8 = lax.rem(iota((80, 128), 1), 8)
    acc = jnp.zeros((80, 128), F32)
    for z in range(8):
        acc = jnp.where(lane8 == z, dot3(ct[z], sel), acc)
    first = ct[0]
    last = ct[7]
    own = jnp.where(half == 0, first, last)
    for v in range(5):
        cut = slice(16 * v, 16 * v + 16)
        a1[:, 0, 10 + v, :] = acc[cut]
        a1[:, 1, 10 + v, :] = own[cut]
        rz[0, v] = first[cut]
        rz[1, v] = last[cut]
    a1[:, 0, 15, :] = jnp.zeros((16, 128), F32)
    a1[:, 1, 15, :] = jnp.zeros((16, 128), F32)

    pl.semaphore_wait(barrier, 3 * NP - 1)
    one = []
    two = []
    for d in range(NP):
        j = peer[d]
        if d:
            one.append(copy(d - 1, a1.at[j], ba.at[me], (s, j)))
            one[-1].start()
        for c in (
            copy(S_X + 2 * d, x1.at[0, j], bx.at[1, me], (down, j)),
            copy(S_X + 2 * d + 1, x1.at[1, j], bx.at[0, me], (up, j)),
        ):
            c.start()
            one.append(c)
    two = [
        copy(S_H, cb.at[:, 0], ocx.at[1], (down, me)),
        copy(S_H + 1, cb.at[:, 15], ocx.at[0], (up, me)),
        copy(S_H + 2, rz.at[1], oz.at[0], (s, peer[1])),
        copy(S_H + 3, rz.at[0], oz.at[1], (s, peer[N1])),
    ]
    for c in two:
        c.start()
    own = pltpu.make_async_copy(a1.at[me], ba.at[me], ls.at[6])
    own.start()

    def place(t, _):
        n = ids[0, t]
        gy = cols[0, n]
        gz = cols[1, n]
        nbr[4, t] = gy
        nbr[5, t] = gz
        nbr[6, t] = gy + 8 * gz + GOFF
        return 0

    lax.fori_loop(0, 32, place, 0)
    src = iota((1024, 256), 0)
    dst = iota((1024, 256), 1)
    zz = 8 * (dst // 128) + 7 - lax.rem(dst, 128) // 16
    pair = ones_where((src // 64 == zz) & (lax.rem(src, 32) // 2 == lax.rem(dst, 16)))

    def interior(p):
        def along_x(j, _):
            cut = pl.ds(pl.multiple_of(128 * j, 128), 128)
            q = [fb[v, p, :, cut] for v in range(5)]
            f, a = flux(q, state(q), 0)
            nxt = lambda t: pltpu.roll(t, 31, 0)
            hi = rusanov(q, f, a, [nxt(t) for t in q], [nxt(t) for t in f], nxt(a))
            inner = iota((32, 128), 0) < 31
            for v in range(5):
                t = jnp.where(inner, hi[v], 0.0)
                chg[v, :, cut] = t - pltpu.roll(t, 1, 0)
            return 0

        lax.fori_loop(0, 8, along_x, 0)

        def rows(c, _):
            cut = pl.ds(pl.multiple_of(8 * c, 8), 8)
            q = [fb[v, p, cut, :] for v in range(5)]
            st = state(q)
            l8 = iota((8, 1024), 1)
            change = [chg[v, cut, :] for v in range(5)]
            for way, shift, inner in ((2, 32, l8 < 992), (1, 1, (l8 & 31) < 31)):
                f, a = flux(q, st, way)
                nxt = lambda t: pltpu.roll(t, 1024 - shift, 1)
                hi = rusanov(q, f, a, [nxt(t) for t in q], [nxt(t) for t in f], nxt(a))
                for v in range(5):
                    t = jnp.where(inner, hi[v], 0.0)
                    change[v] = change[v] + (t - pltpu.roll(t, shift, 1))
            for v in range(5):
                fs[v, p, cut, :] = q[v] - 0.1 * change[v]
            return 0

        lax.fori_loop(0, 4, rows, 0)
        for v in range(5):
            m = dot3(fs[v, p], pair)
            for h in range(2):
                big[h, 0:32, :] = m[:, 128 * h : 128 * h + 128]
                av[:, p, h, v, :] = 0.125 * (big[h, pl.ds(0, 16, 2), :] + big[h, pl.ds(1, 16, 2), :])
        for h in range(2):
            for v in range(5, 8):
                av[:, p, h, v, :] = jnp.zeros((16, 128), F32)

    interior(0)
    interior(1)
    early = []
    for d in range(1, NP):
        early.append(copy(S_A + d - 1, av.at[peer[d]], bb.at[me], (s, peer[d])))
        early[-1].start()
    own_av = pltpu.make_async_copy(av.at[me], bb.at[me], ls.at[7])
    own_av.start()
    for i in range(GOFF):
        grid[0, i] = jnp.int32(-1)

    def find(k, _):
        q = jnp.int32(-1)
        for t in range(32):
            q = jnp.where(nbr[6, t] == k, t, q)
        grid[0, k] = q
        return 0

    lax.fori_loop(GOFF, GOFF + 48, find, 0)
    for i in range(GOFF + 48, 96):
        grid[0, i] = jnp.int32(-1)

    src = iota((128, 128), 0)
    dst = iota((128, 128), 1)
    g = dst // 32
    i = lax.rem(dst, 32) // 2
    base = jnp.where(g == 0, 0, jnp.where(g == 1, 48, jnp.where(g == 2, 64, 80)))
    spread = ones_where(src == base + i)
    sub = iota((32, 128), 0)
    l1 = iota((1, 128), 1)
    want = jnp.zeros((32, 128), I32)
    code = jnp.zeros((32, 128), I32)
    codes = jnp.full((1, 128), -99, I32)
    for i in range(NP):
        for p in range(2):
            k = NP * p + i
            want = jnp.where(sub == k, ids[0, 2 * i + p], want)
            code = jnp.where(sub == k, nbr[6, 2 * i + p], code)
            codes = jnp.where(l1 == k, nbr[6, 2 * i + p], codes)
    want = want.astype(F32)
    own.wait()
    for c in one:
        c.wait()

    lane = iota((8, 128), 1)

    def place_coarse(j, _):
        for p in range(2):
            gy = nbr[4, 2 * j + p]
            gz = nbr[5, 2 * j + p]
            a = 2 * (gz + 1)
            r0 = pltpu.roll(ba[a, 0, 8:16, :], (128 - 8 * gy) & 127, 1)
            r1 = pltpu.roll(ba[a + 1, 0, 8:16, :], (136 - 8 * gy) & 127, 1)
            r2 = pltpu.roll(ba[2 * gz + 1, 1, 8:16, :], (176 - 16 * gy) & 127, 1)
            r3 = pltpu.roll(ba[2 * gz + 4, 1, 8:16, :], (192 - 16 * gy) & 127, 1)
            cg[NP * p + j] = jnp.where(lane < 64, jnp.where((lane & 8) == 0, r0, r1), jnp.where(lane < 80, r2, r3))
        return 0

    lax.fori_loop(0, NP, place_coarse, 0, unroll=2)
    cg[...] = dot3(cg[...].reshape(256, 128), spread).reshape(32, 8, 128)
    packs = [
        jnp.concatenate([ba[:, 0, k, :], ba[:, 1, k, :]], axis=0) for k in range(10)
    ]
    data = jnp.concatenate(packs, axis=1)
    group = iota((32, 128), 1) // 32
    near = []
    absent = jnp.zeros((32, 128), F32)
    for g, step in enumerate((-1, 1, -8, 8)):
        hit = codes == code + step
        near.append(dot3_left(ones_where(hit)[:, 0:32], data))
        some = jnp.sum(jnp.where(hit, 1.0, 0.0), axis=1, keepdims=True)
        absent = jnp.where(group == g, 1.0 - some, absent)
    theirs = []
    mine = []
    low = (group & 1) == 0
    for v in range(5):
        both = []
        for xr in range(2):
            k = 128 * (5 * xr + v)
            n = [t[:, k : k + 128] for t in near]
            n = jnp.where(group == 0, n[0], jnp.where(group == 1, n[1], jnp.where(group == 2, n[2], n[3])))
            both.append(jnp.where(absent > 0.5, cg[:, 2 + v, :], n))
        theirs.append(jnp.concatenate(both, axis=0))
        both = [jnp.where(low, pltpu.roll(packs[5 * xr + v], 96, 1), pltpu.roll(packs[5 * xr + v], 32, 1)) for xr in range(2)]
        mine.append(jnp.concatenate(both, axis=0))
    g1 = iota((64, 128), 1)
    low = ((g1 // 32) & 1) == 0
    isy = g1 < 64

    def face_flux(q):
        r, pr, c = state(q)
        mn = jnp.where(isy, q[2], q[3])
        u = mn * r
        py = jnp.where(isy, pr, 0.0)
        f = [mn, q[1] * u, q[2] * u + py, q[3] * u + (pr - py), (q[4] + pr) * u]
        return f, jnp.abs(u) + c

    ql = [jnp.where(low, theirs[v], mine[v]) for v in range(5)]
    qr = [jnp.where(low, mine[v], theirs[v]) for v in range(5)]
    fl, al = face_flux(ql)
    fr, ar = face_flux(qr)
    f = rusanov(ql, fl, al, qr, fr, ar)
    for v in range(5):
        for p in range(2):
            for xr in range(2):
                a = 32 * xr + 16 * p
                dd[:, p, 5 * xr + v, :] = f[v][a : a + 16]
    sums = jnp.concatenate([f[v][0:32] + f[v][32:64] for v in range(5)], axis=0)
    l16 = iota((16, 128), 1)
    diagonal = l16 == iota((16, 128), 0)
    sides = []
    for way in range(2):
        tag = bx[way, :, 5, :]
        data = jnp.concatenate([bx[way, :, v, :] for v in range(5)], axis=1)
        got = []
        for t in range(2):
            tt_ = pltpu.roll(tag, 64, 1) if t else tag
            row = jnp.sum(jnp.where(diagonal, tt_, 0.0), axis=0, keepdims=True)
            got.append(dot3_left(ones_where(want == row)[:, 0:16], data))
        theirs = []
        for v in range(5):
            g0 = got[0][:, 128 * v : 128 * v + 128]
            g1 = got[1][:, 128 * v : 128 * v + 128]
            a = g0[0:16] + pltpu.roll(g1[0:16], 64, 1)
            b = pltpu.roll(g0[16:32], 64, 1) + g1[16:32]
            t = jnp.where(l16 < 64, a, b)
            theirs.append(jnp.where(s == (0 if way == 0 else NS - 1), ba[:, 2, 8 * way + v, :], t))
        sides.append(theirs)
    mine = [jnp.concatenate([ba[:, 2, v, :], ba[:, 2, 8 + v, :]], axis=0) for v in range(5)]
    theirs = [jnp.concatenate([sides[0][v], sides[1][v]], axis=0) for v in range(5)]
    low = iota((32, 128), 0) < 16
    ql = [jnp.where(low, theirs[v], mine[v]) for v in range(5)]
    qr = [jnp.where(low, mine[v], theirs[v]) for v in range(5)]
    fl, al = flux(ql, state(ql), 0)
    fr, ar = flux(qr, state(qr), 0)
    f = rusanov(ql, fl, al, qr, fr, ar)
    fx = [jnp.where(low, -t, t) for t in f]
    for v in range(5):
        for way in range(2):
            dd[:, way, 10 + v, :] = fx[v][16 * way : 16 * way + 16]
    dd[:, 0, 15, :] = jnp.zeros((16, 128), F32)
    dd[:, 1, 15, :] = jnp.zeros((16, 128), F32)

    late = []
    for d in range(1, NP):
        late.append(copy(S_G + d - 1, dd.at[peer[d]], og.at[me], (s, peer[d])))
        late[-1].start()
    own = pltpu.make_async_copy(dd.at[me], og.at[me], ls.at[6])
    own.start()

    src = iota((128, 256), 0)
    dst = iota((128, 256), 1)
    g = src // 32
    i = lax.rem(src, 32) // 2
    zz = 8 * (dst // 128) + 7 - lax.rem(dst, 128) // 16
    yy = lax.rem(dst, 16)
    far = 15 * (g & 1)
    hit = (zz == jnp.where(g < 2, i, far)) & (yy == jnp.where(g < 2, far, i))
    sign = jnp.where((g & 1) == 0, -1.0, 1.0)
    mean_of = jnp.where(hit, sign, 0.0).astype(BF16)
    src = iota((128, 128), 0)
    dst = iota((128, 128), 1)
    g = src // 32
    i = lax.rem(src, 32) // 2
    z_at = 64 * (i // 8) + 7 - lax.rem(i, 8)
    at = jnp.where(g == 0, z_at, jnp.where(g == 1, z_at + 17, jnp.where(g == 2, 96 + i, 32 + i)))
    reflux = ones_where(dst == at)
    low = ((l1 & 63) < 8) | (l1 >= 96)
    coef = jnp.where(low, -0.05, 0.05).astype(F32) * 0.25
    fix = dot3(sums, mean_of) * -0.0125
    refl = dot3(sums, reflux) * coef
    l32 = iota((32, 128), 1)
    yr = [jnp.zeros((32, 128), F32)] * 2
    zr = [jnp.zeros((32, 128), F32)] * 2
    for v in range(5):
        w = refl[32 * v : 32 * v + 32]
        for h in range(2):
            cc[:, h, v, :] = fix[32 * v : 32 * v + 32, 128 * h : 128 * h + 128]
            yr[h] = jnp.where((l32 >= 25 * v) & (l32 < 25 * v + 25), moved(w, 25 * v - 64 * h), yr[h])
            zr[h] = jnp.where(l32 // 16 == 4 - v, moved(w, 16 * (4 - v) - 64 * h - 32), zr[h])
    for h in range(2):
        cc[:, h, 5, :] = moved(yr[h], -32)
        cc[:, h, 6, :] = moved(zr[h], 48)
        cc[:, h, 7, :] = jnp.zeros((32, 128), F32)
    src = iota((128, 128), 0)
    dst = iota((128, 128), 1)
    sums = jnp.concatenate(fx, axis=0)
    for p in range(2):
        m = dot3(sums, ones_where((src // 64 == p) & ((src & 31) // 2 == (dst & 15)))) * -0.0125
        for v in range(5):
            xt[:, p, v, :] = m[32 * v : 32 * v + 32]
        for v in range(5, 8):
            xt[:, p, v, :] = jnp.zeros((32, 128), F32)
    for c in two:
        c.wait()
    mid = provisional(s, me, cb, oz, ocx, grid, prov)
    own_av.wait()
    for c in early:
        c.wait()

    def turn(i, _):
        for p in range(2):
            gy = nbr[4, 2 * i + p]
            for h in range(2):
                tt[i, p, h] = pltpu.roll(bb[i, p, h] + cc[NP * p + i, h], (16 * gy + 32) & 127, 1)
        return 0

    lax.fori_loop(0, NP, turn, 0, unroll=2)
    lane = iota((8, 128), 1)
    sub = iota((8, 128), 0)
    block = lane // 16
    ring = (block + sub) & 7
    slope = lane + sub - 7
    def expand_to(j):
        h = lax.rem(j, 2)
        r = j // 2
        far = r - 2 + 2 * h
        acc = [jnp.zeros((8, 128), F32)] * 5
        accy = [jnp.zeros((8, 128), F32)] * 5
        accz = jnp.zeros((8, 128), F32)
        covered = jnp.zeros((8, 128), F32)
        side = [jnp.zeros((8, 128), F32)] * 2
        for gy in range(6):
            a = grid[0, gy + 8 * (r - 1) + GOFF]
            b = grid[0, gy + 8 * far + GOFF]
            a0 = jnp.maximum(a, 0)
            b0 = jnp.maximum(b, 0)
            t = tt[a0 // 2, a0 & 1, h]
            zt = tt[b0 // 2, b0 & 1, h, 6:7, :]
            for way in range(2):
                side[way] = jnp.where((block == gy + 1) & (a >= 0), xt[NP * way + a0 // 2, a0 & 1], side[way])
            covered = jnp.where((block == gy + 1) & (a >= 0), 1.0, covered)
            ina = (ring == gy + 1) & (a >= 0)
            accz = jnp.where((ring == gy + 1) & (b >= 0), zt, accz)
            for v in range(5):
                acc[v] = jnp.where(ina, t[v : v + 1], acc[v])
                off = (slope - 16 * gy - 25 * v) & 127
                accy[v] = jnp.where(((off == 0) | (off == 17)) & (a >= 0), t[5:6], accy[v])
        accz = pltpu.roll(accz, 0, 1, stride=16, stride_axis=0)
        for v in range(5):
            val = pltpu.roll(acc[v], 0, 1, stride=16, stride_axis=0)
            add = moved(pltpu.roll(accy[v], 0, 1, stride=1, stride_axis=0), 8 - 25 * v)
            add = add + jnp.where(sub == 7 * h, accz[v : v + 1], 0.0)
            ee[j, v] = jnp.where(covered > 0, val, add)
        ee[j, 5] = side[0]
        ee[j, 6] = side[1]

    def expanded(d):
        j = lax.rem(me + d, NP)
        return copy(S_E + d - 1, ee.at[j], oe.at[me], (s, j))

    def expand_send(d, _):
        expand_to(lax.rem(me + d, NP))
        expanded(d).start()
        return 0

    lax.fori_loop(1, NP, expand_send, 0)
    expand_to(me)
    own_ee = pltpu.make_async_copy(ee.at[me], oe.at[me], ls.at[7])
    own_ee.start()

    src = iota((128, 1024), 0)
    dst = iota((128, 1024), 1)
    g = src // 32
    i = lax.rem(src, 32)
    at = jnp.where(g == 0, 32 * i, jnp.where(g == 1, 32 * i + 31, jnp.where(g == 2, i, 992 + i)))
    sign = jnp.where((g & 1) == 0, -1.0, 1.0)
    expand = jnp.where(dst == at, sign, 0.0).astype(BF16)
    own.wait()
    for c in late:
        c.wait()
    l5 = iota((5, 128), 1)
    for way in range(2):
        for j in range(8):
            e = og[2 * j, way, 10:15, :]
            o = og[2 * j + 1, way, 10:15, :]
            cut = slice(128 * j, 128 * j + 128)
            xg[:, way, cut] = jnp.where(l5 < 64, e, pltpu.roll(o, 64, 1))
            xg[:, 2 + way, cut] = jnp.where(l5 < 64, pltpu.roll(e, 64, 1), o)
    for p in range(2):
        for v in range(5):
            for xr in range(2):
                bf[pl.ds(xr, 16, 2), :] = og[:, p, 5 * xr + v, :]
            fs[v, p] = fs[v, p] - 0.1 * dot3(bf[...], expand)
            for way, x in ((0, 0), (1, 31)):
                fs[v, p, x : x + 1, :] = fs[v, p, x : x + 1, :] - 0.1 * xg[v, 2 * p + way : 2 * p + way + 1, :]
    own_ee.wait()
    for d in range(1, NP):
        expanded(d).wait()
    for x in range(16):
        for v in range(5):
            e = oe[x, v]
            if x in (0, 15):
                e = e + oe[pl.ds(8 * half, 8), 5 + x // 15, v, :]
            prov[v, x] = jnp.where(mid > 0, e, prov[v, x] + e)


def copy_kernel(a, b, a_out, b_out, sems):
    n = a.shape[0]
    copies = []
    for v in range(n):
        copies.append(pltpu.make_async_copy(b.at[v, 0], b_out.at[v, 0], sems.at[n + v]))
        copies.append(pltpu.make_async_copy(b.at[v, 1], b_out.at[v, 1], sems.at[2 * n + v]))
        copies.append(pltpu.make_async_copy(a.at[v], a_out.at[v], sems.at[v]))
    for c in copies:
        c.start()
    for c in copies:
        c.wait()


def vm():
    return pl.BlockSpec(memory_space=pltpu.VMEM)


def hb():
    return pl.BlockSpec(memory_space=pltpu.HBM)


def sds(*shape, dtype=F32):
    return jax.ShapeDtypeStruct(shape, dtype)


def buf(*shape):
    return pltpu.VMEM(shape, F32)


LIMIT = 48 << 20


def pin(x):
    return pltpu.with_memory_space_constraint(x, pltpu.HBM)


def local(coarse, fine, columns, patch_ids):
    fo, co = pl.pallas_call(
        step_kernel,
        out_shape=(sds(5, 2, 32, 1024), sds(5, 16, 8, 128)),
        in_specs=[hb()] * 4,
        out_specs=(vm(), vm()),
        scratch_shapes=[
            pltpu.SMEM((1, 32), I32),
            pltpu.SMEM((2, 32), I32),
            pltpu.SMEM((7, 32), I32),
            pltpu.SMEM((1, 96), I32),
            buf(5, 2, 32, 1024),
            buf(5, 16, 8, 128),
            buf(16, 3, 16, 128),
            buf(2, 16, 8, 128),
            buf(2, 5, 16, 128),
            buf(8, 80, 128),
            buf(32, 128),
            buf(16, 3, 16, 128),
            buf(2, 16, 8, 128),
            buf(32, 8, 128),
            buf(16, 2, 16, 128),
            buf(16, 2, 16, 128),
            buf(2, 5, 16, 128),
            buf(2, 5, 8, 128),
            buf(32, 128),
            buf(5, 4, 1024),
            buf(16, 2, 2, 8, 128),
            buf(16, 2, 2, 8, 128),
            buf(32, 2, 8, 128),
            buf(32, 2, 8, 128),
            buf(16, 2, 2, 8, 128),
            buf(16, 7, 8, 128),
            buf(16, 7, 8, 128),
            buf(2, 32, 128),
            buf(5, 32, 1024),
            pltpu.SemaphoreType.DMA((N_SEM,)),
            pltpu.SemaphoreType.DMA((N_SEM,)),
            pltpu.SemaphoreType.DMA((8,)),
        ],
        compiler_params=pltpu.CompilerParams(collective_id=0, has_side_effects=True, vmem_limit_bytes=LIMIT),
        name="step",
    )(pin(fine), pin(coarse), pin(patch_ids), pin(columns.T))
    return pl.pallas_call(
        copy_kernel,
        out_shape=(sds(5, 16, 8, 128), sds(5, 2, 32, 1024)),
        in_specs=[pl.BlockSpec(memory_space=pl.ANY)] * 2,
        out_specs=(hb(), hb()),
        scratch_shapes=[pltpu.SemaphoreType.DMA((15,))],
        compiler_params=pltpu.CompilerParams(vmem_limit_bytes=LIMIT),
        name="copy_out",
    )(co, fo)


def solution(mesh):
    return jax.shard_map(
        local,
        mesh=mesh,
        in_specs=(
            P(None, "slab", "patch", None),
            P(None, ("slab", "patch"), None, None),
            P(),
            P("slab", None),
        ),
        out_specs=(P(None, "slab", "patch", None), P(None, ("slab", "patch"), None, None)),
        check_vma=False,
    )
```

```python
import jax
import jax.numpy as jnp
from jax import lax
from jax.experimental import pallas as pl
from jax.experimental.pallas import tpu as pltpu
from jax.sharding import PartitionSpec as P

F32 = jnp.float32
BF16 = jnp.bfloat16
I32 = jnp.int32
MESH = pl.DeviceIdType.MESH
NS = 8
NP = 16
GOFF = 16


def iota(shape, dim):
    return lax.broadcasted_iota(I32, shape, dim)


def dot3(x, m):
    hi = x.astype(BF16)
    r = x - hi.astype(F32)
    mid = r.astype(BF16)
    lo = (r - mid.astype(F32)).astype(BF16)
    d = lambda a: jnp.dot(a, m, preferred_element_type=F32)
    return d(hi) + (d(mid) + d(lo))


def dot3_left(m, x):
    hi = x.astype(BF16)
    r = x - hi.astype(F32)
    mid = r.astype(BF16)
    lo = (r - mid.astype(F32)).astype(BF16)
    d = lambda a: jnp.dot(m, a, preferred_element_type=F32)
    return d(hi) + (d(mid) + d(lo))


def moved(x, k):
    return pltpu.roll(x, k % 128, 1) if k % 128 else x


def ones_where(c):
    return jnp.where(c, 1.0, 0.0).astype(BF16)


def state(q):
    r = 1.0 / q[0]
    p = 0.4 * (q[4] - 0.5 * ((q[1] * q[1] + q[2] * q[2] + q[3] * q[3]) * r))
    c = jnp.sqrt(1.4 * p * r)
    return r, p, c


def flux(q, s, d):
    r, p, c = s
    u = q[1 + d] * r
    f = [q[1 + d], q[1] * u, q[2] * u, q[3] * u, (q[4] + p) * u]
    f[1 + d] = f[1 + d] + p
    return f, jnp.abs(u) + c


def rusanov(ql, fl, al, qr, fr, ar):
    a = 0.5 * jnp.maximum(al, ar)
    return [0.5 * (fl[v] + fr[v]) - a * (qr[v] - ql[v]) for v in range(5)]


def provisional(s, me, coarse, oz, ocx, grid, prov):
    r = me // 2
    h = lax.rem(me, 2)
    lane = iota((8, 128), 1)
    sub = iota((8, 128), 0)
    blocks = lane // 16

    def cover(row):
        m = jnp.zeros((8, 128), F32)
        for gy in range(6):
            m = jnp.where((blocks == gy + 1) & (grid[0, gy + 8 * (row - 1) + GOFF] >= 0), 1.0, m)
        return m

    mid = cover(r)
    below = jnp.where(h == 0, cover(r - 1), mid)
    above = jnp.where(h == 1, cover(r + 1), mid)
    free = 1.0 - mid
    fup = free * (1.0 - pltpu.roll(mid, 127, 1))
    flo = free * (1.0 - pltpu.roll(mid, 1, 1))
    zlo = free * (1.0 - jnp.where(sub == 0, below, mid))
    zhi = free * (1.0 - jnp.where(sub == 7, above, mid))

    def cells(x):
        q = [coarse[v, x] for v in range(5)]
        st = state(q)
        return q, st, flux(q, st, 0)

    def face(a, b):
        return rusanov(a[0], a[2][0], a[2][1], b[0], b[2][0], b[2][1])

    first = cells(0)
    q = [jnp.where(s == 0, coarse[v, 0], ocx[0, v]) for v in range(5)]
    st = state(q)
    lower = face((q, st, flux(q, st, 0)), first)
    here = first
    for x in range(16):
        if x < 15:
            there = cells(x + 1)
        else:
            q = [jnp.where(s == NS - 1, coarse[v, 15], ocx[1, v]) for v in range(5)]
            st = state(q)
            there = (q, st, flux(q, st, 0))
        upper = face(here, there)
        q, st, _ = here
        change = [(upper[v] - lower[v]) * free for v in range(5)]
        row = slice(x, x + 1)
        zn = [jnp.where(sub == 7, jnp.where(me == NP - 1, q[v], oz[1, v, row, :]), pltpu.roll(q[v], 7, 0)) for v in range(5)]
        zb = [jnp.where(sub == 0, jnp.where(me == 0, q[v], oz[0, v, row, :]), pltpu.roll(q[v], 1, 0)) for v in range(5)]
        f, a = flux(q, st, 2)
        fn, an = flux(zn, state(zn), 2)
        fb, ab = flux(zb, state(zb), 2)
        up = rusanov(q, f, a, zn, fn, an)
        lo = rusanov(zb, fb, ab, q, f, a)
        change = [change[v] + (up[v] * zhi - lo[v] * zlo) for v in range(5)]
        f, a = flux(q, st, 1)
        nxt = lambda t: jnp.where(lane == 127, t, pltpu.roll(t, 127, 1))
        prv = lambda t: jnp.where(lane == 0, t, pltpu.roll(t, 1, 1))
        up = rusanov(q, f, a, [nxt(t) for t in q], [nxt(t) for t in f], nxt(a))
        lo = rusanov([prv(t) for t in q], [prv(t) for t in f], prv(a), q, f, a)
        for v in range(5):
            prov[v, x] = q[v] - 0.05 * (change[v] + (up[v] * fup - lo[v] * flo))
        here = there
        lower = upper
    return mid


N1 = NP - 1
S_X = N1
S_H = S_X + 2 * NP
S_G = S_H + 4
S_A = S_G + N1
S_E = S_A + N1
S_S = S_E + N1
N_SEM = S_S + N1


def step_kernel(
    fine, coarse, ids_in, cols_in, fs, prov,
    ids, cols, nbr, grid, fb, cb, a1, x1, rz, ct, pk, ba, bx, cg, dd, og, oz, ocx,
    bf, xg, av, bb, cc, xt, tt, ee, oe, se, so, big, chg, ss, rs, ls,
):
    s = lax.axis_index("slab")
    me = lax.axis_index("patch")
    half = lax.rem(me, 2)
    up = lax.rem(s + 1, NS)
    down = lax.rem(s + NS - 1, NS)
    peer = [lax.rem(me + d, NP) for d in range(NP)]
    loads = [pltpu.make_async_copy(fine.at[v], fb.at[v], ls.at[v]) for v in range(5)]
    loads.append(pltpu.make_async_copy(coarse, cb, ls.at[5]))
    loads.append(pltpu.make_async_copy(ids_in, ids, ls.at[6]))
    loads.append(pltpu.make_async_copy(cols_in, cols, ls.at[7]))
    barrier = pltpu.get_barrier_semaphore()
    for c in loads:
        c.start()
    for d in range(NP):
        if d:
            pl.semaphore_signal(barrier, inc=1, device_id=(s, peer[d]), device_id_type=MESH)
        pl.semaphore_signal(barrier, inc=1, device_id=(up, peer[d]), device_id_type=MESH)
        pl.semaphore_signal(barrier, inc=1, device_id=(down, peer[d]), device_id_type=MESH)

    def copy(k, src, dst, dev):
        return pltpu.make_async_remote_copy(
            src_ref=src, dst_ref=dst, send_sem=ss.at[k], recv_sem=rs.at[k],
            device_id=dev, device_id_type=MESH,
        )

    k = iota((1024, 128), 0)
    c = iota((1024, 128), 1)
    g = c // 32
    i = lax.rem(c, 32)
    want = jnp.where(g == 0, 32 * i + 31, jnp.where(g == 1, 32 * i, jnp.where(g == 2, 992 + i, i)))
    sel = ones_where(k == want)
    for v in range(5):
        loads[v].wait()
        for p in range(2):
            pk[...] = dot3(fb[v, p], sel)
            for xr in range(2):
                a1[:, 16 * p + 5 * xr + v, :] = pk[pl.ds(xr, 16, 2), :]
    loads[6].wait()
    loads[7].wait()
    lane = iota((5, 128), 1)
    tag = jnp.where(iota((3, 128), 1) < 64, ids[0, 2 * me], ids[0, 2 * me + 1]).astype(F32)
    for d, row in ((0, 0), (1, 31)):
        for j in range(8):
            t0 = fb[:, 0, row, 128 * j : 128 * j + 128]
            t1 = fb[:, 1, row, 128 * j : 128 * j + 128]
            for o, t in (
                (0, jnp.where(lane < 64, t0, pltpu.roll(t1, 64, 1))),
                (1, jnp.where(lane < 64, pltpu.roll(t0, 64, 1), t1)),
            ):
                x1[d, 2 * j + o, 0:5, :] = t
                if d == 0:
                    a1[2 * j + o, 32:37, :] = t
                else:
                    a1[2 * j + o, 37:40, :] = t[0:3]
                    a1[2 * j + o, 15:16, :] = t[3:4]
                    a1[2 * j + o, 31:32, :] = t[4:5]
            x1[d, 2 * j, 5:8, :] = tag
            x1[d, 2 * j + 1, 5:8, :] = tag
    loads[5].wait()
    for v in range(5):
        for z in range(8):
            ct[z, 16 * v : 16 * v + 16, :] = cb[v, :, z, :]
    y = iota((128, 128), 0)
    k = iota((128, 128), 1) // 8
    plane = jnp.where(k < 6, 16 * (k + 1) - 1, jnp.where(k < 12, 16 * (k - 4), -1))
    sel = ones_where(y == plane)
    lane8 = lax.rem(iota((80, 128), 1), 8)
    acc = jnp.zeros((80, 128), F32)
    for z in range(8):
        acc = jnp.where(lane8 == z, dot3(ct[z], sel), acc)
    first = ct[0]
    last = ct[7]
    own = jnp.where(half == 0, first, last)
    for v in range(5):
        cut = slice(16 * v, 16 * v + 16)
        a1[:, 10 + v, :] = acc[cut]
        a1[:, 26 + v, :] = own[cut]
        rz[0, v] = first[cut]
        rz[1, v] = last[cut]

    pl.semaphore_wait(barrier, 3 * NP - 1)
    one = []
    two = []
    for d in range(NP):
        j = peer[d]
        if d:
            one.append(copy(d - 1, a1.at[j], ba.at[me], (s, j)))
            one[-1].start()
        for c in (
            copy(S_X + 2 * d, x1.at[0, j], bx.at[1, me], (down, j)),
            copy(S_X + 2 * d + 1, x1.at[1, j], bx.at[0, me], (up, j)),
        ):
            c.start()
            one.append(c)
    two = [
        copy(S_H, cb.at[:, 0], ocx.at[1], (down, me)),
        copy(S_H + 1, cb.at[:, 15], ocx.at[0], (up, me)),
        copy(S_H + 2, rz.at[1], oz.at[0], (s, peer[1])),
        copy(S_H + 3, rz.at[0], oz.at[1], (s, peer[N1])),
    ]
    for c in two:
        c.start()
    own = pltpu.make_async_copy(a1.at[me], ba.at[me], ls.at[6])
    own.start()

    def place(t, _):
        n = ids[0, t]
        gy = cols[0, n]
        gz = cols[1, n]
        nbr[4, t] = gy
        nbr[5, t] = gz
        nbr[6, t] = gy + 8 * gz + GOFF
        return 0

    lax.fori_loop(0, 32, place, 0)
    src = iota((1024, 256), 0)
    dst = iota((1024, 256), 1)
    zz = 8 * (dst // 128) + 7 - lax.rem(dst, 128) // 16
    pair = ones_where((src // 64 == zz) & (lax.rem(src, 32) // 2 == lax.rem(dst, 16)))

    def interior(p):
        def along_x(j, _):
            cut = pl.ds(pl.multiple_of(128 * j, 128), 128)
            q = [fb[v, p, :, cut] for v in range(5)]
            f, a = flux(q, state(q), 0)
            nxt = lambda t: pltpu.roll(t, 31, 0)
            hi = rusanov(q, f, a, [nxt(t) for t in q], [nxt(t) for t in f], nxt(a))
            inner = iota((32, 128), 0) < 31
            for v in range(5):
                t = jnp.where(inner, hi[v], 0.0)
                chg[v, :, cut] = t - pltpu.roll(t, 1, 0)
            return 0

        lax.fori_loop(0, 8, along_x, 0)

        def rows(c, _):
            cut = pl.ds(pl.multiple_of(8 * c, 8), 8)
            q = [fb[v, p, cut, :] for v in range(5)]
            st = state(q)
            l8 = iota((8, 1024), 1)
            change = [chg[v, cut, :] for v in range(5)]
            for way, shift, inner in ((2, 32, l8 < 992), (1, 1, (l8 & 31) < 31)):
                f, a = flux(q, st, way)
                nxt = lambda t: pltpu.roll(t, 1024 - shift, 1)
                hi = rusanov(q, f, a, [nxt(t) for t in q], [nxt(t) for t in f], nxt(a))
                for v in range(5):
                    t = jnp.where(inner, hi[v], 0.0)
                    change[v] = change[v] + (t - pltpu.roll(t, shift, 1))
            for v in range(5):
                fs[v, p, cut, :] = q[v] - 0.1 * change[v]
            return 0

        lax.fori_loop(0, 4, rows, 0)
        for v in range(5):
            m = dot3(fs[v, p], pair)
            for h in range(2):
                big[h, 0:32, :] = m[:, 128 * h : 128 * h + 128]
                av[:, 10 * p + 5 * h + v, :] = 0.125 * (big[h, pl.ds(0, 16, 2), :] + big[h, pl.ds(1, 16, 2), :])
        for k in range(2):
            av[:, 20 + 2 * p + k, :] = jnp.zeros((16, 128), F32)

    interior(0)
    interior(1)
    early = []
    for d in range(1, NP):
        early.append(copy(S_A + d - 1, av.at[peer[d]], bb.at[me], (s, peer[d])))
        early[-1].start()
    own_av = pltpu.make_async_copy(av.at[me], bb.at[me], ls.at[7])
    own_av.start()
    for i in range(GOFF):
        grid[0, i] = jnp.int32(-1)

    def find(k, _):
        q = jnp.int32(-1)
        for t in range(32):
            q = jnp.where(nbr[6, t] == k, t, q)
        grid[0, k] = q
        return 0

    lax.fori_loop(GOFF, GOFF + 48, find, 0)
    for i in range(GOFF + 48, 96):
        grid[0, i] = jnp.int32(-1)

    src = iota((128, 128), 0)
    dst = iota((128, 128), 1)
    g = dst // 32
    i = lax.rem(dst, 32) // 2
    base = jnp.where(g == 0, 0, jnp.where(g == 1, 48, jnp.where(g == 2, 64, 80)))
    spread = ones_where(src == base + i)
    sub = iota((32, 128), 0)
    l1 = iota((1, 128), 1)
    want = jnp.zeros((32, 128), I32)
    code = jnp.zeros((32, 128), I32)
    codes = jnp.full((1, 128), -99, I32)
    for i in range(NP):
        for p in range(2):
            k = NP * p + i
            want = jnp.where(sub == k, ids[0, 2 * i + p], want)
            code = jnp.where(sub == k, nbr[6, 2 * i + p], code)
            codes = jnp.where(l1 == k, nbr[6, 2 * i + p], codes)
    want = want.astype(F32)
    own.wait()
    for c in one:
        c.wait()

    lane = iota((8, 128), 1)

    def place_coarse(j, _):
        for p in range(2):
            gy = nbr[4, 2 * j + p]
            gz = nbr[5, 2 * j + p]
            a = 2 * (gz + 1)
            r0 = pltpu.roll(ba[a, 8:16, :], (128 - 8 * gy) & 127, 1)
            r1 = pltpu.roll(ba[a + 1, 8:16, :], (136 - 8 * gy) & 127, 1)
            r2 = pltpu.roll(ba[2 * gz + 1, 24:32, :], (176 - 16 * gy) & 127, 1)
            r3 = pltpu.roll(ba[2 * gz + 4, 24:32, :], (192 - 16 * gy) & 127, 1)
            cg[NP * p + j] = jnp.where(lane < 64, jnp.where((lane & 8) == 0, r0, r1), jnp.where(lane < 80, r2, r3))
        return 0

    lax.fori_loop(0, NP, place_coarse, 0, unroll=2)
    cg[...] = dot3(cg[...].reshape(256, 128), spread).reshape(32, 8, 128)
    packs = [
        jnp.concatenate([ba[:, k, :], ba[:, 16 + k, :]], axis=0) for k in range(10)
    ]
    data = jnp.concatenate(packs, axis=1)
    group = iota((32, 128), 1) // 32
    near = []
    absent = jnp.zeros((32, 128), F32)
    for g, step in enumerate((-1, 1, -8, 8)):
        hit = codes == code + step
        near.append(dot3_left(ones_where(hit)[:, 0:32], data))
        some = jnp.sum(jnp.where(hit, 1.0, 0.0), axis=1, keepdims=True)
        absent = jnp.where(group == g, 1.0 - some, absent)
    theirs = []
    mine = []
    low = (group & 1) == 0
    for v in range(5):
        both = []
        for xr in range(2):
            k = 128 * (5 * xr + v)
            n = [t[:, k : k + 128] for t in near]
            n = jnp.where(group == 0, n[0], jnp.where(group == 1, n[1], jnp.where(group == 2, n[2], n[3])))
            both.append(jnp.where(absent > 0.5, cg[:, 2 + v, :], n))
        theirs.append(jnp.concatenate(both, axis=0))
        both = [jnp.where(low, pltpu.roll(packs[5 * xr + v], 96, 1), pltpu.roll(packs[5 * xr + v], 32, 1)) for xr in range(2)]
        mine.append(jnp.concatenate(both, axis=0))
    g1 = iota((64, 128), 1)
    low = ((g1 // 32) & 1) == 0
    isy = g1 < 64

    def face_flux(q):
        r, pr, c = state(q)
        mn = jnp.where(isy, q[2], q[3])
        u = mn * r
        py = jnp.where(isy, pr, 0.0)
        f = [mn, q[1] * u, q[2] * u + py, q[3] * u + (pr - py), (q[4] + pr) * u]
        return f, jnp.abs(u) + c

    ql = [jnp.where(low, theirs[v], mine[v]) for v in range(5)]
    qr = [jnp.where(low, mine[v], theirs[v]) for v in range(5)]
    fl, al = face_flux(ql)
    fr, ar = face_flux(qr)
    f = rusanov(ql, fl, al, qr, fr, ar)
    for v in range(5):
        for p in range(2):
            for xr in range(2):
                a = 32 * xr + 16 * p
                dd[:, p, 5 * xr + v, :] = f[v][a : a + 16]
    sums = jnp.concatenate([f[v][0:32] + f[v][32:64] for v in range(5)], axis=0)
    l16 = iota((16, 128), 1)
    diagonal = l16 == iota((16, 128), 0)
    own_x = [32 + k for k in range(8)] + [15, 31]
    sides = []
    for way in range(2):
        tag = bx[way, :, 5, :]
        data = jnp.concatenate([bx[way, :, v, :] for v in range(5)], axis=1)
        got = []
        for t in range(2):
            tt_ = pltpu.roll(tag, 64, 1) if t else tag
            row = jnp.sum(jnp.where(diagonal, tt_, 0.0), axis=0, keepdims=True)
            got.append(dot3_left(ones_where(want == row)[:, 0:16], data))
        theirs = []
        for v in range(5):
            g0 = got[0][:, 128 * v : 128 * v + 128]
            g1 = got[1][:, 128 * v : 128 * v + 128]
            a = g0[0:16] + pltpu.roll(g1[0:16], 64, 1)
            b = pltpu.roll(g0[16:32], 64, 1) + g1[16:32]
            t = jnp.where(l16 < 64, a, b)
            theirs.append(jnp.where(s == (0 if way == 0 else NS - 1), ba[:, own_x[5 * way + v], :], t))
        sides.append(theirs)
    mine = [jnp.concatenate([ba[:, own_x[v], :], ba[:, own_x[5 + v], :]], axis=0) for v in range(5)]
    theirs = [jnp.concatenate([sides[0][v], sides[1][v]], axis=0) for v in range(5)]
    low = iota((32, 128), 0) < 16
    ql = [jnp.where(low, theirs[v], mine[v]) for v in range(5)]
    qr = [jnp.where(low, mine[v], theirs[v]) for v in range(5)]
    fl, al = flux(ql, state(ql), 0)
    fr, ar = flux(qr, state(qr), 0)
    f = rusanov(ql, fl, al, qr, fr, ar)
    fx = [jnp.where(low, -t, t) for t in f]
    for v in range(5):
        for way in range(2):
            dd[:, way, 10 + v, :] = fx[v][16 * way : 16 * way + 16]
    dd[:, 0, 15, :] = jnp.zeros((16, 128), F32)
    dd[:, 1, 15, :] = jnp.zeros((16, 128), F32)

    late = []
    for d in range(1, NP):
        late.append(copy(S_G + d - 1, dd.at[peer[d]], og.at[me], (s, peer[d])))
        late[-1].start()
    own = pltpu.make_async_copy(dd.at[me], og.at[me], ls.at[6])
    own.start()

    src = iota((128, 256), 0)
    dst = iota((128, 256), 1)
    g = src // 32
    i = lax.rem(src, 32) // 2
    zz = 8 * (dst // 128) + 7 - lax.rem(dst, 128) // 16
    yy = lax.rem(dst, 16)
    far = 15 * (g & 1)
    hit = (zz == jnp.where(g < 2, i, far)) & (yy == jnp.where(g < 2, far, i))
    sign = jnp.where((g & 1) == 0, -1.0, 1.0)
    mean_of = jnp.where(hit, sign, 0.0).astype(BF16)
    src = iota((128, 128), 0)
    dst = iota((128, 128), 1)
    g = src // 32
    i = lax.rem(src, 32) // 2
    z_at = 64 * (i // 8) + 7 - lax.rem(i, 8)
    at = jnp.where(g == 0, z_at, jnp.where(g == 1, z_at + 17, jnp.where(g == 2, 96 + i, 32 + i)))
    reflux = ones_where(dst == at)
    low = ((l1 & 63) < 8) | (l1 >= 96)
    coef = jnp.where(low, -0.05, 0.05).astype(F32) * 0.25
    fix = dot3(sums, mean_of) * -0.0125
    refl = dot3(sums, reflux) * coef
    l32 = iota((32, 128), 1)
    yr = [jnp.zeros((32, 128), F32)] * 2
    zr = [jnp.zeros((32, 128), F32)] * 2
    for v in range(5):
        w = refl[32 * v : 32 * v + 32]
        for h in range(2):
            cc[:, h, v, :] = fix[32 * v : 32 * v + 32, 128 * h : 128 * h + 128]
            yr[h] = jnp.where((l32 >= 25 * v) & (l32 < 25 * v + 25), moved(w, 25 * v - 64 * h), yr[h])
            zr[h] = jnp.where(l32 // 16 == 4 - v, moved(w, 16 * (4 - v) - 64 * h - 32), zr[h])
    for h in range(2):
        cc[:, h, 5, :] = moved(yr[h], -32)
        cc[:, h, 6, :] = moved(zr[h], 48)
        cc[:, h, 7, :] = jnp.zeros((32, 128), F32)
    src = iota((128, 128), 0)
    dst = iota((128, 128), 1)
    sums = jnp.concatenate(fx, axis=0)
    for p in range(2):
        m = dot3(sums, ones_where((src // 64 == p) & ((src & 31) // 2 == (dst & 15)))) * -0.0125
        for v in range(5):
            xt[:, p, v, :] = m[32 * v : 32 * v + 32]
        for v in range(5, 8):
            xt[:, p, v, :] = jnp.zeros((32, 128), F32)
    for c in two:
        c.wait()
    mid = provisional(s, me, cb, oz, ocx, grid, prov)
    own_av.wait()
    for c in early:
        c.wait()

    def turn(i, _):
        for p in range(2):
            gy = nbr[4, 2 * i + p]
            for h in range(2):
                k = 10 * p + 5 * h
                t = jnp.concatenate([bb[i, k : k + 5, :], jnp.zeros((3, 128), F32)], axis=0)
                tt[i, p, h] = pltpu.roll(t + cc[NP * p + i, h], (16 * gy + 32) & 127, 1)
        return 0

    lax.fori_loop(0, NP, turn, 0, unroll=2)
    lane = iota((8, 128), 1)
    sub = iota((8, 128), 0)
    block = lane // 16
    ring = (block + sub) & 7
    slope = lane + sub - 7
    def expand_to(j):
        h = lax.rem(j, 2)
        r = j // 2
        far = r - 2 + 2 * h
        acc = [jnp.zeros((8, 128), F32)] * 5
        accy = [jnp.zeros((8, 128), F32)] * 5
        accz = jnp.zeros((8, 128), F32)
        covered = jnp.zeros((8, 128), F32)
        side = [jnp.zeros((8, 128), F32)] * 2
        for gy in range(6):
            a = grid[0, gy + 8 * (r - 1) + GOFF]
            b = grid[0, gy + 8 * far + GOFF]
            a0 = jnp.maximum(a, 0)
            b0 = jnp.maximum(b, 0)
            t = tt[a0 // 2, a0 & 1, h]
            zt = tt[b0 // 2, b0 & 1, h, 6:7, :]
            for way in range(2):
                side[way] = jnp.where((block == gy + 1) & (a >= 0), xt[NP * way + a0 // 2, a0 & 1], side[way])
            covered = jnp.where((block == gy + 1) & (a >= 0), 1.0, covered)
            ina = (ring == gy + 1) & (a >= 0)
            accz = jnp.where((ring == gy + 1) & (b >= 0), zt, accz)
            for v in range(5):
                acc[v] = jnp.where(ina, t[v : v + 1], acc[v])
                off = (slope - 16 * gy - 25 * v) & 127
                accy[v] = jnp.where(((off == 0) | (off == 17)) & (a >= 0), t[5:6], accy[v])
        accz = pltpu.roll(accz, 0, 1, stride=16, stride_axis=0)
        for v in range(5):
            val = pltpu.roll(acc[v], 0, 1, stride=16, stride_axis=0)
            add = moved(pltpu.roll(accy[v], 0, 1, stride=1, stride_axis=0), 8 - 25 * v)
            add = add + jnp.where(sub == 7 * h, accz[v : v + 1], 0.0)
            ee[j, v] = jnp.where(covered > 0, val, add)
        se[j, 0] = side[0]
        se[j, 1] = side[1]

    def expanded(d):
        j = lax.rem(me + d, NP)
        return copy(S_E + d - 1, ee.at[j], oe.at[me], (s, j))

    def sided(d):
        j = lax.rem(me + d, NP)
        return copy(S_S + d - 1, se.at[j], so.at[lax.rem(me, 8)], (s, j))

    def takes(j):
        return (j > 0) & (j < NP - 1)

    def takes_side(j, m):
        return (j > 1) & (j < NP - 2) & (lax.rem(j, 2) == m // 8)

    def expand_send(d, _):
        j = lax.rem(me + d, NP)
        expand_to(j)

        @pl.when(takes(j))
        def _():
            expanded(d).start()

        @pl.when(takes_side(j, me))
        def _():
            sided(d).start()

        return 0

    lax.fori_loop(1, NP, expand_send, 0)
    expand_to(me)
    own_ee = pltpu.make_async_copy(ee.at[me], oe.at[me], ls.at[7])
    own_se = pltpu.make_async_copy(se.at[me], so.at[lax.rem(me, 8)], ls.at[0])

    @pl.when(takes(me))
    def _():
        own_ee.start()

    @pl.when(takes_side(me, me))
    def _():
        own_se.start()

    @pl.when(jnp.logical_not(takes(me)))
    def _():
        oe[...] = jnp.zeros((16, 5, 8, 128), F32)

    @pl.when((me < 2) | (me >= NP - 2))
    def _():
        so[...] = jnp.zeros((8, 2, 8, 128), F32)

    src = iota((128, 1024), 0)
    dst = iota((128, 1024), 1)
    g = src // 32
    i = lax.rem(src, 32)
    at = jnp.where(g == 0, 32 * i, jnp.where(g == 1, 32 * i + 31, jnp.where(g == 2, i, 992 + i)))
    sign = jnp.where((g & 1) == 0, -1.0, 1.0)
    expand = jnp.where(dst == at, sign, 0.0).astype(BF16)
    own.wait()
    for c in late:
        c.wait()
    l5 = iota((5, 128), 1)
    for way in range(2):
        for j in range(8):
            e = og[2 * j, way, 10:15, :]
            o = og[2 * j + 1, way, 10:15, :]
            cut = slice(128 * j, 128 * j + 128)
            xg[:, way, cut] = jnp.where(l5 < 64, e, pltpu.roll(o, 64, 1))
            xg[:, 2 + way, cut] = jnp.where(l5 < 64, pltpu.roll(e, 64, 1), o)
    for p in range(2):
        for v in range(5):
            for xr in range(2):
                bf[pl.ds(xr, 16, 2), :] = og[:, p, 5 * xr + v, :]
            fs[v, p] = fs[v, p] - 0.1 * dot3(bf[...], expand)
            for way, x in ((0, 0), (1, 31)):
                fs[v, p, x : x + 1, :] = fs[v, p, x : x + 1, :] - 0.1 * xg[v, 2 * p + way : 2 * p + way + 1, :]

    @pl.when(takes(me))
    def _():
        own_ee.wait()
        for d in range(1, NP):
            expanded(d).wait_recv()

    @pl.when(takes_side(me, me))
    def _():
        own_se.wait()

    for d in range(1, NP):
        @pl.when(takes(peer[d]))
        def _():
            expanded(d).wait_send()

        @pl.when(takes_side(peer[d], me))
        def _():
            sided(d).wait_send()

        @pl.when(takes_side(me, peer[NP - d]))
        def _():
            sided(d).wait_recv()

    for x in range(16):
        for v in range(5):
            e = oe[x, v]
            if x in (0, 15):
                e = e + so[:, x // 15, v, :]
            prov[v, x] = jnp.where(mid > 0, e, prov[v, x] + e)


def copy_kernel(a, b, a_out, b_out, sems):
    n = a.shape[0]
    copies = []
    for v in range(n):
        copies.append(pltpu.make_async_copy(b.at[v, 0], b_out.at[v, 0], sems.at[n + v]))
        copies.append(pltpu.make_async_copy(b.at[v, 1], b_out.at[v, 1], sems.at[2 * n + v]))
        copies.append(pltpu.make_async_copy(a.at[v], a_out.at[v], sems.at[v]))
    for c in copies:
        c.start()
    for c in copies:
        c.wait()


def vm():
    return pl.BlockSpec(memory_space=pltpu.VMEM)


def hb():
    return pl.BlockSpec(memory_space=pltpu.HBM)


def sds(*shape, dtype=F32):
    return jax.ShapeDtypeStruct(shape, dtype)


def buf(*shape):
    return pltpu.VMEM(shape, F32)


LIMIT = 48 << 20


def pin(x):
    return pltpu.with_memory_space_constraint(x, pltpu.HBM)


def local(coarse, fine, columns, patch_ids):
    fo, co = pl.pallas_call(
        step_kernel,
        out_shape=(sds(5, 2, 32, 1024), sds(5, 16, 8, 128)),
        in_specs=[hb()] * 4,
        out_specs=(vm(), vm()),
        scratch_shapes=[
            pltpu.SMEM((1, 32), I32),
            pltpu.SMEM((2, 32), I32),
            pltpu.SMEM((7, 32), I32),
            pltpu.SMEM((1, 96), I32),
            buf(5, 2, 32, 1024),
            buf(5, 16, 8, 128),
            buf(16, 40, 128),
            buf(2, 16, 8, 128),
            buf(2, 5, 16, 128),
            buf(8, 80, 128),
            buf(32, 128),
            buf(16, 40, 128),
            buf(2, 16, 8, 128),
            buf(32, 8, 128),
            buf(16, 2, 16, 128),
            buf(16, 2, 16, 128),
            buf(2, 5, 16, 128),
            buf(2, 5, 8, 128),
            buf(32, 128),
            buf(5, 4, 1024),
            buf(16, 24, 128),
            buf(16, 24, 128),
            buf(32, 2, 8, 128),
            buf(32, 2, 8, 128),
            buf(16, 2, 2, 8, 128),
            buf(16, 5, 8, 128),
            buf(16, 5, 8, 128),
            buf(16, 2, 8, 128),
            buf(8, 2, 8, 128),
            buf(2, 32, 128),
            buf(5, 32, 1024),
            pltpu.SemaphoreType.DMA((N_SEM,)),
            pltpu.SemaphoreType.DMA((N_SEM,)),
            pltpu.SemaphoreType.DMA((8,)),
        ],
        compiler_params=pltpu.CompilerParams(collective_id=0, has_side_effects=True, vmem_limit_bytes=LIMIT),
        name="step",
    )(pin(fine), pin(coarse), pin(patch_ids), pin(columns.T))
    return pl.pallas_call(
        copy_kernel,
        out_shape=(sds(5, 16, 8, 128), sds(5, 2, 32, 1024)),
        in_specs=[pl.BlockSpec(memory_space=pl.ANY)] * 2,
        out_specs=(hb(), hb()),
        scratch_shapes=[pltpu.SemaphoreType.DMA((15,))],
        compiler_params=pltpu.CompilerParams(vmem_limit_bytes=LIMIT),
        name="copy_out",
    )(co, fo)


def solution(mesh):
    return jax.shard_map(
        local,
        mesh=mesh,
        in_specs=(
            P(None, "slab", "patch", None),
            P(None, ("slab", "patch"), None, None),
            P(),
            P("slab", None),
        ),
        out_specs=(P(None, "slab", "patch", None), P(None, ("slab", "patch"), None, None)),
        check_vma=False,
    )
```

```python
import jax
import jax.numpy as jnp
from jax import lax
from jax.experimental import pallas as pl
from jax.experimental.pallas import tpu as pltpu
from jax.sharding import PartitionSpec as P

F32 = jnp.float32
BF16 = jnp.bfloat16
I32 = jnp.int32
MESH = pl.DeviceIdType.MESH
NS = 8
NP = 16
GOFF = 16


def iota(shape, dim):
    return lax.broadcasted_iota(I32, shape, dim)


def dot3(x, m):
    hi = x.astype(BF16)
    r = x - hi.astype(F32)
    mid = r.astype(BF16)
    lo = (r - mid.astype(F32)).astype(BF16)
    d = lambda a: jnp.dot(a, m, preferred_element_type=F32)
    return d(hi) + (d(mid) + d(lo))


def dot3_left(m, x):
    hi = x.astype(BF16)
    r = x - hi.astype(F32)
    mid = r.astype(BF16)
    lo = (r - mid.astype(F32)).astype(BF16)
    d = lambda a: jnp.dot(m, a, preferred_element_type=F32)
    return d(hi) + (d(mid) + d(lo))


def moved(x, k):
    return pltpu.roll(x, k % 128, 1) if k % 128 else x


def ones_where(c):
    return jnp.where(c, 1.0, 0.0).astype(BF16)


def state(q):
    r = 1.0 / q[0]
    p = 0.4 * (q[4] - 0.5 * ((q[1] * q[1] + q[2] * q[2] + q[3] * q[3]) * r))
    c = jnp.sqrt(1.4 * p * r)
    return r, p, c


def flux(q, s, d):
    r, p, c = s
    u = q[1 + d] * r
    f = [q[1 + d], q[1] * u, q[2] * u, q[3] * u, (q[4] + p) * u]
    f[1 + d] = f[1 + d] + p
    return f, jnp.abs(u) + c


def rusanov(ql, fl, al, qr, fr, ar):
    a = 0.5 * jnp.maximum(al, ar)
    return [0.5 * (fl[v] + fr[v]) - a * (qr[v] - ql[v]) for v in range(5)]


def provisional(s, me, coarse, oz, ocx, grid, prov):
    r = me // 2
    h = lax.rem(me, 2)
    lane = iota((8, 128), 1)
    sub = iota((8, 128), 0)
    blocks = lane // 16

    def cover(row):
        m = jnp.zeros((8, 128), F32)
        for gy in range(6):
            m = jnp.where((blocks == gy + 1) & (grid[0, gy + 8 * (row - 1) + GOFF] >= 0), 1.0, m)
        return m

    mid = cover(r)
    below = jnp.where(h == 0, cover(r - 1), mid)
    above = jnp.where(h == 1, cover(r + 1), mid)
    free = 1.0 - mid
    fup = free * (1.0 - pltpu.roll(mid, 127, 1))
    flo = free * (1.0 - pltpu.roll(mid, 1, 1))
    zlo = free * (1.0 - jnp.where(sub == 0, below, mid))
    zhi = free * (1.0 - jnp.where(sub == 7, above, mid))

    def cells(x):
        q = [coarse[v, x] for v in range(5)]
        st = state(q)
        return q, st, flux(q, st, 0)

    def face(a, b):
        return rusanov(a[0], a[2][0], a[2][1], b[0], b[2][0], b[2][1])

    first = cells(0)
    q = [jnp.where(s == 0, coarse[v, 0], ocx[0, v]) for v in range(5)]
    st = state(q)
    lower = face((q, st, flux(q, st, 0)), first)
    here = first
    for x in range(16):
        if x < 15:
            there = cells(x + 1)
        else:
            q = [jnp.where(s == NS - 1, coarse[v, 15], ocx[1, v]) for v in range(5)]
            st = state(q)
            there = (q, st, flux(q, st, 0))
        upper = face(here, there)
        q, st, _ = here
        change = [(upper[v] - lower[v]) * free for v in range(5)]
        row = slice(x, x + 1)
        zn = [jnp.where(sub == 7, jnp.where(me == NP - 1, q[v], oz[1, v, row, :]), pltpu.roll(q[v], 7, 0)) for v in range(5)]
        zb = [jnp.where(sub == 0, jnp.where(me == 0, q[v], oz[0, v, row, :]), pltpu.roll(q[v], 1, 0)) for v in range(5)]
        f, a = flux(q, st, 2)
        fn, an = flux(zn, state(zn), 2)
        fb, ab = flux(zb, state(zb), 2)
        up = rusanov(q, f, a, zn, fn, an)
        lo = rusanov(zb, fb, ab, q, f, a)
        change = [change[v] + (up[v] * zhi - lo[v] * zlo) for v in range(5)]
        f, a = flux(q, st, 1)
        nxt = lambda t: jnp.where(lane == 127, t, pltpu.roll(t, 127, 1))
        prv = lambda t: jnp.where(lane == 0, t, pltpu.roll(t, 1, 1))
        up = rusanov(q, f, a, [nxt(t) for t in q], [nxt(t) for t in f], nxt(a))
        lo = rusanov([prv(t) for t in q], [prv(t) for t in f], prv(a), q, f, a)
        for v in range(5):
            prov[v, x] = q[v] - 0.05 * (change[v] + (up[v] * fup - lo[v] * flo))
        here = there
        lower = upper
    return mid


N1 = NP - 1
OFFSETS = sorted(
    ((dx, dz) for dx in range(4) for dz in range(4)),
    key=lambda o: (o != (0, 0), -(min(o[0], 4 - o[0]) + min(o[1], 4 - o[1]))),
)
S_X = N1
S_H = S_X + 2 * NP
S_G = S_H + 4
S_A = S_G + N1
S_E = S_A + N1
S_S = S_E + N1
N_SEM = S_S + N1


def step_kernel(
    fine, coarse, ids_in, cols_in, fs, prov,
    ids, cols, nbr, grid, fb, cb, a1, x1, rz, ct, pk, ba, bx, cg, dd, og, oz, ocx,
    bf, xg, av, bb, cc, xt, tt, ee, oe, se, so, big, chg, ss, rs, ls,
):
    s = lax.axis_index("slab")
    me = lax.axis_index("patch")
    half = lax.rem(me, 2)
    up = lax.rem(s + 1, NS)
    down = lax.rem(s + NS - 1, NS)
    x, z = me // 4, lax.rem(me, 4)
    peer = [lax.rem(x + dx, 4) * 4 + lax.rem(z + dz, 4) for dx, dz in OFFSETS]
    source = [lax.rem(x + 4 - dx, 4) * 4 + lax.rem(z + 4 - dz, 4) for dx, dz in OFFSETS]
    loads = [pltpu.make_async_copy(fine.at[v], fb.at[v], ls.at[v]) for v in range(5)]
    loads.append(pltpu.make_async_copy(coarse, cb, ls.at[5]))
    loads.append(pltpu.make_async_copy(ids_in, ids, ls.at[6]))
    loads.append(pltpu.make_async_copy(cols_in, cols, ls.at[7]))
    barrier = pltpu.get_barrier_semaphore()
    for c in loads:
        c.start()
    for d in range(NP):
        if d:
            pl.semaphore_signal(barrier, inc=1, device_id=(s, peer[d]), device_id_type=MESH)
        pl.semaphore_signal(barrier, inc=1, device_id=(up, peer[d]), device_id_type=MESH)
        pl.semaphore_signal(barrier, inc=1, device_id=(down, peer[d]), device_id_type=MESH)

    def copy(k, src, dst, dev):
        return pltpu.make_async_remote_copy(
            src_ref=src, dst_ref=dst, send_sem=ss.at[k], recv_sem=rs.at[k],
            device_id=dev, device_id_type=MESH,
        )

    k = iota((1024, 128), 0)
    c = iota((1024, 128), 1)
    g = c // 32
    i = lax.rem(c, 32)
    want = jnp.where(g == 0, 32 * i + 31, jnp.where(g == 1, 32 * i, jnp.where(g == 2, 992 + i, i)))
    sel = ones_where(k == want)
    for v in range(5):
        loads[v].wait()
        for p in range(2):
            pk[...] = dot3(fb[v, p], sel)
            for xr in range(2):
                a1[:, 16 * p + 5 * xr + v, :] = pk[pl.ds(xr, 16, 2), :]
    loads[6].wait()
    loads[7].wait()
    lane = iota((5, 128), 1)
    tag = jnp.where(iota((3, 128), 1) < 64, ids[0, 2 * me], ids[0, 2 * me + 1]).astype(F32)
    for d, row in ((0, 0), (1, 31)):
        for j in range(8):
            t0 = fb[:, 0, row, 128 * j : 128 * j + 128]
            t1 = fb[:, 1, row, 128 * j : 128 * j + 128]
            for o, t in (
                (0, jnp.where(lane < 64, t0, pltpu.roll(t1, 64, 1))),
                (1, jnp.where(lane < 64, pltpu.roll(t0, 64, 1), t1)),
            ):
                x1[d, 2 * j + o, 0:5, :] = t
                if d == 0:
                    a1[2 * j + o, 32:37, :] = t
                else:
                    a1[2 * j + o, 37:40, :] = t[0:3]
                    a1[2 * j + o, 15:16, :] = t[3:4]
                    a1[2 * j + o, 31:32, :] = t[4:5]
            x1[d, 2 * j, 5:8, :] = tag
            x1[d, 2 * j + 1, 5:8, :] = tag
    loads[5].wait()
    for v in range(5):
        for z in range(8):
            ct[z, 16 * v : 16 * v + 16, :] = cb[v, :, z, :]
    y = iota((128, 128), 0)
    k = iota((128, 128), 1) // 8
    plane = jnp.where(k < 6, 16 * (k + 1) - 1, jnp.where(k < 12, 16 * (k - 4), -1))
    sel = ones_where(y == plane)
    lane8 = lax.rem(iota((80, 128), 1), 8)
    acc = jnp.zeros((80, 128), F32)
    for z in range(8):
        acc = jnp.where(lane8 == z, dot3(ct[z], sel), acc)
    first = ct[0]
    last = ct[7]
    own = jnp.where(half == 0, first, last)
    for v in range(5):
        cut = slice(16 * v, 16 * v + 16)
        a1[:, 10 + v, :] = acc[cut]
        a1[:, 26 + v, :] = own[cut]
        rz[0, v] = first[cut]
        rz[1, v] = last[cut]

    pl.semaphore_wait(barrier, 3 * NP - 1)
    one = []
    two = []
    for d in [*range(1, NP), 0]:
        j = peer[d]
        if d:
            one.append(copy(d - 1, a1.at[j], ba.at[me], (s, j)))
            one[-1].start()
        for c in (
            copy(S_X + 2 * d, x1.at[0, j], bx.at[1, me], (down, j)),
            copy(S_X + 2 * d + 1, x1.at[1, j], bx.at[0, me], (up, j)),
        ):
            c.start()
            one.append(c)
    two = [
        copy(S_H, cb.at[:, 0], ocx.at[1], (down, me)),
        copy(S_H + 1, cb.at[:, 15], ocx.at[0], (up, me)),
        copy(S_H + 2, rz.at[1], oz.at[0], (s, lax.rem(me + 1, NP))),
        copy(S_H + 3, rz.at[0], oz.at[1], (s, lax.rem(me + N1, NP))),
    ]
    for c in two:
        c.start()
    own = pltpu.make_async_copy(a1.at[me], ba.at[me], ls.at[6])
    own.start()

    src = iota((1024, 256), 0)
    dst = iota((1024, 256), 1)
    zz = 8 * (dst // 128) + 7 - lax.rem(dst, 128) // 16
    pair = ones_where((src // 64 == zz) & (lax.rem(src, 32) // 2 == lax.rem(dst, 16)))

    def interior(p):
        def along_x(j, _):
            cut = pl.ds(pl.multiple_of(128 * j, 128), 128)
            q = [fb[v, p, :, cut] for v in range(5)]
            f, a = flux(q, state(q), 0)
            nxt = lambda t: pltpu.roll(t, 31, 0)
            hi = rusanov(q, f, a, [nxt(t) for t in q], [nxt(t) for t in f], nxt(a))
            inner = iota((32, 128), 0) < 31
            for v in range(5):
                t = jnp.where(inner, hi[v], 0.0)
                chg[v, :, cut] = t - pltpu.roll(t, 1, 0)
            return 0

        lax.fori_loop(0, 8, along_x, 0)

        def rows(c, _):
            cut = pl.ds(pl.multiple_of(8 * c, 8), 8)
            q = [fb[v, p, cut, :] for v in range(5)]
            st = state(q)
            l8 = iota((8, 1024), 1)
            change = [chg[v, cut, :] for v in range(5)]
            for way, shift, inner in ((2, 32, l8 < 992), (1, 1, (l8 & 31) < 31)):
                f, a = flux(q, st, way)
                nxt = lambda t: pltpu.roll(t, 1024 - shift, 1)
                hi = rusanov(q, f, a, [nxt(t) for t in q], [nxt(t) for t in f], nxt(a))
                for v in range(5):
                    t = jnp.where(inner, hi[v], 0.0)
                    change[v] = change[v] + (t - pltpu.roll(t, shift, 1))
            for v in range(5):
                fs[v, p, cut, :] = q[v] - 0.1 * change[v]
            return 0

        lax.fori_loop(0, 4, rows, 0)
        for v in range(5):
            m = dot3(fs[v, p], pair)
            for h in range(2):
                big[h, 0:32, :] = m[:, 128 * h : 128 * h + 128]
                av[:, 10 * p + 5 * h + v, :] = 0.125 * (big[h, pl.ds(0, 16, 2), :] + big[h, pl.ds(1, 16, 2), :])
        for k in range(2):
            av[:, 20 + 2 * p + k, :] = jnp.zeros((16, 128), F32)

    interior(0)
    interior(1)
    early = []
    for d in range(1, NP):
        early.append(copy(S_A + d - 1, av.at[peer[d]], bb.at[me], (s, peer[d])))
        early[-1].start()
    own_av = pltpu.make_async_copy(av.at[me], bb.at[me], ls.at[7])
    own_av.start()
    def place(t, _):
        n = ids[0, t]
        gy = cols[0, n]
        gz = cols[1, n]
        nbr[4, t] = gy
        nbr[5, t] = gz
        nbr[6, t] = gy + 8 * gz + GOFF
        return 0

    lax.fori_loop(0, 32, place, 0)
    for i in range(GOFF):
        grid[0, i] = jnp.int32(-1)

    def find(k, _):
        q = jnp.int32(-1)
        for t in range(32):
            q = jnp.where(nbr[6, t] == k, t, q)
        grid[0, k] = q
        return 0

    lax.fori_loop(GOFF, GOFF + 48, find, 0)
    for i in range(GOFF + 48, 96):
        grid[0, i] = jnp.int32(-1)

    src = iota((128, 128), 0)
    dst = iota((128, 128), 1)
    g = dst // 32
    i = lax.rem(dst, 32) // 2
    base = jnp.where(g == 0, 0, jnp.where(g == 1, 48, jnp.where(g == 2, 64, 80)))
    spread = ones_where(src == base + i)
    sub = iota((32, 128), 0)
    l1 = iota((1, 128), 1)
    want = jnp.zeros((32, 128), I32)
    code = jnp.zeros((32, 128), I32)
    codes = jnp.full((1, 128), -99, I32)
    for i in range(NP):
        for p in range(2):
            k = NP * p + i
            want = jnp.where(sub == k, ids[0, 2 * i + p], want)
            code = jnp.where(sub == k, nbr[6, 2 * i + p], code)
            codes = jnp.where(l1 == k, nbr[6, 2 * i + p], codes)
    want = want.astype(F32)
    own.wait()
    for c in one:
        c.wait()

    lane = iota((8, 128), 1)

    def place_coarse(j, _):
        for p in range(2):
            gy = nbr[4, 2 * j + p]
            gz = nbr[5, 2 * j + p]
            a = 2 * (gz + 1)
            r0 = pltpu.roll(ba[a, 8:16, :], (128 - 8 * gy) & 127, 1)
            r1 = pltpu.roll(ba[a + 1, 8:16, :], (136 - 8 * gy) & 127, 1)
            r2 = pltpu.roll(ba[2 * gz + 1, 24:32, :], (176 - 16 * gy) & 127, 1)
            r3 = pltpu.roll(ba[2 * gz + 4, 24:32, :], (192 - 16 * gy) & 127, 1)
            cg[NP * p + j] = jnp.where(lane < 64, jnp.where((lane & 8) == 0, r0, r1), jnp.where(lane < 80, r2, r3))
        return 0

    lax.fori_loop(0, NP, place_coarse, 0, unroll=4)
    cg[...] = dot3(cg[...].reshape(256, 128), spread).reshape(32, 8, 128)
    packs = [
        jnp.concatenate([ba[:, k, :], ba[:, 16 + k, :]], axis=0) for k in range(10)
    ]
    data = jnp.concatenate(packs, axis=1)
    group = iota((32, 128), 1) // 32
    near = []
    absent = jnp.zeros((32, 128), F32)
    for g, step in enumerate((-1, 1, -8, 8)):
        hit = codes == code + step
        near.append(dot3_left(ones_where(hit)[:, 0:32], data))
        some = jnp.sum(jnp.where(hit, 1.0, 0.0), axis=1, keepdims=True)
        absent = jnp.where(group == g, 1.0 - some, absent)
    theirs = []
    mine = []
    low = (group & 1) == 0
    for v in range(5):
        both = []
        for xr in range(2):
            k = 128 * (5 * xr + v)
            n = [t[:, k : k + 128] for t in near]
            n = jnp.where(group == 0, n[0], jnp.where(group == 1, n[1], jnp.where(group == 2, n[2], n[3])))
            both.append(jnp.where(absent > 0.5, cg[:, 2 + v, :], n))
        theirs.append(jnp.concatenate(both, axis=0))
        both = [jnp.where(low, pltpu.roll(packs[5 * xr + v], 96, 1), pltpu.roll(packs[5 * xr + v], 32, 1)) for xr in range(2)]
        mine.append(jnp.concatenate(both, axis=0))
    g1 = iota((64, 128), 1)
    low = ((g1 // 32) & 1) == 0
    isy = g1 < 64

    def face_flux(q):
        r, pr, c = state(q)
        mn = jnp.where(isy, q[2], q[3])
        u = mn * r
        py = jnp.where(isy, pr, 0.0)
        f = [mn, q[1] * u, q[2] * u + py, q[3] * u + (pr - py), (q[4] + pr) * u]
        return f, jnp.abs(u) + c

    ql = [jnp.where(low, theirs[v], mine[v]) for v in range(5)]
    qr = [jnp.where(low, mine[v], theirs[v]) for v in range(5)]
    fl, al = face_flux(ql)
    fr, ar = face_flux(qr)
    f = rusanov(ql, fl, al, qr, fr, ar)
    for v in range(5):
        for p in range(2):
            for xr in range(2):
                a = 32 * xr + 16 * p
                dd[:, p, 5 * xr + v, :] = f[v][a : a + 16]
    sums = jnp.concatenate([f[v][0:32] + f[v][32:64] for v in range(5)], axis=0)
    l16 = iota((16, 128), 1)
    diagonal = l16 == iota((16, 128), 0)
    own_x = [32 + k for k in range(8)] + [15, 31]
    sides = []
    for way in range(2):
        tag = bx[way, :, 5, :]
        data = jnp.concatenate([bx[way, :, v, :] for v in range(5)], axis=1)
        got = []
        for t in range(2):
            tt_ = pltpu.roll(tag, 64, 1) if t else tag
            row = jnp.sum(jnp.where(diagonal, tt_, 0.0), axis=0, keepdims=True)
            got.append(dot3_left(ones_where(want == row)[:, 0:16], data))
        theirs = []
        for v in range(5):
            g0 = got[0][:, 128 * v : 128 * v + 128]
            g1 = got[1][:, 128 * v : 128 * v + 128]
            a = g0[0:16] + pltpu.roll(g1[0:16], 64, 1)
            b = pltpu.roll(g0[16:32], 64, 1) + g1[16:32]
            t = jnp.where(l16 < 64, a, b)
            theirs.append(jnp.where(s == (0 if way == 0 else NS - 1), ba[:, own_x[5 * way + v], :], t))
        sides.append(theirs)
    mine = [jnp.concatenate([ba[:, own_x[v], :], ba[:, own_x[5 + v], :]], axis=0) for v in range(5)]
    theirs = [jnp.concatenate([sides[0][v], sides[1][v]], axis=0) for v in range(5)]
    low = iota((32, 128), 0) < 16
    ql = [jnp.where(low, theirs[v], mine[v]) for v in range(5)]
    qr = [jnp.where(low, mine[v], theirs[v]) for v in range(5)]
    fl, al = flux(ql, state(ql), 0)
    fr, ar = flux(qr, state(qr), 0)
    f = rusanov(ql, fl, al, qr, fr, ar)
    fx = [jnp.where(low, -t, t) for t in f]
    for v in range(5):
        for way in range(2):
            dd[:, way, 10 + v, :] = fx[v][16 * way : 16 * way + 16]
    dd[:, 0, 15, :] = jnp.zeros((16, 128), F32)
    dd[:, 1, 15, :] = jnp.zeros((16, 128), F32)

    late = []
    for d in range(1, NP):
        late.append(copy(S_G + d - 1, dd.at[peer[d]], og.at[me], (s, peer[d])))
        late[-1].start()
    own = pltpu.make_async_copy(dd.at[me], og.at[me], ls.at[6])
    own.start()

    src = iota((128, 256), 0)
    dst = iota((128, 256), 1)
    g = src // 32
    i = lax.rem(src, 32) // 2
    zz = 8 * (dst // 128) + 7 - lax.rem(dst, 128) // 16
    yy = lax.rem(dst, 16)
    far = 15 * (g & 1)
    hit = (zz == jnp.where(g < 2, i, far)) & (yy == jnp.where(g < 2, far, i))
    sign = jnp.where((g & 1) == 0, -1.0, 1.0)
    mean_of = jnp.where(hit, sign, 0.0).astype(BF16)
    src = iota((128, 128), 0)
    dst = iota((128, 128), 1)
    g = src // 32
    i = lax.rem(src, 32) // 2
    z_at = 64 * (i // 8) + 7 - lax.rem(i, 8)
    at = jnp.where(g == 0, z_at, jnp.where(g == 1, z_at + 17, jnp.where(g == 2, 96 + i, 32 + i)))
    reflux = ones_where(dst == at)
    low = ((l1 & 63) < 8) | (l1 >= 96)
    coef = jnp.where(low, -0.05, 0.05).astype(F32) * 0.25
    fix = dot3(sums, mean_of) * -0.0125
    refl = dot3(sums, reflux) * coef
    l32 = iota((32, 128), 1)
    yr = [jnp.zeros((32, 128), F32)] * 2
    zr = [jnp.zeros((32, 128), F32)] * 2
    for v in range(5):
        w = refl[32 * v : 32 * v + 32]
        for h in range(2):
            cc[:, h, v, :] = fix[32 * v : 32 * v + 32, 128 * h : 128 * h + 128]
            yr[h] = jnp.where((l32 >= 25 * v) & (l32 < 25 * v + 25), moved(w, 25 * v - 64 * h), yr[h])
            zr[h] = jnp.where(l32 // 16 == 4 - v, moved(w, 16 * (4 - v) - 64 * h - 32), zr[h])
    for h in range(2):
        cc[:, h, 5, :] = moved(yr[h], -32)
        cc[:, h, 6, :] = moved(zr[h], 48)
        cc[:, h, 7, :] = jnp.zeros((32, 128), F32)
    src = iota((128, 128), 0)
    dst = iota((128, 128), 1)
    sums = jnp.concatenate(fx, axis=0)
    for p in range(2):
        m = dot3(sums, ones_where((src // 64 == p) & ((src & 31) // 2 == (dst & 15)))) * -0.0125
        for v in range(5):
            xt[:, p, v, :] = m[32 * v : 32 * v + 32]
        for v in range(5, 8):
            xt[:, p, v, :] = jnp.zeros((32, 128), F32)
    for c in two:
        c.wait()
    mid = provisional(s, me, cb, oz, ocx, grid, prov)
    own_av.wait()
    for c in early:
        c.wait()

    def turn(i, _):
        for p in range(2):
            gy = nbr[4, 2 * i + p]
            for h in range(2):
                k = 10 * p + 5 * h
                t = jnp.concatenate([bb[i, k : k + 5, :], jnp.zeros((3, 128), F32)], axis=0)
                tt[i, p, h] = pltpu.roll(t + cc[NP * p + i, h], (16 * gy + 32) & 127, 1)
        return 0

    lax.fori_loop(0, NP, turn, 0, unroll=4)
    lane = iota((8, 128), 1)
    sub = iota((8, 128), 0)
    block = lane // 16
    ring = (block + sub) & 7
    slope = lane + sub - 7
    def expand_to(j):
        h = lax.rem(j, 2)
        r = j // 2
        far = r - 2 + 2 * h
        acc = [jnp.zeros((8, 128), F32)] * 5
        accy = [jnp.zeros((8, 128), F32)] * 5
        accz = jnp.zeros((8, 128), F32)
        covered = jnp.zeros((8, 128), F32)
        side = [jnp.zeros((8, 128), F32)] * 2
        for gy in range(6):
            a = grid[0, gy + 8 * (r - 1) + GOFF]
            b = grid[0, gy + 8 * far + GOFF]
            a0 = jnp.maximum(a, 0)
            b0 = jnp.maximum(b, 0)
            t = tt[a0 // 2, a0 & 1, h]
            zt = tt[b0 // 2, b0 & 1, h, 6:7, :]
            for way in range(2):
                side[way] = jnp.where((block == gy + 1) & (a >= 0), xt[NP * way + a0 // 2, a0 & 1], side[way])
            covered = jnp.where((block == gy + 1) & (a >= 0), 1.0, covered)
            ina = (ring == gy + 1) & (a >= 0)
            accz = jnp.where((ring == gy + 1) & (b >= 0), zt, accz)
            for v in range(5):
                acc[v] = jnp.where(ina, t[v : v + 1], acc[v])
                off = (slope - 16 * gy - 25 * v) & 127
                accy[v] = jnp.where(((off == 0) | (off == 17)) & (a >= 0), t[5:6], accy[v])
        accz = pltpu.roll(accz, 0, 1, stride=16, stride_axis=0)
        for v in range(5):
            val = pltpu.roll(acc[v], 0, 1, stride=16, stride_axis=0)
            add = moved(pltpu.roll(accy[v], 0, 1, stride=1, stride_axis=0), 8 - 25 * v)
            add = add + jnp.where(sub == 7 * h, accz[v : v + 1], 0.0)
            ee[j, v] = jnp.where(covered > 0, val, add)
        se[j, 0] = side[0]
        se[j, 1] = side[1]

    def expanded(d):
        return copy(S_E + d - 1, ee.at[peer[d]], oe.at[me], (s, peer[d]))

    def sided(d):
        return copy(S_S + d - 1, se.at[peer[d]], so.at[lax.rem(me, 8)], (s, peer[d]))

    def takes(j):
        return (j > 0) & (j < NP - 1)

    def takes_side(j, m):
        return (j > 1) & (j < NP - 2) & (lax.rem(j, 2) == m // 8)

    order = [*range(1, NP), 0]
    for b in range(0, NP, 4):
        for d in order[b : b + 4]:
            expand_to(peer[d])
        for d in order[b : b + 4]:
            if d == 0:
                continue

            @pl.when(takes(peer[d]))
            def _():
                expanded(d).start()

            @pl.when(takes_side(peer[d], me))
            def _():
                sided(d).start()

    own_ee = pltpu.make_async_copy(ee.at[me], oe.at[me], ls.at[7])
    own_se = pltpu.make_async_copy(se.at[me], so.at[lax.rem(me, 8)], ls.at[0])

    @pl.when(takes(me))
    def _():
        own_ee.start()

    @pl.when(takes_side(me, me))
    def _():
        own_se.start()

    @pl.when(jnp.logical_not(takes(me)))
    def _():
        oe[...] = jnp.zeros((16, 5, 8, 128), F32)

    @pl.when((me < 2) | (me >= NP - 2))
    def _():
        so[...] = jnp.zeros((8, 2, 8, 128), F32)

    src = iota((128, 1024), 0)
    dst = iota((128, 1024), 1)
    g = src // 32
    i = lax.rem(src, 32)
    at = jnp.where(g == 0, 32 * i, jnp.where(g == 1, 32 * i + 31, jnp.where(g == 2, i, 992 + i)))
    sign = jnp.where((g & 1) == 0, -1.0, 1.0)
    expand = jnp.where(dst == at, sign, 0.0).astype(BF16)
    own.wait()
    for c in late:
        c.wait()
    l5 = iota((5, 128), 1)
    for way in range(2):
        for j in range(8):
            e = og[2 * j, way, 10:15, :]
            o = og[2 * j + 1, way, 10:15, :]
            cut = slice(128 * j, 128 * j + 128)
            xg[:, way, cut] = jnp.where(l5 < 64, e, pltpu.roll(o, 64, 1))
            xg[:, 2 + way, cut] = jnp.where(l5 < 64, pltpu.roll(e, 64, 1), o)
    for p in range(2):
        for v in range(5):
            for xr in range(2):
                bf[pl.ds(xr, 16, 2), :] = og[:, p, 5 * xr + v, :]
            fs[v, p] = fs[v, p] - 0.1 * dot3(bf[...], expand)
            for way, x in ((0, 0), (1, 31)):
                fs[v, p, x : x + 1, :] = fs[v, p, x : x + 1, :] - 0.1 * xg[v, 2 * p + way : 2 * p + way + 1, :]

    @pl.when(takes(me))
    def _():
        own_ee.wait()
        for d in range(1, NP):
            expanded(d).wait_recv()

    @pl.when(takes_side(me, me))
    def _():
        own_se.wait()

    for d in range(1, NP):
        @pl.when(takes(peer[d]))
        def _():
            expanded(d).wait_send()

        @pl.when(takes_side(peer[d], me))
        def _():
            sided(d).wait_send()

        @pl.when(takes_side(me, source[d]))
        def _():
            sided(d).wait_recv()

    for x in range(16):
        for v in range(5):
            e = oe[x, v]
            if x in (0, 15):
                e = e + so[:, x // 15, v, :]
            prov[v, x] = jnp.where(mid > 0, e, prov[v, x] + e)


def copy_kernel(a, b, a_out, b_out, sems):
    n = a.shape[0]
    copies = []
    for v in range(n):
        copies.append(pltpu.make_async_copy(b.at[v, 0], b_out.at[v, 0], sems.at[n + v]))
        copies.append(pltpu.make_async_copy(b.at[v, 1], b_out.at[v, 1], sems.at[2 * n + v]))
        copies.append(pltpu.make_async_copy(a.at[v], a_out.at[v], sems.at[v]))
    for c in copies:
        c.start()
    for c in copies:
        c.wait()


def vm():
    return pl.BlockSpec(memory_space=pltpu.VMEM)


def hb():
    return pl.BlockSpec(memory_space=pltpu.HBM)


def sds(*shape, dtype=F32):
    return jax.ShapeDtypeStruct(shape, dtype)


def buf(*shape):
    return pltpu.VMEM(shape, F32)


LIMIT = 48 << 20


def pin(x):
    return pltpu.with_memory_space_constraint(x, pltpu.HBM)


def local(coarse, fine, columns, patch_ids):
    fo, co = pl.pallas_call(
        step_kernel,
        out_shape=(sds(5, 2, 32, 1024), sds(5, 16, 8, 128)),
        in_specs=[hb()] * 4,
        out_specs=(vm(), vm()),
        scratch_shapes=[
            pltpu.SMEM((1, 32), I32),
            pltpu.SMEM((2, 32), I32),
            pltpu.SMEM((7, 32), I32),
            pltpu.SMEM((1, 96), I32),
            buf(5, 2, 32, 1024),
            buf(5, 16, 8, 128),
            buf(16, 40, 128),
            buf(2, 16, 8, 128),
            buf(2, 5, 16, 128),
            buf(8, 80, 128),
            buf(32, 128),
            buf(16, 40, 128),
            buf(2, 16, 8, 128),
            buf(32, 8, 128),
            buf(16, 2, 16, 128),
            buf(16, 2, 16, 128),
            buf(2, 5, 16, 128),
            buf(2, 5, 8, 128),
            buf(32, 128),
            buf(5, 4, 1024),
            buf(16, 24, 128),
            buf(16, 24, 128),
            buf(32, 2, 8, 128),
            buf(32, 2, 8, 128),
            buf(16, 2, 2, 8, 128),
            buf(16, 5, 8, 128),
            buf(16, 5, 8, 128),
            buf(16, 2, 8, 128),
            buf(8, 2, 8, 128),
            buf(2, 32, 128),
            buf(5, 32, 1024),
            pltpu.SemaphoreType.DMA((N_SEM,)),
            pltpu.SemaphoreType.DMA((N_SEM,)),
            pltpu.SemaphoreType.DMA((8,)),
        ],
        compiler_params=pltpu.CompilerParams(collective_id=0, has_side_effects=True, vmem_limit_bytes=LIMIT),
        name="step",
    )(pin(fine), pin(coarse), pin(patch_ids), pin(columns.T))
    return pl.pallas_call(
        copy_kernel,
        out_shape=(sds(5, 16, 8, 128), sds(5, 2, 32, 1024)),
        in_specs=[pl.BlockSpec(memory_space=pl.ANY)] * 2,
        out_specs=(hb(), hb()),
        scratch_shapes=[pltpu.SemaphoreType.DMA((15,))],
        compiler_params=pltpu.CompilerParams(vmem_limit_bytes=LIMIT),
        name="copy_out",
    )(co, fo)


def solution(mesh):
    return jax.shard_map(
        local,
        mesh=mesh,
        in_specs=(
            P(None, "slab", "patch", None),
            P(None, ("slab", "patch"), None, None),
            P(),
            P("slab", None),
        ),
        out_specs=(P(None, "slab", "patch", None), P(None, ("slab", "patch"), None, None)),
        check_vma=False,
    )
```

```python
import jax
import jax.numpy as jnp
from jax import lax
from jax.experimental import pallas as pl
from jax.experimental.pallas import tpu as pltpu
from jax.sharding import PartitionSpec as P

F32 = jnp.float32
BF16 = jnp.bfloat16
I32 = jnp.int32
MESH = pl.DeviceIdType.MESH
NS = 8
NP = 16
GOFF = 16


def iota(shape, dim):
    return lax.broadcasted_iota(I32, shape, dim)


def dot3(x, m):
    hi = x.astype(BF16)
    r = x - hi.astype(F32)
    mid = r.astype(BF16)
    lo = (r - mid.astype(F32)).astype(BF16)
    n = x.shape[0]
    y = jnp.dot(jnp.concatenate([hi, mid, lo], axis=0), m, preferred_element_type=F32)
    return y[0:n] + (y[n : 2 * n] + y[2 * n : 3 * n])


def dot3_left(m, x):
    hi = x.astype(BF16)
    r = x - hi.astype(F32)
    mid = r.astype(BF16)
    lo = (r - mid.astype(F32)).astype(BF16)
    d = lambda a: jnp.dot(m, a, preferred_element_type=F32)
    return d(hi) + (d(mid) + d(lo))


def moved(x, k):
    return pltpu.roll(x, k % 128, 1) if k % 128 else x


def ones_where(c):
    return jnp.where(c, 1.0, 0.0).astype(BF16)


def state(q):
    r = 1.0 / q[0]
    p = 0.4 * (q[4] - 0.5 * ((q[1] * q[1] + q[2] * q[2] + q[3] * q[3]) * r))
    c = jnp.sqrt(1.4 * p * r)
    return r, p, c


def flux(q, s, d):
    r, p, c = s
    u = q[1 + d] * r
    f = [q[1 + d], q[1] * u, q[2] * u, q[3] * u, (q[4] + p) * u]
    f[1 + d] = f[1 + d] + p
    return f, jnp.abs(u) + c


def rusanov(ql, fl, al, qr, fr, ar):
    a = 0.5 * jnp.maximum(al, ar)
    return [0.5 * (fl[v] + fr[v]) - a * (qr[v] - ql[v]) for v in range(5)]


def provisional(s, me, coarse, oz, ocx, grid, prov):
    r = me // 2
    h = lax.rem(me, 2)
    lane = iota((8, 128), 1)
    sub = iota((8, 128), 0)
    blocks = lane // 16

    def cover(row):
        m = jnp.zeros((8, 128), F32)
        for gy in range(6):
            m = jnp.where((blocks == gy + 1) & (grid[0, gy + 8 * (row - 1) + GOFF] >= 0), 1.0, m)
        return m

    mid = cover(r)
    below = jnp.where(h == 0, cover(r - 1), mid)
    above = jnp.where(h == 1, cover(r + 1), mid)
    free = 1.0 - mid
    fup = free * (1.0 - pltpu.roll(mid, 127, 1))
    flo = free * (1.0 - pltpu.roll(mid, 1, 1))
    zlo = free * (1.0 - jnp.where(sub == 0, below, mid))
    zhi = free * (1.0 - jnp.where(sub == 7, above, mid))

    def cells(x):
        q = [coarse[v, x] for v in range(5)]
        st = state(q)
        return q, st, flux(q, st, 0)

    def face(a, b):
        return rusanov(a[0], a[2][0], a[2][1], b[0], b[2][0], b[2][1])

    first = cells(0)
    q = [jnp.where(s == 0, coarse[v, 0], ocx[0, v]) for v in range(5)]
    st = state(q)
    lower = face((q, st, flux(q, st, 0)), first)
    here = first
    for x in range(16):
        if x < 15:
            there = cells(x + 1)
        else:
            q = [jnp.where(s == NS - 1, coarse[v, 15], ocx[1, v]) for v in range(5)]
            st = state(q)
            there = (q, st, flux(q, st, 0))
        upper = face(here, there)
        q, st, _ = here
        change = [(upper[v] - lower[v]) * free for v in range(5)]
        row = slice(x, x + 1)
        zn = [jnp.where(sub == 7, jnp.where(me == NP - 1, q[v], oz[1, v, row, :]), pltpu.roll(q[v], 7, 0)) for v in range(5)]
        zb = [jnp.where(sub == 0, jnp.where(me == 0, q[v], oz[0, v, row, :]), pltpu.roll(q[v], 1, 0)) for v in range(5)]
        f, a = flux(q, st, 2)
        fn, an = flux(zn, state(zn), 2)
        fb, ab = flux(zb, state(zb), 2)
        up = rusanov(q, f, a, zn, fn, an)
        lo = rusanov(zb, fb, ab, q, f, a)
        change = [change[v] + (up[v] * zhi - lo[v] * zlo) for v in range(5)]
        f, a = flux(q, st, 1)
        nxt = lambda t: jnp.where(lane == 127, t, pltpu.roll(t, 127, 1))
        prv = lambda t: jnp.where(lane == 0, t, pltpu.roll(t, 1, 1))
        up = rusanov(q, f, a, [nxt(t) for t in q], [nxt(t) for t in f], nxt(a))
        lo = rusanov([prv(t) for t in q], [prv(t) for t in f], prv(a), q, f, a)
        for v in range(5):
            prov[v, x] = q[v] - 0.05 * (change[v] + (up[v] * fup - lo[v] * flo))
        here = there
        lower = upper
    return mid


N1 = NP - 1
OFFSETS = sorted(
    ((dx, dz) for dx in range(4) for dz in range(4)),
    key=lambda o: (o != (0, 0), -(min(o[0], 4 - o[0]) + min(o[1], 4 - o[1]))),
)
S_X = N1
S_H = S_X + 2 * NP
S_G = S_H + 4
S_A = S_G + N1
S_E = S_A + N1
S_S = S_E + N1
N_SEM = S_S + N1


def step_kernel(
    fine, coarse, ids_in, cols_in, fs, prov,
    ids, cols, nbr, grid, fb, cb, a1, x1, rz, ct, pk, ba, bx, cg, dd, og, oz, ocx,
    bf, xg, av, bb, cc, xt, tt, ee, oe, se, so, big, chg, ss, rs, ls,
):
    s = lax.axis_index("slab")
    me = lax.axis_index("patch")
    half = lax.rem(me, 2)
    up = lax.rem(s + 1, NS)
    down = lax.rem(s + NS - 1, NS)
    x, z = me // 4, lax.rem(me, 4)
    peer = [lax.rem(x + dx, 4) * 4 + lax.rem(z + dz, 4) for dx, dz in OFFSETS]
    source = [lax.rem(x + 4 - dx, 4) * 4 + lax.rem(z + 4 - dz, 4) for dx, dz in OFFSETS]
    loads = [pltpu.make_async_copy(fine.at[v], fb.at[v], ls.at[v]) for v in range(5)]
    loads.append(pltpu.make_async_copy(coarse, cb, ls.at[5]))
    loads.append(pltpu.make_async_copy(ids_in, ids, ls.at[6]))
    loads.append(pltpu.make_async_copy(cols_in, cols, ls.at[7]))
    barrier = pltpu.get_barrier_semaphore()
    for c in loads:
        c.start()
    for d in range(NP):
        if d:
            pl.semaphore_signal(barrier, inc=1, device_id=(s, peer[d]), device_id_type=MESH)
        pl.semaphore_signal(barrier, inc=1, device_id=(up, peer[d]), device_id_type=MESH)
        pl.semaphore_signal(barrier, inc=1, device_id=(down, peer[d]), device_id_type=MESH)

    def copy(k, src, dst, dev):
        return pltpu.make_async_remote_copy(
            src_ref=src, dst_ref=dst, send_sem=ss.at[k], recv_sem=rs.at[k],
            device_id=dev, device_id_type=MESH,
        )

    k = iota((1024, 128), 0)
    c = iota((1024, 128), 1)
    g = c // 32
    i = lax.rem(c, 32)
    want = jnp.where(g == 0, 32 * i + 31, jnp.where(g == 1, 32 * i, jnp.where(g == 2, 992 + i, i)))
    sel = ones_where(k == want)
    for v in range(5):
        loads[v].wait()
    pk[...] = dot3(fb[...].reshape(320, 1024), sel)
    for v in range(5):
        for p in range(2):
            for xr in range(2):
                a1[:, 16 * p + 5 * xr + v, :] = pk[pl.ds(64 * v + 32 * p + xr, 16, 2), :]
    loads[6].wait()
    loads[7].wait()
    lane = iota((5, 128), 1)
    tag = jnp.where(iota((3, 128), 1) < 64, ids[0, 2 * me], ids[0, 2 * me + 1]).astype(F32)
    for d, row in ((0, 0), (1, 31)):
        for j in range(8):
            t0 = fb[:, 0, row, 128 * j : 128 * j + 128]
            t1 = fb[:, 1, row, 128 * j : 128 * j + 128]
            for o, t in (
                (0, jnp.where(lane < 64, t0, pltpu.roll(t1, 64, 1))),
                (1, jnp.where(lane < 64, pltpu.roll(t0, 64, 1), t1)),
            ):
                x1[d, 2 * j + o, 0:5, :] = t
                if d == 0:
                    a1[2 * j + o, 32:37, :] = t
                else:
                    a1[2 * j + o, 37:40, :] = t[0:3]
                    a1[2 * j + o, 15:16, :] = t[3:4]
                    a1[2 * j + o, 31:32, :] = t[4:5]
            x1[d, 2 * j, 5:8, :] = tag
            x1[d, 2 * j + 1, 5:8, :] = tag
    loads[5].wait()
    for v in range(5):
        for z in range(8):
            ct[z, 16 * v : 16 * v + 16, :] = cb[v, :, z, :]
    y = iota((128, 128), 0)
    k = iota((128, 128), 1) // 8
    plane = jnp.where(k < 6, 16 * (k + 1) - 1, jnp.where(k < 12, 16 * (k - 4), -1))
    sel = ones_where(y == plane)
    lane8 = lax.rem(iota((80, 128), 1), 8)
    acc = jnp.zeros((80, 128), F32)
    planes = dot3(ct[...].reshape(640, 128), sel)
    for z in range(8):
        acc = jnp.where(lane8 == z, planes[80 * z : 80 * z + 80], acc)
    first = ct[0]
    last = ct[7]
    own = jnp.where(half == 0, first, last)
    for v in range(5):
        cut = slice(16 * v, 16 * v + 16)
        a1[:, 10 + v, :] = acc[cut]
        a1[:, 26 + v, :] = own[cut]
        rz[0, v] = first[cut]
        rz[1, v] = last[cut]

    pl.semaphore_wait(barrier, 3 * NP - 1)
    one = []
    two = []
    for d in [*range(1, NP), 0]:
        j = peer[d]
        if d:
            one.append(copy(d - 1, a1.at[j], ba.at[me], (s, j)))
            one[-1].start()
        for c in (
            copy(S_X + 2 * d, x1.at[0, j], bx.at[1, me], (down, j)),
            copy(S_X + 2 * d + 1, x1.at[1, j], bx.at[0, me], (up, j)),
        ):
            c.start()
            one.append(c)
    two = [
        copy(S_H, cb.at[:, 0], ocx.at[1], (down, me)),
        copy(S_H + 1, cb.at[:, 15], ocx.at[0], (up, me)),
        copy(S_H + 2, rz.at[1], oz.at[0], (s, lax.rem(me + 1, NP))),
        copy(S_H + 3, rz.at[0], oz.at[1], (s, lax.rem(me + N1, NP))),
    ]
    for c in two:
        c.start()
    own = pltpu.make_async_copy(a1.at[me], ba.at[me], ls.at[6])
    own.start()

    src = iota((1024, 256), 0)
    dst = iota((1024, 256), 1)
    zz = 8 * (dst // 128) + 7 - lax.rem(dst, 128) // 16
    pair = ones_where((src // 64 == zz) & (lax.rem(src, 32) // 2 == lax.rem(dst, 16)))

    def interior(p):
        def along_x(j, _):
            cut = pl.ds(pl.multiple_of(128 * j, 128), 128)
            q = [fb[v, p, :, cut] for v in range(5)]
            f, a = flux(q, state(q), 0)
            nxt = lambda t: pltpu.roll(t, 31, 0)
            hi = rusanov(q, f, a, [nxt(t) for t in q], [nxt(t) for t in f], nxt(a))
            inner = iota((32, 128), 0) < 31
            for v in range(5):
                t = jnp.where(inner, hi[v], 0.0)
                chg[v, :, cut] = t - pltpu.roll(t, 1, 0)
            return 0

        lax.fori_loop(0, 8, along_x, 0)

        def rows(c, _):
            cut = pl.ds(pl.multiple_of(8 * c, 8), 8)
            q = [fb[v, p, cut, :] for v in range(5)]
            st = state(q)
            l8 = iota((8, 1024), 1)
            change = [chg[v, cut, :] for v in range(5)]
            for way, shift, inner in ((2, 32, l8 < 992), (1, 1, (l8 & 31) < 31)):
                f, a = flux(q, st, way)
                nxt = lambda t: pltpu.roll(t, 1024 - shift, 1)
                hi = rusanov(q, f, a, [nxt(t) for t in q], [nxt(t) for t in f], nxt(a))
                for v in range(5):
                    t = jnp.where(inner, hi[v], 0.0)
                    change[v] = change[v] + (t - pltpu.roll(t, shift, 1))
            for v in range(5):
                fs[v, p, cut, :] = q[v] - 0.1 * change[v]
            return 0

        lax.fori_loop(0, 4, rows, 0)
        m = dot3(fs[:, p].reshape(160, 1024), pair)
        for h in range(2):
            big[h] = m[:, 128 * h : 128 * h + 128]
            for v in range(5):
                a = 32 * v
                av[:, 10 * p + 5 * h + v, :] = 0.125 * (big[h, pl.ds(a, 16, 2), :] + big[h, pl.ds(a + 1, 16, 2), :])
        for k in range(2):
            av[:, 20 + 2 * p + k, :] = jnp.zeros((16, 128), F32)

    interior(0)
    interior(1)
    early = []
    for d in range(1, NP):
        early.append(copy(S_A + d - 1, av.at[peer[d]], bb.at[me], (s, peer[d])))
        early[-1].start()
    own_av = pltpu.make_async_copy(av.at[me], bb.at[me], ls.at[7])
    own_av.start()
    def place(t, _):
        n = ids[0, t]
        gy = cols[0, n]
        gz = cols[1, n]
        nbr[4, t] = gy
        nbr[5, t] = gz
        nbr[6, t] = gy + 8 * gz + GOFF
        return 0

    lax.fori_loop(0, 32, place, 0)
    for i in range(GOFF):
        grid[0, i] = jnp.int32(-1)

    def find(k, _):
        q = jnp.int32(-1)
        for t in range(32):
            q = jnp.where(nbr[6, t] == k, t, q)
        grid[0, k] = q
        return 0

    lax.fori_loop(GOFF, GOFF + 48, find, 0)
    for i in range(GOFF + 48, 96):
        grid[0, i] = jnp.int32(-1)

    src = iota((128, 128), 0)
    dst = iota((128, 128), 1)
    g = dst // 32
    i = lax.rem(dst, 32) // 2
    base = jnp.where(g == 0, 0, jnp.where(g == 1, 48, jnp.where(g == 2, 64, 80)))
    spread = ones_where(src == base + i)
    sub = iota((32, 128), 0)
    l1 = iota((1, 128), 1)
    want = jnp.zeros((32, 128), I32)
    code = jnp.zeros((32, 128), I32)
    codes = jnp.full((1, 128), -99, I32)
    for i in range(NP):
        for p in range(2):
            k = NP * p + i
            want = jnp.where(sub == k, ids[0, 2 * i + p], want)
            code = jnp.where(sub == k, nbr[6, 2 * i + p], code)
            codes = jnp.where(l1 == k, nbr[6, 2 * i + p], codes)
    want = want.astype(F32)
    own.wait()
    for c in one:
        c.wait()

    lane = iota((8, 128), 1)

    def place_coarse(j, _):
        for p in range(2):
            gy = nbr[4, 2 * j + p]
            gz = nbr[5, 2 * j + p]
            a = 2 * (gz + 1)
            r0 = pltpu.roll(ba[a, 8:16, :], (128 - 8 * gy) & 127, 1)
            r1 = pltpu.roll(ba[a + 1, 8:16, :], (136 - 8 * gy) & 127, 1)
            r2 = pltpu.roll(ba[2 * gz + 1, 24:32, :], (176 - 16 * gy) & 127, 1)
            r3 = pltpu.roll(ba[2 * gz + 4, 24:32, :], (192 - 16 * gy) & 127, 1)
            cg[NP * p + j] = jnp.where(lane < 64, jnp.where((lane & 8) == 0, r0, r1), jnp.where(lane < 80, r2, r3))
        return 0

    lax.fori_loop(0, NP, place_coarse, 0, unroll=4)
    cg[...] = dot3(cg[...].reshape(256, 128), spread).reshape(32, 8, 128)
    packs = [
        jnp.concatenate([ba[:, k, :], ba[:, 16 + k, :]], axis=0) for k in range(10)
    ]
    data = jnp.concatenate(packs, axis=1)
    group = iota((32, 128), 1) // 32
    near = []
    absent = jnp.zeros((32, 128), F32)
    for g, step in enumerate((-1, 1, -8, 8)):
        hit = codes == code + step
        near.append(ones_where(hit)[:, 0:32])
        some = jnp.sum(jnp.where(hit, 1.0, 0.0), axis=1, keepdims=True)
        absent = jnp.where(group == g, 1.0 - some, absent)
    near = dot3_left(jnp.concatenate(near, axis=0), data)
    theirs = []
    mine = []
    low = (group & 1) == 0
    for v in range(5):
        both = []
        for xr in range(2):
            k = 128 * (5 * xr + v)
            n = [near[32 * g : 32 * g + 32, k : k + 128] for g in range(4)]
            n = jnp.where(group == 0, n[0], jnp.where(group == 1, n[1], jnp.where(group == 2, n[2], n[3])))
            both.append(jnp.where(absent > 0.5, cg[:, 2 + v, :], n))
        theirs.append(jnp.concatenate(both, axis=0))
        both = [jnp.where(low, pltpu.roll(packs[5 * xr + v], 96, 1), pltpu.roll(packs[5 * xr + v], 32, 1)) for xr in range(2)]
        mine.append(jnp.concatenate(both, axis=0))
    g1 = iota((64, 128), 1)
    low = ((g1 // 32) & 1) == 0
    isy = g1 < 64

    def face_flux(q):
        r, pr, c = state(q)
        mn = jnp.where(isy, q[2], q[3])
        u = mn * r
        py = jnp.where(isy, pr, 0.0)
        f = [mn, q[1] * u, q[2] * u + py, q[3] * u + (pr - py), (q[4] + pr) * u]
        return f, jnp.abs(u) + c

    ql = [jnp.where(low, theirs[v], mine[v]) for v in range(5)]
    qr = [jnp.where(low, mine[v], theirs[v]) for v in range(5)]
    fl, al = face_flux(ql)
    fr, ar = face_flux(qr)
    f = rusanov(ql, fl, al, qr, fr, ar)
    for v in range(5):
        for p in range(2):
            for xr in range(2):
                a = 32 * xr + 16 * p
                dd[:, p, 5 * xr + v, :] = f[v][a : a + 16]
    sums = jnp.concatenate([f[v][0:32] + f[v][32:64] for v in range(5)], axis=0)
    l16 = iota((16, 128), 1)
    diagonal = l16 == iota((16, 128), 0)
    own_x = [32 + k for k in range(8)] + [15, 31]
    sides = []
    for way in range(2):
        tag = bx[way, :, 5, :]
        data = jnp.concatenate([bx[way, :, v, :] for v in range(5)], axis=1)
        got = []
        for t in range(2):
            tt_ = pltpu.roll(tag, 64, 1) if t else tag
            row = jnp.sum(jnp.where(diagonal, tt_, 0.0), axis=0, keepdims=True)
            got.append(ones_where(want == row)[:, 0:16])
        got = dot3_left(jnp.concatenate(got, axis=0), data)
        theirs = []
        for v in range(5):
            g0 = got[0:32, 128 * v : 128 * v + 128]
            g1 = got[32:64, 128 * v : 128 * v + 128]
            a = g0[0:16] + pltpu.roll(g1[0:16], 64, 1)
            b = pltpu.roll(g0[16:32], 64, 1) + g1[16:32]
            t = jnp.where(l16 < 64, a, b)
            theirs.append(jnp.where(s == (0 if way == 0 else NS - 1), ba[:, own_x[5 * way + v], :], t))
        sides.append(theirs)
    mine = [jnp.concatenate([ba[:, own_x[v], :], ba[:, own_x[5 + v], :]], axis=0) for v in range(5)]
    theirs = [jnp.concatenate([sides[0][v], sides[1][v]], axis=0) for v in range(5)]
    low = iota((32, 128), 0) < 16
    ql = [jnp.where(low, theirs[v], mine[v]) for v in range(5)]
    qr = [jnp.where(low, mine[v], theirs[v]) for v in range(5)]
    fl, al = flux(ql, state(ql), 0)
    fr, ar = flux(qr, state(qr), 0)
    f = rusanov(ql, fl, al, qr, fr, ar)
    fx = [jnp.where(low, -t, t) for t in f]
    for v in range(5):
        for way in range(2):
            dd[:, way, 10 + v, :] = fx[v][16 * way : 16 * way + 16]
    dd[:, 0, 15, :] = jnp.zeros((16, 128), F32)
    dd[:, 1, 15, :] = jnp.zeros((16, 128), F32)

    late = []
    for d in range(1, NP):
        late.append(copy(S_G + d - 1, dd.at[peer[d]], og.at[me], (s, peer[d])))
        late[-1].start()
    own = pltpu.make_async_copy(dd.at[me], og.at[me], ls.at[6])
    own.start()

    src = iota((128, 256), 0)
    dst = iota((128, 256), 1)
    g = src // 32
    i = lax.rem(src, 32) // 2
    zz = 8 * (dst // 128) + 7 - lax.rem(dst, 128) // 16
    yy = lax.rem(dst, 16)
    far = 15 * (g & 1)
    hit = (zz == jnp.where(g < 2, i, far)) & (yy == jnp.where(g < 2, far, i))
    sign = jnp.where((g & 1) == 0, -1.0, 1.0)
    mean_of = jnp.where(hit, sign, 0.0).astype(BF16)
    src = iota((128, 128), 0)
    dst = iota((128, 128), 1)
    g = src // 32
    i = lax.rem(src, 32) // 2
    z_at = 64 * (i // 8) + 7 - lax.rem(i, 8)
    at = jnp.where(g == 0, z_at, jnp.where(g == 1, z_at + 17, jnp.where(g == 2, 96 + i, 32 + i)))
    reflux = ones_where(dst == at)
    low = ((l1 & 63) < 8) | (l1 >= 96)
    coef = jnp.where(low, -0.05, 0.05).astype(F32) * 0.25
    fix = dot3(sums, mean_of) * -0.0125
    refl = dot3(sums, reflux) * coef
    l32 = iota((32, 128), 1)
    yr = [jnp.zeros((32, 128), F32)] * 2
    zr = [jnp.zeros((32, 128), F32)] * 2
    for v in range(5):
        w = refl[32 * v : 32 * v + 32]
        for h in range(2):
            cc[:, h, v, :] = fix[32 * v : 32 * v + 32, 128 * h : 128 * h + 128]
            yr[h] = jnp.where((l32 >= 25 * v) & (l32 < 25 * v + 25), moved(w, 25 * v - 64 * h), yr[h])
            zr[h] = jnp.where(l32 // 16 == 4 - v, moved(w, 16 * (4 - v) - 64 * h - 32), zr[h])
    for h in range(2):
        cc[:, h, 5, :] = moved(yr[h], -32)
        cc[:, h, 6, :] = moved(zr[h], 48)
        cc[:, h, 7, :] = jnp.zeros((32, 128), F32)
    src = iota((128, 128), 0)
    dst = iota((128, 128), 1)
    sums = jnp.concatenate(fx, axis=0)
    for p in range(2):
        m = dot3(sums, ones_where((src // 64 == p) & ((src & 31) // 2 == (dst & 15)))) * -0.0125
        for v in range(5):
            xt[:, p, v, :] = m[32 * v : 32 * v + 32]
        for v in range(5, 8):
            xt[:, p, v, :] = jnp.zeros((32, 128), F32)
    for c in two:
        c.wait()
    mid = provisional(s, me, cb, oz, ocx, grid, prov)
    own_av.wait()
    for c in early:
        c.wait()

    def turn(i, _):
        for p in range(2):
            gy = nbr[4, 2 * i + p]
            for h in range(2):
                k = 10 * p + 5 * h
                t = jnp.concatenate([bb[i, k : k + 5, :], jnp.zeros((3, 128), F32)], axis=0)
                tt[i, p, h] = pltpu.roll(t + cc[NP * p + i, h], (16 * gy + 32) & 127, 1)
        return 0

    lax.fori_loop(0, NP, turn, 0, unroll=4)
    lane = iota((8, 128), 1)
    sub = iota((8, 128), 0)
    block = lane // 16
    ring = (block + sub) & 7
    slope = lane + sub - 7
    def expand_to(j):
        h = lax.rem(j, 2)
        r = j // 2
        far = r - 2 + 2 * h
        acc = [jnp.zeros((8, 128), F32)] * 5
        accy = [jnp.zeros((8, 128), F32)] * 5
        accz = jnp.zeros((8, 128), F32)
        covered = jnp.zeros((8, 128), F32)
        side = [jnp.zeros((8, 128), F32)] * 2
        for gy in range(6):
            a = grid[0, gy + 8 * (r - 1) + GOFF]
            b = grid[0, gy + 8 * far + GOFF]
            a0 = jnp.maximum(a, 0)
            b0 = jnp.maximum(b, 0)
            t = tt[a0 // 2, a0 & 1, h]
            zt = tt[b0 // 2, b0 & 1, h, 6:7, :]
            for way in range(2):
                side[way] = jnp.where((block == gy + 1) & (a >= 0), xt[NP * way + a0 // 2, a0 & 1], side[way])
            covered = jnp.where((block == gy + 1) & (a >= 0), 1.0, covered)
            ina = (ring == gy + 1) & (a >= 0)
            accz = jnp.where((ring == gy + 1) & (b >= 0), zt, accz)
            for v in range(5):
                acc[v] = jnp.where(ina, t[v : v + 1], acc[v])
                off = (slope - 16 * gy - 25 * v) & 127
                accy[v] = jnp.where(((off == 0) | (off == 17)) & (a >= 0), t[5:6], accy[v])
        accz = pltpu.roll(accz, 0, 1, stride=16, stride_axis=0)
        for v in range(5):
            val = pltpu.roll(acc[v], 0, 1, stride=16, stride_axis=0)
            add = moved(pltpu.roll(accy[v], 0, 1, stride=1, stride_axis=0), 8 - 25 * v)
            add = add + jnp.where(sub == 7 * h, accz[v : v + 1], 0.0)
            ee[j, v] = jnp.where(covered > 0, val, add)
        se[j, 0] = side[0]
        se[j, 1] = side[1]

    def expanded(d):
        return copy(S_E + d - 1, ee.at[peer[d]], oe.at[me], (s, peer[d]))

    def sided(d):
        return copy(S_S + d - 1, se.at[peer[d]], so.at[lax.rem(me, 8)], (s, peer[d]))

    def takes(j):
        return (j > 0) & (j < NP - 1)

    def takes_side(j, m):
        return (j > 1) & (j < NP - 2) & (lax.rem(j, 2) == m // 8)

    order = [*range(1, NP), 0]
    for b in range(0, NP, 4):
        for d in order[b : b + 4]:
            expand_to(peer[d])
        for d in order[b : b + 4]:
            if d == 0:
                continue

            @pl.when(takes(peer[d]))
            def _():
                expanded(d).start()

            @pl.when(takes_side(peer[d], me))
            def _():
                sided(d).start()

    own_ee = pltpu.make_async_copy(ee.at[me], oe.at[me], ls.at[7])
    own_se = pltpu.make_async_copy(se.at[me], so.at[lax.rem(me, 8)], ls.at[0])

    @pl.when(takes(me))
    def _():
        own_ee.start()

    @pl.when(takes_side(me, me))
    def _():
        own_se.start()

    @pl.when(jnp.logical_not(takes(me)))
    def _():
        oe[...] = jnp.zeros((16, 5, 8, 128), F32)

    @pl.when((me < 2) | (me >= NP - 2))
    def _():
        so[...] = jnp.zeros((8, 2, 8, 128), F32)

    src = iota((128, 1024), 0)
    dst = iota((128, 1024), 1)
    g = src // 32
    i = lax.rem(src, 32)
    at = jnp.where(g == 0, 32 * i, jnp.where(g == 1, 32 * i + 31, jnp.where(g == 2, i, 992 + i)))
    sign = jnp.where((g & 1) == 0, -1.0, 1.0)
    expand = jnp.where(dst == at, sign, 0.0).astype(BF16)
    own.wait()
    for c in late:
        c.wait()
    l5 = iota((5, 128), 1)
    for way in range(2):
        for j in range(8):
            e = og[2 * j, way, 10:15, :]
            o = og[2 * j + 1, way, 10:15, :]
            cut = slice(128 * j, 128 * j + 128)
            xg[:, way, cut] = jnp.where(l5 < 64, e, pltpu.roll(o, 64, 1))
            xg[:, 2 + way, cut] = jnp.where(l5 < 64, pltpu.roll(e, 64, 1), o)
    for p in range(2):
        for v in range(5):
            for xr in range(2):
                bf[pl.ds(32 * v + xr, 16, 2), :] = og[:, p, 5 * xr + v, :]
        m = dot3(bf[...], expand)
        for v in range(5):
            fs[v, p] = fs[v, p] - 0.1 * m[32 * v : 32 * v + 32]
            for way, x in ((0, 0), (1, 31)):
                fs[v, p, x : x + 1, :] = fs[v, p, x : x + 1, :] - 0.1 * xg[v, 2 * p + way : 2 * p + way + 1, :]

    @pl.when(takes(me))
    def _():
        own_ee.wait()
        for d in range(1, NP):
            expanded(d).wait_recv()

    @pl.when(takes_side(me, me))
    def _():
        own_se.wait()

    for d in range(1, NP):
        @pl.when(takes(peer[d]))
        def _():
            expanded(d).wait_send()

        @pl.when(takes_side(peer[d], me))
        def _():
            sided(d).wait_send()

        @pl.when(takes_side(me, source[d]))
        def _():
            sided(d).wait_recv()

    for x in range(16):
        for v in range(5):
            e = oe[x, v]
            if x in (0, 15):
                e = e + so[:, x // 15, v, :]
            prov[v, x] = jnp.where(mid > 0, e, prov[v, x] + e)


def copy_kernel(a, b, a_out, b_out, sems):
    n = a.shape[0]
    copies = []
    for v in range(n):
        copies.append(pltpu.make_async_copy(b.at[v, 0], b_out.at[v, 0], sems.at[n + v]))
        copies.append(pltpu.make_async_copy(b.at[v, 1], b_out.at[v, 1], sems.at[2 * n + v]))
        copies.append(pltpu.make_async_copy(a.at[v], a_out.at[v], sems.at[v]))
    for c in copies:
        c.start()
    for c in copies:
        c.wait()


def vm():
    return pl.BlockSpec(memory_space=pltpu.VMEM)


def hb():
    return pl.BlockSpec(memory_space=pltpu.HBM)


def sds(*shape, dtype=F32):
    return jax.ShapeDtypeStruct(shape, dtype)


def buf(*shape):
    return pltpu.VMEM(shape, F32)


LIMIT = 48 << 20


def pin(x):
    return pltpu.with_memory_space_constraint(x, pltpu.HBM)


def local(coarse, fine, columns, patch_ids):
    fo, co = pl.pallas_call(
        step_kernel,
        out_shape=(sds(5, 2, 32, 1024), sds(5, 16, 8, 128)),
        in_specs=[hb()] * 4,
        out_specs=(vm(), vm()),
        scratch_shapes=[
            pltpu.SMEM((1, 32), I32),
            pltpu.SMEM((2, 32), I32),
            pltpu.SMEM((7, 32), I32),
            pltpu.SMEM((1, 96), I32),
            buf(5, 2, 32, 1024),
            buf(5, 16, 8, 128),
            buf(16, 40, 128),
            buf(2, 16, 8, 128),
            buf(2, 5, 16, 128),
            buf(8, 80, 128),
            buf(320, 128),
            buf(16, 40, 128),
            buf(2, 16, 8, 128),
            buf(32, 8, 128),
            buf(16, 2, 16, 128),
            buf(16, 2, 16, 128),
            buf(2, 5, 16, 128),
            buf(2, 5, 8, 128),
            buf(160, 128),
            buf(5, 4, 1024),
            buf(16, 24, 128),
            buf(16, 24, 128),
            buf(32, 2, 8, 128),
            buf(32, 2, 8, 128),
            buf(16, 2, 2, 8, 128),
            buf(16, 5, 8, 128),
            buf(16, 5, 8, 128),
            buf(16, 2, 8, 128),
            buf(8, 2, 8, 128),
            buf(2, 160, 128),
            buf(5, 32, 1024),
            pltpu.SemaphoreType.DMA((N_SEM,)),
            pltpu.SemaphoreType.DMA((N_SEM,)),
            pltpu.SemaphoreType.DMA((8,)),
        ],
        compiler_params=pltpu.CompilerParams(collective_id=0, has_side_effects=True, vmem_limit_bytes=LIMIT),
        name="step",
    )(pin(fine), pin(coarse), pin(patch_ids), pin(columns.T))
    return pl.pallas_call(
        copy_kernel,
        out_shape=(sds(5, 16, 8, 128), sds(5, 2, 32, 1024)),
        in_specs=[pl.BlockSpec(memory_space=pl.ANY)] * 2,
        out_specs=(hb(), hb()),
        scratch_shapes=[pltpu.SemaphoreType.DMA((15,))],
        compiler_params=pltpu.CompilerParams(vmem_limit_bytes=LIMIT),
        name="copy_out",
    )(co, fo)


def solution(mesh):
    return jax.shard_map(
        local,
        mesh=mesh,
        in_specs=(
            P(None, "slab", "patch", None),
            P(None, ("slab", "patch"), None, None),
            P(),
            P("slab", None),
        ),
        out_specs=(P(None, "slab", "patch", None), P(None, ("slab", "patch"), None, None)),
        check_vma=False,
    )
```

```python
import jax
import jax.numpy as jnp
from jax import lax
from jax.experimental import pallas as pl
from jax.experimental.pallas import tpu as pltpu
from jax.sharding import PartitionSpec as P

F32 = jnp.float32
BF16 = jnp.bfloat16
I32 = jnp.int32
MESH = pl.DeviceIdType.MESH
NS = 8
NP = 16
GOFF = 16


def iota(shape, dim):
    return lax.broadcasted_iota(I32, shape, dim)


def dot3(x, m):
    hi = x.astype(BF16)
    r = x - hi.astype(F32)
    mid = r.astype(BF16)
    lo = (r - mid.astype(F32)).astype(BF16)
    n = x.shape[0]
    y = jnp.dot(jnp.concatenate([hi, mid, lo], axis=0), m, preferred_element_type=F32)
    return y[0:n] + (y[n : 2 * n] + y[2 * n : 3 * n])


def dot3_left(m, x):
    hi = x.astype(BF16)
    r = x - hi.astype(F32)
    mid = r.astype(BF16)
    lo = (r - mid.astype(F32)).astype(BF16)
    d = lambda a: jnp.dot(m, a, preferred_element_type=F32)
    return d(hi) + (d(mid) + d(lo))


def moved(x, k):
    return pltpu.roll(x, k % 128, 1) if k % 128 else x


def ones_where(c):
    return jnp.where(c, 1.0, 0.0).astype(BF16)


def state(q):
    r = 1.0 / q[0]
    p = 0.4 * (q[4] - 0.5 * ((q[1] * q[1] + q[2] * q[2] + q[3] * q[3]) * r))
    c = jnp.sqrt(1.4 * p * r)
    return r, p, c


def flux(q, s, d):
    r, p, c = s
    u = q[1 + d] * r
    f = [q[1 + d], q[1] * u, q[2] * u, q[3] * u, (q[4] + p) * u]
    f[1 + d] = f[1 + d] + p
    return f, jnp.abs(u) + c


def rusanov(ql, fl, al, qr, fr, ar):
    a = 0.5 * jnp.maximum(al, ar)
    return [0.5 * (fl[v] + fr[v]) - a * (qr[v] - ql[v]) for v in range(5)]


def provisional(s, me, coarse, oz, ocx, grid, prov):
    r = me // 2
    h = lax.rem(me, 2)
    lane = iota((8, 128), 1)
    sub = iota((8, 128), 0)
    blocks = lane // 16

    def cover(row):
        m = jnp.zeros((8, 128), F32)
        for gy in range(6):
            m = jnp.where((blocks == gy + 1) & (grid[0, gy + 8 * (row - 1) + GOFF] >= 0), 1.0, m)
        return m

    mid = cover(r)
    below = jnp.where(h == 0, cover(r - 1), mid)
    above = jnp.where(h == 1, cover(r + 1), mid)
    free = 1.0 - mid
    fup = free * (1.0 - pltpu.roll(mid, 127, 1))
    flo = free * (1.0 - pltpu.roll(mid, 1, 1))
    zlo = free * (1.0 - jnp.where(sub == 0, below, mid))
    zhi = free * (1.0 - jnp.where(sub == 7, above, mid))

    def cells(x):
        q = [coarse[v, x] for v in range(5)]
        st = state(q)
        return q, st, flux(q, st, 0)

    def face(a, b):
        return rusanov(a[0], a[2][0], a[2][1], b[0], b[2][0], b[2][1])

    first = cells(0)
    q = [jnp.where(s == 0, coarse[v, 0], ocx[0, v]) for v in range(5)]
    st = state(q)
    lower = face((q, st, flux(q, st, 0)), first)
    here = first
    for x in range(16):
        if x < 15:
            there = cells(x + 1)
        else:
            q = [jnp.where(s == NS - 1, coarse[v, 15], ocx[1, v]) for v in range(5)]
            st = state(q)
            there = (q, st, flux(q, st, 0))
        upper = face(here, there)
        q, st, _ = here
        change = [(upper[v] - lower[v]) * free for v in range(5)]
        row = slice(x, x + 1)
        zn = [jnp.where(sub == 7, jnp.where(me == NP - 1, q[v], oz[1, v, row, :]), pltpu.roll(q[v], 7, 0)) for v in range(5)]
        zb = [jnp.where(sub == 0, jnp.where(me == 0, q[v], oz[0, v, row, :]), pltpu.roll(q[v], 1, 0)) for v in range(5)]
        f, a = flux(q, st, 2)
        fn, an = flux(zn, state(zn), 2)
        fb, ab = flux(zb, state(zb), 2)
        up = rusanov(q, f, a, zn, fn, an)
        lo = rusanov(zb, fb, ab, q, f, a)
        change = [change[v] + (up[v] * zhi - lo[v] * zlo) for v in range(5)]
        f, a = flux(q, st, 1)
        nxt = lambda t: jnp.where(lane == 127, t, pltpu.roll(t, 127, 1))
        prv = lambda t: jnp.where(lane == 0, t, pltpu.roll(t, 1, 1))
        up = rusanov(q, f, a, [nxt(t) for t in q], [nxt(t) for t in f], nxt(a))
        lo = rusanov([prv(t) for t in q], [prv(t) for t in f], prv(a), q, f, a)
        for v in range(5):
            prov[v, x] = q[v] - 0.05 * (change[v] + (up[v] * fup - lo[v] * flo))
        here = there
        lower = upper
    return mid


N1 = NP - 1
OFFSETS = sorted(
    ((dx, dz) for dx in range(4) for dz in range(4)),
    key=lambda o: (o != (0, 0), -(min(o[0], 4 - o[0]) + min(o[1], 4 - o[1]))),
)
S_X = N1
S_H = S_X + 2 * NP
S_G = S_H + 4
S_A = S_G + N1
S_E = S_A + N1
S_S = S_E + N1
N_SEM = S_S + N1


def step_kernel(
    fine, coarse, ids_in, cols_in, fs, prov,
    ids, cols, nbr, grid, fb, cb, a1, x1, rz, ct, pk, ba, bx, cg, dd, og, oz, ocx,
    bf, xg, av, bb, cc, xt, tt, ee, oe, se, so, big, chg, ss, rs, ls,
):
    s = lax.axis_index("slab")
    me = lax.axis_index("patch")
    half = lax.rem(me, 2)
    up = lax.rem(s + 1, NS)
    down = lax.rem(s + NS - 1, NS)
    x, z = me // 4, lax.rem(me, 4)
    peer = [lax.rem(x + dx, 4) * 4 + lax.rem(z + dz, 4) for dx, dz in OFFSETS]
    source = [lax.rem(x + 4 - dx, 4) * 4 + lax.rem(z + 4 - dz, 4) for dx, dz in OFFSETS]
    loads = [pltpu.make_async_copy(fine.at[v], fb.at[v], ls.at[v]) for v in range(5)]
    loads.append(pltpu.make_async_copy(coarse, cb, ls.at[5]))
    loads.append(pltpu.make_async_copy(ids_in, ids, ls.at[6]))
    loads.append(pltpu.make_async_copy(cols_in, cols, ls.at[7]))
    barrier = pltpu.get_barrier_semaphore()
    for c in loads:
        c.start()
    for d in range(NP):
        if d:
            pl.semaphore_signal(barrier, inc=1, device_id=(s, peer[d]), device_id_type=MESH)
        pl.semaphore_signal(barrier, inc=1, device_id=(up, peer[d]), device_id_type=MESH)
        pl.semaphore_signal(barrier, inc=1, device_id=(down, peer[d]), device_id_type=MESH)

    def copy(k, src, dst, dev):
        return pltpu.make_async_remote_copy(
            src_ref=src, dst_ref=dst, send_sem=ss.at[k], recv_sem=rs.at[k],
            device_id=dev, device_id_type=MESH,
        )

    k = iota((1024, 128), 0)
    c = iota((1024, 128), 1)
    g = c // 32
    i = lax.rem(c, 32)
    want = jnp.where(g == 0, 32 * i + 31, jnp.where(g == 1, 32 * i, jnp.where(g == 2, 992 + i, i)))
    sel = ones_where(k == want)
    for v in range(5):
        loads[v].wait()
    pk[...] = dot3(fb[...].reshape(320, 1024), sel)
    for v in range(5):
        for p in range(2):
            for xr in range(2):
                a1[:, 16 * p + 5 * xr + v, :] = pk[pl.ds(64 * v + 32 * p + xr, 16, 2), :]
    loads[6].wait()
    loads[7].wait()
    lane = iota((5, 128), 1)
    tag = jnp.where(iota((3, 128), 1) < 64, ids[0, 2 * me], ids[0, 2 * me + 1]).astype(F32)
    for d, row in ((0, 0), (1, 31)):
        for j in range(8):
            t0 = fb[:, 0, row, 128 * j : 128 * j + 128]
            t1 = fb[:, 1, row, 128 * j : 128 * j + 128]
            for o, t in (
                (0, jnp.where(lane < 64, t0, pltpu.roll(t1, 64, 1))),
                (1, jnp.where(lane < 64, pltpu.roll(t0, 64, 1), t1)),
            ):
                x1[d, 2 * j + o, 0:5, :] = t
                if d == 0:
                    a1[2 * j + o, 32:37, :] = t
                else:
                    a1[2 * j + o, 37:40, :] = t[0:3]
                    a1[2 * j + o, 15:16, :] = t[3:4]
                    a1[2 * j + o, 31:32, :] = t[4:5]
            x1[d, 2 * j, 5:8, :] = tag
            x1[d, 2 * j + 1, 5:8, :] = tag
    loads[5].wait()
    for v in range(5):
        for z in range(8):
            ct[z, 16 * v : 16 * v + 16, :] = cb[v, :, z, :]
    y = iota((128, 128), 0)
    k = iota((128, 128), 1) // 8
    plane = jnp.where(k < 6, 16 * (k + 1) - 1, jnp.where(k < 12, 16 * (k - 4), -1))
    sel = ones_where(y == plane)
    lane8 = lax.rem(iota((80, 128), 1), 8)
    acc = jnp.zeros((80, 128), F32)
    planes = dot3(ct[...].reshape(640, 128), sel)
    for z in range(8):
        acc = jnp.where(lane8 == z, planes[80 * z : 80 * z + 80], acc)
    first = ct[0]
    last = ct[7]
    own = jnp.where(half == 0, first, last)
    for v in range(5):
        cut = slice(16 * v, 16 * v + 16)
        a1[:, 10 + v, :] = acc[cut]
        a1[:, 26 + v, :] = own[cut]
        rz[0, v] = first[cut]
        rz[1, v] = last[cut]

    pl.semaphore_wait(barrier, 3 * NP - 1)
    one = []
    two = []
    for d in [*range(1, NP), 0]:
        j = peer[d]
        if d:
            one.append(copy(d - 1, a1.at[j], ba.at[me], (s, j)))
            one[-1].start()
        for c in (
            copy(S_X + 2 * d, x1.at[0, j], bx.at[1, me], (down, j)),
            copy(S_X + 2 * d + 1, x1.at[1, j], bx.at[0, me], (up, j)),
        ):
            c.start()
            one.append(c)
    two = [
        copy(S_H, cb.at[:, 0], ocx.at[1], (down, me)),
        copy(S_H + 1, cb.at[:, 15], ocx.at[0], (up, me)),
        copy(S_H + 2, rz.at[1], oz.at[0], (s, lax.rem(me + 1, NP))),
        copy(S_H + 3, rz.at[0], oz.at[1], (s, lax.rem(me + N1, NP))),
    ]
    for c in two:
        c.start()
    own = pltpu.make_async_copy(a1.at[me], ba.at[me], ls.at[6])
    own.start()

    src = iota((1024, 256), 0)
    dst = iota((1024, 256), 1)
    zz = 8 * (dst // 128) + 7 - lax.rem(dst, 128) // 16
    pair = ones_where((src // 64 == zz) & (lax.rem(src, 32) // 2 == lax.rem(dst, 16)))

    def interior(p):
        def along_x(j, _):
            cut = pl.ds(pl.multiple_of(128 * j, 128), 128)
            q = [fb[v, p, :, cut] for v in range(5)]
            f, a = flux(q, state(q), 0)
            nxt = lambda t: pltpu.roll(t, 31, 0)
            hi = rusanov(q, f, a, [nxt(t) for t in q], [nxt(t) for t in f], nxt(a))
            inner = iota((32, 128), 0) < 31
            for v in range(5):
                t = jnp.where(inner, hi[v], 0.0)
                chg[v, :, cut] = t - pltpu.roll(t, 1, 0)
            return 0

        lax.fori_loop(0, 8, along_x, 0, unroll=2)

        def rows(c, _):
            cut = pl.ds(pl.multiple_of(8 * c, 8), 8)
            q = [fb[v, p, cut, :] for v in range(5)]
            st = state(q)
            l8 = iota((8, 1024), 1)
            change = [chg[v, cut, :] for v in range(5)]
            for way, shift, inner in ((2, 32, l8 < 992), (1, 1, (l8 & 31) < 31)):
                f, a = flux(q, st, way)
                nxt = lambda t: pltpu.roll(t, 1024 - shift, 1)
                hi = rusanov(q, f, a, [nxt(t) for t in q], [nxt(t) for t in f], nxt(a))
                for v in range(5):
                    t = jnp.where(inner, hi[v], 0.0)
                    change[v] = change[v] + (t - pltpu.roll(t, shift, 1))
            for v in range(5):
                fs[v, p, cut, :] = q[v] - 0.1 * change[v]
            return 0

        lax.fori_loop(0, 4, rows, 0)
        m = dot3(fs[:, p].reshape(160, 1024), pair)
        for h in range(2):
            big[h] = m[:, 128 * h : 128 * h + 128]
            for v in range(5):
                a = 32 * v
                av[:, 10 * p + 5 * h + v, :] = 0.125 * (big[h, pl.ds(a, 16, 2), :] + big[h, pl.ds(a + 1, 16, 2), :])
        for k in range(2):
            av[:, 20 + 2 * p + k, :] = jnp.zeros((16, 128), F32)

    interior(0)
    interior(1)
    early = []
    for d in range(1, NP):
        early.append(copy(S_A + d - 1, av.at[peer[d]], bb.at[me], (s, peer[d])))
        early[-1].start()
    own_av = pltpu.make_async_copy(av.at[me], bb.at[me], ls.at[7])
    own_av.start()
    def place(t, _):
        n = ids[0, t]
        gy = cols[0, n]
        gz = cols[1, n]
        nbr[4, t] = gy
        nbr[5, t] = gz
        nbr[6, t] = gy + 8 * gz + GOFF
        return 0

    lax.fori_loop(0, 32, place, 0)
    for i in range(GOFF):
        grid[0, i] = jnp.int32(-1)

    def find(k, _):
        q = jnp.int32(-1)
        for t in range(32):
            q = jnp.where(nbr[6, t] == k, t, q)
        grid[0, k] = q
        return 0

    lax.fori_loop(GOFF, GOFF + 48, find, 0)
    for i in range(GOFF + 48, 96):
        grid[0, i] = jnp.int32(-1)

    src = iota((128, 128), 0)
    dst = iota((128, 128), 1)
    g = dst // 32
    i = lax.rem(dst, 32) // 2
    base = jnp.where(g == 0, 0, jnp.where(g == 1, 48, jnp.where(g == 2, 64, 80)))
    spread = ones_where(src == base + i)
    sub = iota((32, 128), 0)
    l1 = iota((1, 128), 1)
    want = jnp.zeros((32, 128), I32)
    code = jnp.zeros((32, 128), I32)
    codes = jnp.full((1, 128), -99, I32)
    for i in range(NP):
        for p in range(2):
            k = NP * p + i
            want = jnp.where(sub == k, ids[0, 2 * i + p], want)
            code = jnp.where(sub == k, nbr[6, 2 * i + p], code)
            codes = jnp.where(l1 == k, nbr[6, 2 * i + p], codes)
    want = want.astype(F32)
    own.wait()
    for c in one:
        c.wait()

    lane = iota((8, 128), 1)

    def place_coarse(j, _):
        for p in range(2):
            gy = nbr[4, 2 * j + p]
            gz = nbr[5, 2 * j + p]
            a = 2 * (gz + 1)
            r0 = pltpu.roll(ba[a, 8:16, :], (128 - 8 * gy) & 127, 1)
            r1 = pltpu.roll(ba[a + 1, 8:16, :], (136 - 8 * gy) & 127, 1)
            r2 = pltpu.roll(ba[2 * gz + 1, 24:32, :], (176 - 16 * gy) & 127, 1)
            r3 = pltpu.roll(ba[2 * gz + 4, 24:32, :], (192 - 16 * gy) & 127, 1)
            cg[NP * p + j] = jnp.where(lane < 64, jnp.where((lane & 8) == 0, r0, r1), jnp.where(lane < 80, r2, r3))
        return 0

    lax.fori_loop(0, NP, place_coarse, 0, unroll=4)
    cg[...] = dot3(cg[...].reshape(256, 128), spread).reshape(32, 8, 128)
    packs = [
        jnp.concatenate([ba[:, k, :], ba[:, 16 + k, :]], axis=0) for k in range(10)
    ]
    data = jnp.concatenate(packs, axis=1)
    group = iota((32, 128), 1) // 32
    near = []
    absent = jnp.zeros((32, 128), F32)
    for g, step in enumerate((-1, 1, -8, 8)):
        hit = codes == code + step
        near.append(ones_where(hit)[:, 0:32])
        some = jnp.sum(jnp.where(hit, 1.0, 0.0), axis=1, keepdims=True)
        absent = jnp.where(group == g, 1.0 - some, absent)
    near = dot3_left(jnp.concatenate(near, axis=0), data)
    theirs = []
    mine = []
    low = (group & 1) == 0
    for v in range(5):
        both = []
        for xr in range(2):
            k = 128 * (5 * xr + v)
            n = [near[32 * g : 32 * g + 32, k : k + 128] for g in range(4)]
            n = jnp.where(group == 0, n[0], jnp.where(group == 1, n[1], jnp.where(group == 2, n[2], n[3])))
            both.append(jnp.where(absent > 0.5, cg[:, 2 + v, :], n))
        theirs.append(jnp.concatenate(both, axis=0))
        both = [jnp.where(low, pltpu.roll(packs[5 * xr + v], 96, 1), pltpu.roll(packs[5 * xr + v], 32, 1)) for xr in range(2)]
        mine.append(jnp.concatenate(both, axis=0))
    g1 = iota((64, 128), 1)
    low = ((g1 // 32) & 1) == 0
    isy = g1 < 64

    def face_flux(q):
        r, pr, c = state(q)
        mn = jnp.where(isy, q[2], q[3])
        u = mn * r
        py = jnp.where(isy, pr, 0.0)
        f = [mn, q[1] * u, q[2] * u + py, q[3] * u + (pr - py), (q[4] + pr) * u]
        return f, jnp.abs(u) + c

    ql = [jnp.where(low, theirs[v], mine[v]) for v in range(5)]
    qr = [jnp.where(low, mine[v], theirs[v]) for v in range(5)]
    fl, al = face_flux(ql)
    fr, ar = face_flux(qr)
    f = rusanov(ql, fl, al, qr, fr, ar)
    for v in range(5):
        for p in range(2):
            for xr in range(2):
                a = 32 * xr + 16 * p
                dd[:, p, 5 * xr + v, :] = f[v][a : a + 16]
    sums = jnp.concatenate([f[v][0:32] + f[v][32:64] for v in range(5)], axis=0)
    l16 = iota((16, 128), 1)
    diagonal = l16 == iota((16, 128), 0)
    own_x = [32 + k for k in range(8)] + [15, 31]
    sides = []
    for way in range(2):
        tag = bx[way, :, 5, :]
        data = jnp.concatenate([bx[way, :, v, :] for v in range(5)], axis=1)
        got = []
        for t in range(2):
            tt_ = pltpu.roll(tag, 64, 1) if t else tag
            row = jnp.sum(jnp.where(diagonal, tt_, 0.0), axis=0, keepdims=True)
            got.append(ones_where(want == row)[:, 0:16])
        got = dot3_left(jnp.concatenate(got, axis=0), data)
        theirs = []
        for v in range(5):
            g0 = got[0:32, 128 * v : 128 * v + 128]
            g1 = got[32:64, 128 * v : 128 * v + 128]
            a = g0[0:16] + pltpu.roll(g1[0:16], 64, 1)
            b = pltpu.roll(g0[16:32], 64, 1) + g1[16:32]
            t = jnp.where(l16 < 64, a, b)
            theirs.append(jnp.where(s == (0 if way == 0 else NS - 1), ba[:, own_x[5 * way + v], :], t))
        sides.append(theirs)
    mine = [jnp.concatenate([ba[:, own_x[v], :], ba[:, own_x[5 + v], :]], axis=0) for v in range(5)]
    theirs = [jnp.concatenate([sides[0][v], sides[1][v]], axis=0) for v in range(5)]
    low = iota((32, 128), 0) < 16
    ql = [jnp.where(low, theirs[v], mine[v]) for v in range(5)]
    qr = [jnp.where(low, mine[v], theirs[v]) for v in range(5)]
    fl, al = flux(ql, state(ql), 0)
    fr, ar = flux(qr, state(qr), 0)
    f = rusanov(ql, fl, al, qr, fr, ar)
    fx = [jnp.where(low, -t, t) for t in f]
    for v in range(5):
        for way in range(2):
            dd[:, way, 10 + v, :] = fx[v][16 * way : 16 * way + 16]
    dd[:, 0, 15, :] = jnp.zeros((16, 128), F32)
    dd[:, 1, 15, :] = jnp.zeros((16, 128), F32)

    late = []
    for d in range(1, NP):
        late.append(copy(S_G + d - 1, dd.at[peer[d]], og.at[me], (s, peer[d])))
        late[-1].start()
    own = pltpu.make_async_copy(dd.at[me], og.at[me], ls.at[6])
    own.start()

    src = iota((128, 256), 0)
    dst = iota((128, 256), 1)
    g = src // 32
    i = lax.rem(src, 32) // 2
    zz = 8 * (dst // 128) + 7 - lax.rem(dst, 128) // 16
    yy = lax.rem(dst, 16)
    far = 15 * (g & 1)
    hit = (zz == jnp.where(g < 2, i, far)) & (yy == jnp.where(g < 2, far, i))
    sign = jnp.where((g & 1) == 0, -1.0, 1.0)
    mean_of = jnp.where(hit, sign, 0.0).astype(BF16)
    src = iota((128, 128), 0)
    dst = iota((128, 128), 1)
    g = src // 32
    i = lax.rem(src, 32) // 2
    z_at = 64 * (i // 8) + 7 - lax.rem(i, 8)
    at = jnp.where(g == 0, z_at, jnp.where(g == 1, z_at + 17, jnp.where(g == 2, 96 + i, 32 + i)))
    reflux = ones_where(dst == at)
    low = ((l1 & 63) < 8) | (l1 >= 96)
    coef = jnp.where(low, -0.05, 0.05).astype(F32) * 0.25
    fix = dot3(sums, mean_of) * -0.0125
    refl = dot3(sums, reflux) * coef
    l32 = iota((32, 128), 1)
    yr = [jnp.zeros((32, 128), F32)] * 2
    zr = [jnp.zeros((32, 128), F32)] * 2
    for v in range(5):
        w = refl[32 * v : 32 * v + 32]
        for h in range(2):
            cc[:, h, v, :] = fix[32 * v : 32 * v + 32, 128 * h : 128 * h + 128]
            yr[h] = jnp.where((l32 >= 25 * v) & (l32 < 25 * v + 25), moved(w, 25 * v - 64 * h), yr[h])
            zr[h] = jnp.where(l32 // 16 == 4 - v, moved(w, 16 * (4 - v) - 64 * h - 32), zr[h])
    for h in range(2):
        cc[:, h, 5, :] = moved(yr[h], -32)
        cc[:, h, 6, :] = moved(zr[h], 48)
        cc[:, h, 7, :] = jnp.zeros((32, 128), F32)
    src = iota((128, 128), 0)
    dst = iota((128, 128), 1)
    sums = jnp.concatenate(fx, axis=0)
    for p in range(2):
        m = dot3(sums, ones_where((src // 64 == p) & ((src & 31) // 2 == (dst & 15)))) * -0.0125
        for v in range(5):
            xt[:, p, v, :] = m[32 * v : 32 * v + 32]
        for v in range(5, 8):
            xt[:, p, v, :] = jnp.zeros((32, 128), F32)
    for c in two:
        c.wait()
    mid = provisional(s, me, cb, oz, ocx, grid, prov)
    own_av.wait()
    for c in early:
        c.wait()

    def turn(i, _):
        for p in range(2):
            gy = nbr[4, 2 * i + p]
            for h in range(2):
                k = 10 * p + 5 * h
                t = jnp.concatenate([bb[i, k : k + 5, :], jnp.zeros((3, 128), F32)], axis=0)
                tt[i, p, h] = pltpu.roll(t + cc[NP * p + i, h], (16 * gy + 32) & 127, 1)
        return 0

    lax.fori_loop(0, NP, turn, 0, unroll=4)
    lane = iota((8, 128), 1)
    sub = iota((8, 128), 0)
    block = lane // 16
    ring = (block + sub) & 7
    slope = lane + sub - 7
    def expand_to(j):
        h = lax.rem(j, 2)
        r = j // 2
        far = r - 2 + 2 * h
        acc = [jnp.zeros((8, 128), F32)] * 5
        accy = [jnp.zeros((8, 128), F32)] * 5
        accz = jnp.zeros((8, 128), F32)
        covered = jnp.zeros((8, 128), F32)
        side = [jnp.zeros((8, 128), F32)] * 2
        for gy in range(6):
            a = grid[0, gy + 8 * (r - 1) + GOFF]
            b = grid[0, gy + 8 * far + GOFF]
            a0 = jnp.maximum(a, 0)
            b0 = jnp.maximum(b, 0)
            t = tt[a0 // 2, a0 & 1, h]
            zt = tt[b0 // 2, b0 & 1, h, 6:7, :]
            for way in range(2):
                side[way] = jnp.where((block == gy + 1) & (a >= 0), xt[NP * way + a0 // 2, a0 & 1], side[way])
            covered = jnp.where((block == gy + 1) & (a >= 0), 1.0, covered)
            ina = (ring == gy + 1) & (a >= 0)
            accz = jnp.where((ring == gy + 1) & (b >= 0), zt, accz)
            for v in range(5):
                acc[v] = jnp.where(ina, t[v : v + 1], acc[v])
                off = (slope - 16 * gy - 25 * v) & 127
                accy[v] = jnp.where(((off == 0) | (off == 17)) & (a >= 0), t[5:6], accy[v])
        accz = pltpu.roll(accz, 0, 1, stride=16, stride_axis=0)
        for v in range(5):
            val = pltpu.roll(acc[v], 0, 1, stride=16, stride_axis=0)
            add = moved(pltpu.roll(accy[v], 0, 1, stride=1, stride_axis=0), 8 - 25 * v)
            add = add + jnp.where(sub == 7 * h, accz[v : v + 1], 0.0)
            ee[j, v] = jnp.where(covered > 0, val, add)
        se[j, 0] = side[0]
        se[j, 1] = side[1]

    def expanded(d):
        return copy(S_E + d - 1, ee.at[peer[d]], oe.at[me], (s, peer[d]))

    def sided(d):
        return copy(S_S + d - 1, se.at[peer[d]], so.at[lax.rem(me, 8)], (s, peer[d]))

    def takes(j):
        return (j > 0) & (j < NP - 1)

    def takes_side(j, m):
        return (j > 1) & (j < NP - 2) & (lax.rem(j, 2) == m // 8)

    order = [*range(1, NP), 0]
    for b in range(0, NP, 4):
        for d in order[b : b + 4]:
            expand_to(peer[d])
        for d in order[b : b + 4]:
            if d == 0:
                continue

            @pl.when(takes(peer[d]))
            def _():
                expanded(d).start()

            @pl.when(takes_side(peer[d], me))
            def _():
                sided(d).start()

    own_ee = pltpu.make_async_copy(ee.at[me], oe.at[me], ls.at[7])
    own_se = pltpu.make_async_copy(se.at[me], so.at[lax.rem(me, 8)], ls.at[0])

    @pl.when(takes(me))
    def _():
        own_ee.start()

    @pl.when(takes_side(me, me))
    def _():
        own_se.start()

    @pl.when(jnp.logical_not(takes(me)))
    def _():
        oe[...] = jnp.zeros((16, 5, 8, 128), F32)

    @pl.when((me < 2) | (me >= NP - 2))
    def _():
        so[...] = jnp.zeros((8, 2, 8, 128), F32)

    src = iota((128, 1024), 0)
    dst = iota((128, 1024), 1)
    g = src // 32
    i = lax.rem(src, 32)
    at = jnp.where(g == 0, 32 * i, jnp.where(g == 1, 32 * i + 31, jnp.where(g == 2, i, 992 + i)))
    sign = jnp.where((g & 1) == 0, -1.0, 1.0)
    expand = jnp.where(dst == at, sign, 0.0).astype(BF16)
    own.wait()
    for c in late:
        c.wait()
    l5 = iota((5, 128), 1)
    for way in range(2):
        for j in range(8):
            e = og[2 * j, way, 10:15, :]
            o = og[2 * j + 1, way, 10:15, :]
            cut = slice(128 * j, 128 * j + 128)
            xg[:, way, cut] = jnp.where(l5 < 64, e, pltpu.roll(o, 64, 1))
            xg[:, 2 + way, cut] = jnp.where(l5 < 64, pltpu.roll(e, 64, 1), o)
    for p in range(2):
        for v in range(5):
            for xr in range(2):
                bf[pl.ds(32 * v + xr, 16, 2), :] = og[:, p, 5 * xr + v, :]
        m = dot3(bf[...], expand)
        for v in range(5):
            fs[v, p] = fs[v, p] - 0.1 * m[32 * v : 32 * v + 32]
            for way, x in ((0, 0), (1, 31)):
                fs[v, p, x : x + 1, :] = fs[v, p, x : x + 1, :] - 0.1 * xg[v, 2 * p + way : 2 * p + way + 1, :]

    @pl.when(takes(me))
    def _():
        own_ee.wait()
        for d in range(1, NP):
            expanded(d).wait_recv()

    @pl.when(takes_side(me, me))
    def _():
        own_se.wait()

    for d in range(1, NP):
        @pl.when(takes(peer[d]))
        def _():
            expanded(d).wait_send()

        @pl.when(takes_side(peer[d], me))
        def _():
            sided(d).wait_send()

        @pl.when(takes_side(me, source[d]))
        def _():
            sided(d).wait_recv()

    for x in range(16):
        for v in range(5):
            e = oe[x, v]
            if x in (0, 15):
                e = e + so[:, x // 15, v, :]
            prov[v, x] = jnp.where(mid > 0, e, prov[v, x] + e)


def copy_kernel(a, b, a_out, b_out, sems):
    n = a.shape[0]
    copies = []
    for v in range(n):
        copies.append(pltpu.make_async_copy(b.at[v, 0], b_out.at[v, 0], sems.at[n + v]))
        copies.append(pltpu.make_async_copy(b.at[v, 1], b_out.at[v, 1], sems.at[2 * n + v]))
        copies.append(pltpu.make_async_copy(a.at[v], a_out.at[v], sems.at[v]))
    for c in copies:
        c.start()
    for c in copies:
        c.wait()


def vm():
    return pl.BlockSpec(memory_space=pltpu.VMEM)


def hb():
    return pl.BlockSpec(memory_space=pltpu.HBM)


def sds(*shape, dtype=F32):
    return jax.ShapeDtypeStruct(shape, dtype)


def buf(*shape):
    return pltpu.VMEM(shape, F32)


LIMIT = 48 << 20


def pin(x):
    return pltpu.with_memory_space_constraint(x, pltpu.HBM)


def local(coarse, fine, columns, patch_ids):
    fo, co = pl.pallas_call(
        step_kernel,
        out_shape=(sds(5, 2, 32, 1024), sds(5, 16, 8, 128)),
        in_specs=[hb()] * 4,
        out_specs=(vm(), vm()),
        scratch_shapes=[
            pltpu.SMEM((1, 32), I32),
            pltpu.SMEM((2, 32), I32),
            pltpu.SMEM((7, 32), I32),
            pltpu.SMEM((1, 96), I32),
            buf(5, 2, 32, 1024),
            buf(5, 16, 8, 128),
            buf(16, 40, 128),
            buf(2, 16, 8, 128),
            buf(2, 5, 16, 128),
            buf(8, 80, 128),
            buf(320, 128),
            buf(16, 40, 128),
            buf(2, 16, 8, 128),
            buf(32, 8, 128),
            buf(16, 2, 16, 128),
            buf(16, 2, 16, 128),
            buf(2, 5, 16, 128),
            buf(2, 5, 8, 128),
            buf(160, 128),
            buf(5, 4, 1024),
            buf(16, 24, 128),
            buf(16, 24, 128),
            buf(32, 2, 8, 128),
            buf(32, 2, 8, 128),
            buf(16, 2, 2, 8, 128),
            buf(16, 5, 8, 128),
            buf(16, 5, 8, 128),
            buf(16, 2, 8, 128),
            buf(8, 2, 8, 128),
            buf(2, 160, 128),
            buf(5, 32, 1024),
            pltpu.SemaphoreType.DMA((N_SEM,)),
            pltpu.SemaphoreType.DMA((N_SEM,)),
            pltpu.SemaphoreType.DMA((8,)),
        ],
        compiler_params=pltpu.CompilerParams(collective_id=0, has_side_effects=True, vmem_limit_bytes=LIMIT),
        name="step",
    )(pin(fine), pin(coarse), pin(patch_ids), pin(columns.T))
    return pl.pallas_call(
        copy_kernel,
        out_shape=(sds(5, 16, 8, 128), sds(5, 2, 32, 1024)),
        in_specs=[pl.BlockSpec(memory_space=pl.ANY)] * 2,
        out_specs=(hb(), hb()),
        scratch_shapes=[pltpu.SemaphoreType.DMA((15,))],
        compiler_params=pltpu.CompilerParams(vmem_limit_bytes=LIMIT),
        name="copy_out",
    )(co, fo)


def solution(mesh):
    return jax.shard_map(
        local,
        mesh=mesh,
        in_specs=(
            P(None, "slab", "patch", None),
            P(None, ("slab", "patch"), None, None),
            P(),
            P("slab", None),
        ),
        out_specs=(P(None, "slab", "patch", None), P(None, ("slab", "patch"), None, None)),
        check_vma=False,
    )
```

```python
import jax
import jax.numpy as jnp
from jax import lax
from jax.experimental import pallas as pl
from jax.experimental.pallas import tpu as pltpu
from jax.sharding import PartitionSpec as P

F32 = jnp.float32
BF16 = jnp.bfloat16
I32 = jnp.int32
MESH = pl.DeviceIdType.MESH
NS = 8
NP = 16
GOFF = 16


def iota(shape, dim):
    return lax.broadcasted_iota(I32, shape, dim)


def dot3(x, m):
    hi = x.astype(BF16)
    r = x - hi.astype(F32)
    mid = r.astype(BF16)
    lo = (r - mid.astype(F32)).astype(BF16)
    n = x.shape[0]
    y = jnp.dot(jnp.concatenate([hi, mid, lo], axis=0), m, preferred_element_type=F32)
    return y[0:n] + (y[n : 2 * n] + y[2 * n : 3 * n])


def dot3_left(m, x):
    hi = x.astype(BF16)
    r = x - hi.astype(F32)
    mid = r.astype(BF16)
    lo = (r - mid.astype(F32)).astype(BF16)
    d = lambda a: jnp.dot(m, a, preferred_element_type=F32)
    return d(hi) + (d(mid) + d(lo))


def moved(x, k):
    return pltpu.roll(x, k % 128, 1) if k % 128 else x


def ones_where(c):
    return jnp.where(c, 1.0, 0.0).astype(BF16)


def state(q):
    r = 1.0 / q[0]
    p = 0.4 * (q[4] - 0.5 * ((q[1] * q[1] + q[2] * q[2] + q[3] * q[3]) * r))
    c = jnp.sqrt(1.4 * p * r)
    return r, p, c


def flux(q, s, d):
    r, p, c = s
    u = q[1 + d] * r
    f = [q[1 + d], q[1] * u, q[2] * u, q[3] * u, (q[4] + p) * u]
    f[1 + d] = f[1 + d] + p
    return f, jnp.abs(u) + c


def rusanov(ql, fl, al, qr, fr, ar):
    a = 0.5 * jnp.maximum(al, ar)
    return [0.5 * (fl[v] + fr[v]) - a * (qr[v] - ql[v]) for v in range(5)]


def provisional(s, me, coarse, oz, ocx, grid, prov):
    r = me // 2
    h = lax.rem(me, 2)
    lane = iota((8, 128), 1)
    sub = iota((8, 128), 0)
    blocks = lane // 16

    def cover(row):
        m = jnp.zeros((8, 128), F32)
        for gy in range(6):
            m = jnp.where((blocks == gy + 1) & (grid[0, gy + 8 * (row - 1) + GOFF] >= 0), 1.0, m)
        return m

    mid = cover(r)
    below = jnp.where(h == 0, cover(r - 1), mid)
    above = jnp.where(h == 1, cover(r + 1), mid)
    free = 1.0 - mid
    fup = free * (1.0 - pltpu.roll(mid, 127, 1))
    flo = free * (1.0 - pltpu.roll(mid, 1, 1))
    zlo = free * (1.0 - jnp.where(sub == 0, below, mid))
    zhi = free * (1.0 - jnp.where(sub == 7, above, mid))

    def cells(x):
        q = [coarse[v, x] for v in range(5)]
        st = state(q)
        return q, st, flux(q, st, 0)

    def face(a, b):
        return rusanov(a[0], a[2][0], a[2][1], b[0], b[2][0], b[2][1])

    first = cells(0)
    q = [jnp.where(s == 0, coarse[v, 0], ocx[0, v]) for v in range(5)]
    st = state(q)
    lower = face((q, st, flux(q, st, 0)), first)
    here = first
    for x in range(16):
        if x < 15:
            there = cells(x + 1)
        else:
            q = [jnp.where(s == NS - 1, coarse[v, 15], ocx[1, v]) for v in range(5)]
            st = state(q)
            there = (q, st, flux(q, st, 0))
        upper = face(here, there)
        q, st, _ = here
        change = [(upper[v] - lower[v]) * free for v in range(5)]
        row = slice(x, x + 1)
        zn = [jnp.where(sub == 7, jnp.where(me == NP - 1, q[v], oz[1, v, row, :]), pltpu.roll(q[v], 7, 0)) for v in range(5)]
        zb = [jnp.where(sub == 0, jnp.where(me == 0, q[v], oz[0, v, row, :]), pltpu.roll(q[v], 1, 0)) for v in range(5)]
        f, a = flux(q, st, 2)
        fn, an = flux(zn, state(zn), 2)
        fb, ab = flux(zb, state(zb), 2)
        up = rusanov(q, f, a, zn, fn, an)
        lo = rusanov(zb, fb, ab, q, f, a)
        change = [change[v] + (up[v] * zhi - lo[v] * zlo) for v in range(5)]
        f, a = flux(q, st, 1)
        nxt = lambda t: jnp.where(lane == 127, t, pltpu.roll(t, 127, 1))
        prv = lambda t: jnp.where(lane == 0, t, pltpu.roll(t, 1, 1))
        up = rusanov(q, f, a, [nxt(t) for t in q], [nxt(t) for t in f], nxt(a))
        lo = rusanov([prv(t) for t in q], [prv(t) for t in f], prv(a), q, f, a)
        for v in range(5):
            prov[v, x] = q[v] - 0.05 * (change[v] + (up[v] * fup - lo[v] * flo))
        here = there
        lower = upper
    return mid


N1 = NP - 1
OFFSETS = sorted(
    ((dx, dz) for dx in range(4) for dz in range(4)),
    key=lambda o: (o != (0, 0), -(min(o[0], 4 - o[0]) + min(o[1], 4 - o[1]))),
)
S_X = N1
S_H = S_X + 2 * NP
S_G = S_H + 4
S_A = S_G + N1
S_E = S_A + N1
S_S = S_E + N1
N_SEM = S_S + N1


def step_kernel(
    fine, coarse, ids_in, cols_in, fs, prov,
    ids, cols, nbr, grid, fb, cb, a1, x1, rz, ct, pk, ba, bx, cg, dd, og, oz, ocx,
    bf, xg, av, bb, cc, xt, tt, ee, oe, se, so, big, chg, ss, rs, ls,
):
    s = lax.axis_index("slab")
    me = lax.axis_index("patch")
    half = lax.rem(me, 2)
    up = lax.rem(s + 1, NS)
    down = lax.rem(s + NS - 1, NS)
    x, z = me // 4, lax.rem(me, 4)
    peer = [lax.rem(x + dx, 4) * 4 + lax.rem(z + dz, 4) for dx, dz in OFFSETS]
    source = [lax.rem(x + 4 - dx, 4) * 4 + lax.rem(z + 4 - dz, 4) for dx, dz in OFFSETS]
    loads = [pltpu.make_async_copy(fine.at[v], fb.at[v], ls.at[v]) for v in range(5)]
    loads.append(pltpu.make_async_copy(coarse, cb, ls.at[5]))
    loads.append(pltpu.make_async_copy(ids_in, ids, ls.at[6]))
    loads.append(pltpu.make_async_copy(cols_in, cols, ls.at[7]))
    barrier = pltpu.get_barrier_semaphore()
    for c in loads:
        c.start()
    for d in range(NP):
        if d:
            pl.semaphore_signal(barrier, inc=1, device_id=(s, peer[d]), device_id_type=MESH)
        pl.semaphore_signal(barrier, inc=1, device_id=(up, peer[d]), device_id_type=MESH)
        pl.semaphore_signal(barrier, inc=1, device_id=(down, peer[d]), device_id_type=MESH)

    def copy(k, src, dst, dev):
        return pltpu.make_async_remote_copy(
            src_ref=src, dst_ref=dst, send_sem=ss.at[k], recv_sem=rs.at[k],
            device_id=dev, device_id_type=MESH,
        )

    k = iota((1024, 128), 0)
    c = iota((1024, 128), 1)
    g = c // 32
    i = lax.rem(c, 32)
    want = jnp.where(g == 0, 32 * i + 31, jnp.where(g == 1, 32 * i, jnp.where(g == 2, 992 + i, i)))
    sel = ones_where(k == want)
    for v in range(5):
        loads[v].wait()
    pk[...] = dot3(fb[...].reshape(320, 1024), sel)
    for v in range(5):
        for p in range(2):
            for xr in range(2):
                a1[:, 16 * p + 5 * xr + v, :] = pk[pl.ds(64 * v + 32 * p + xr, 16, 2), :]
    loads[6].wait()
    loads[7].wait()
    lane = iota((5, 128), 1)
    tag = jnp.where(iota((3, 128), 1) < 64, ids[0, 2 * me], ids[0, 2 * me + 1]).astype(F32)
    for d, row in ((0, 0), (1, 31)):
        for j in range(8):
            t0 = fb[:, 0, row, 128 * j : 128 * j + 128]
            t1 = fb[:, 1, row, 128 * j : 128 * j + 128]
            for o, t in (
                (0, jnp.where(lane < 64, t0, pltpu.roll(t1, 64, 1))),
                (1, jnp.where(lane < 64, pltpu.roll(t0, 64, 1), t1)),
            ):
                x1[d, 2 * j + o, 0:5, :] = t
                if d == 0:
                    a1[2 * j + o, 32:37, :] = t
                else:
                    a1[2 * j + o, 37:40, :] = t[0:3]
                    a1[2 * j + o, 15:16, :] = t[3:4]
                    a1[2 * j + o, 31:32, :] = t[4:5]
            x1[d, 2 * j, 5:8, :] = tag
            x1[d, 2 * j + 1, 5:8, :] = tag
    loads[5].wait()
    for v in range(5):
        for z in range(8):
            ct[z, 16 * v : 16 * v + 16, :] = cb[v, :, z, :]
    y = iota((128, 128), 0)
    k = iota((128, 128), 1) // 8
    plane = jnp.where(k < 6, 16 * (k + 1) - 1, jnp.where(k < 12, 16 * (k - 4), -1))
    sel = ones_where(y == plane)
    lane8 = lax.rem(iota((80, 128), 1), 8)
    acc = jnp.zeros((80, 128), F32)
    planes = dot3(ct[...].reshape(640, 128), sel)
    for z in range(8):
        acc = jnp.where(lane8 == z, planes[80 * z : 80 * z + 80], acc)
    first = ct[0]
    last = ct[7]
    own = jnp.where(half == 0, first, last)
    for v in range(5):
        cut = slice(16 * v, 16 * v + 16)
        a1[:, 10 + v, :] = acc[cut]
        a1[:, 26 + v, :] = own[cut]
        rz[0, v] = first[cut]
        rz[1, v] = last[cut]

    pl.semaphore_wait(barrier, 3 * NP - 1)
    one = []
    two = []
    for d in [*range(1, NP), 0]:
        j = peer[d]
        if d:
            one.append(copy(d - 1, a1.at[j], ba.at[me], (s, j)))
            one[-1].start()
        for c in (
            copy(S_X + 2 * d, x1.at[0, j], bx.at[1, me], (down, j)),
            copy(S_X + 2 * d + 1, x1.at[1, j], bx.at[0, me], (up, j)),
        ):
            c.start()
            one.append(c)
    two = [
        copy(S_H, cb.at[:, 0], ocx.at[1], (down, me)),
        copy(S_H + 1, cb.at[:, 15], ocx.at[0], (up, me)),
        copy(S_H + 2, rz.at[1], oz.at[0], (s, lax.rem(me + 1, NP))),
        copy(S_H + 3, rz.at[0], oz.at[1], (s, lax.rem(me + N1, NP))),
    ]
    for c in two:
        c.start()
    own = pltpu.make_async_copy(a1.at[me], ba.at[me], ls.at[6])
    own.start()

    src = iota((1024, 256), 0)
    dst = iota((1024, 256), 1)
    zz = 8 * (dst // 128) + 7 - lax.rem(dst, 128) // 16
    pair = ones_where((src // 64 == zz) & (lax.rem(src, 32) // 2 == lax.rem(dst, 16)))

    def interior(p):
        def along_x(j, _):
            cut = pl.ds(pl.multiple_of(128 * j, 128), 128)
            q = [fb[v, p, :, cut] for v in range(5)]
            f, a = flux(q, state(q), 0)
            nxt = lambda t: pltpu.roll(t, 31, 0)
            hi = rusanov(q, f, a, [nxt(t) for t in q], [nxt(t) for t in f], nxt(a))
            inner = iota((32, 128), 0) < 31
            for v in range(5):
                t = jnp.where(inner, hi[v], 0.0)
                chg[v, :, cut] = t - pltpu.roll(t, 1, 0)
            return 0

        lax.fori_loop(0, 8, along_x, 0)

        def rows(c, _):
            cut = pl.ds(pl.multiple_of(8 * c, 8), 8)
            q = [fb[v, p, cut, :] for v in range(5)]
            st = state(q)
            l8 = iota((8, 1024), 1)
            change = [chg[v, cut, :] for v in range(5)]
            for way, shift, inner in ((2, 32, l8 < 992), (1, 1, (l8 & 31) < 31)):
                f, a = flux(q, st, way)
                nxt = lambda t: pltpu.roll(t, 1024 - shift, 1)
                hi = rusanov(q, f, a, [nxt(t) for t in q], [nxt(t) for t in f], nxt(a))
                for v in range(5):
                    t = jnp.where(inner, hi[v], 0.0)
                    change[v] = change[v] + (t - pltpu.roll(t, shift, 1))
            for v in range(5):
                fs[v, p, cut, :] = q[v] - 0.1 * change[v]
            return 0

        lax.fori_loop(0, 4, rows, 0)
        m = dot3(fs[:, p].reshape(160, 1024), pair)
        for h in range(2):
            big[h] = m[:, 128 * h : 128 * h + 128]
            for v in range(5):
                a = 32 * v
                av[:, 10 * p + 5 * h + v, :] = 0.125 * (big[h, pl.ds(a, 16, 2), :] + big[h, pl.ds(a + 1, 16, 2), :])
        for k in range(2):
            av[:, 20 + 2 * p + k, :] = jnp.zeros((16, 128), F32)

    interior(0)
    interior(1)
    early = []
    for d in range(1, NP):
        early.append(copy(S_A + d - 1, av.at[peer[d]], bb.at[me], (s, peer[d])))
        early[-1].start()
    own_av = pltpu.make_async_copy(av.at[me], bb.at[me], ls.at[7])
    own_av.start()
    def place(t, _):
        n = ids[0, t]
        gy = cols[0, n]
        gz = cols[1, n]
        nbr[4, t] = gy
        nbr[5, t] = gz
        nbr[6, t] = gy + 8 * gz + GOFF
        return 0

    lax.fori_loop(0, 32, place, 0)
    for i in range(GOFF):
        grid[0, i] = jnp.int32(-1)

    def find(k, _):
        q = jnp.int32(-1)
        for t in range(32):
            q = jnp.where(nbr[6, t] == k, t, q)
        grid[0, k] = q
        return 0

    lax.fori_loop(GOFF, GOFF + 48, find, 0)
    for i in range(GOFF + 48, 96):
        grid[0, i] = jnp.int32(-1)

    src = iota((128, 128), 0)
    dst = iota((128, 128), 1)
    g = dst // 32
    i = lax.rem(dst, 32) // 2
    base = jnp.where(g == 0, 0, jnp.where(g == 1, 48, jnp.where(g == 2, 64, 80)))
    spread = ones_where(src == base + i)
    sub = iota((32, 128), 0)
    l1 = iota((1, 128), 1)
    want = jnp.zeros((32, 128), I32)
    code = jnp.zeros((32, 128), I32)
    codes = jnp.full((1, 128), -99, I32)
    for i in range(NP):
        for p in range(2):
            k = NP * p + i
            want = jnp.where(sub == k, ids[0, 2 * i + p], want)
            code = jnp.where(sub == k, nbr[6, 2 * i + p], code)
            codes = jnp.where(l1 == k, nbr[6, 2 * i + p], codes)
    want = want.astype(F32)
    own.wait()
    for c in one:
        c.wait()

    lane = iota((8, 128), 1)

    def place_coarse(j, _):
        for p in range(2):
            gy = nbr[4, 2 * j + p]
            gz = nbr[5, 2 * j + p]
            a = 2 * (gz + 1)
            r0 = pltpu.roll(ba[a, 8:16, :], (128 - 8 * gy) & 127, 1)
            r1 = pltpu.roll(ba[a + 1, 8:16, :], (136 - 8 * gy) & 127, 1)
            r2 = pltpu.roll(ba[2 * gz + 1, 24:32, :], (176 - 16 * gy) & 127, 1)
            r3 = pltpu.roll(ba[2 * gz + 4, 24:32, :], (192 - 16 * gy) & 127, 1)
            cg[NP * p + j] = jnp.where(lane < 64, jnp.where((lane & 8) == 0, r0, r1), jnp.where(lane < 80, r2, r3))
        return 0

    lax.fori_loop(0, NP, place_coarse, 0, unroll=4)
    cg[...] = dot3(cg[...].reshape(256, 128), spread).reshape(32, 8, 128)
    packs = [
        jnp.concatenate([ba[:, k, :], ba[:, 16 + k, :]], axis=0) for k in range(10)
    ]
    data = jnp.concatenate(packs, axis=1)
    group = iota((32, 128), 1) // 32
    near = []
    absent = jnp.zeros((32, 128), F32)
    for g, step in enumerate((-1, 1, -8, 8)):
        hit = codes == code + step
        near.append(ones_where(hit)[:, 0:32])
        some = jnp.sum(jnp.where(hit, 1.0, 0.0), axis=1, keepdims=True)
        absent = jnp.where(group == g, 1.0 - some, absent)
    near = dot3_left(jnp.concatenate(near, axis=0), data)
    theirs = []
    mine = []
    low = (group & 1) == 0
    for v in range(5):
        both = []
        for xr in range(2):
            k = 128 * (5 * xr + v)
            n = [near[32 * g : 32 * g + 32, k : k + 128] for g in range(4)]
            n = jnp.where(group == 0, n[0], jnp.where(group == 1, n[1], jnp.where(group == 2, n[2], n[3])))
            both.append(jnp.where(absent > 0.5, cg[:, 2 + v, :], n))
        theirs.append(jnp.concatenate(both, axis=0))
        both = [jnp.where(low, pltpu.roll(packs[5 * xr + v], 96, 1), pltpu.roll(packs[5 * xr + v], 32, 1)) for xr in range(2)]
        mine.append(jnp.concatenate(both, axis=0))
    g1 = iota((64, 128), 1)
    low = ((g1 // 32) & 1) == 0
    isy = g1 < 64

    def face_flux(q):
        r, pr, c = state(q)
        mn = jnp.where(isy, q[2], q[3])
        u = mn * r
        py = jnp.where(isy, pr, 0.0)
        f = [mn, q[1] * u, q[2] * u + py, q[3] * u + (pr - py), (q[4] + pr) * u]
        return f, jnp.abs(u) + c

    ql = [jnp.where(low, theirs[v], mine[v]) for v in range(5)]
    qr = [jnp.where(low, mine[v], theirs[v]) for v in range(5)]
    fl, al = face_flux(ql)
    fr, ar = face_flux(qr)
    f = rusanov(ql, fl, al, qr, fr, ar)
    for v in range(5):
        for p in range(2):
            for xr in range(2):
                a = 32 * xr + 16 * p
                dd[:, p, 5 * xr + v, :] = f[v][a : a + 16]
    sums = jnp.concatenate([f[v][0:32] + f[v][32:64] for v in range(5)], axis=0)
    l16 = iota((16, 128), 1)
    diagonal = l16 == iota((16, 128), 0)
    own_x = [32 + k for k in range(8)] + [15, 31]
    sides = []
    for way in range(2):
        tag = bx[way, :, 5, :]
        data = jnp.concatenate([bx[way, :, v, :] for v in range(5)], axis=1)
        got = []
        for t in range(2):
            tt_ = pltpu.roll(tag, 64, 1) if t else tag
            row = jnp.sum(jnp.where(diagonal, tt_, 0.0), axis=0, keepdims=True)
            got.append(ones_where(want == row)[:, 0:16])
        got = dot3_left(jnp.concatenate(got, axis=0), data)
        theirs = []
        for v in range(5):
            g0 = got[0:32, 128 * v : 128 * v + 128]
            g1 = got[32:64, 128 * v : 128 * v + 128]
            a = g0[0:16] + pltpu.roll(g1[0:16], 64, 1)
            b = pltpu.roll(g0[16:32], 64, 1) + g1[16:32]
            t = jnp.where(l16 < 64, a, b)
            theirs.append(jnp.where(s == (0 if way == 0 else NS - 1), ba[:, own_x[5 * way + v], :], t))
        sides.append(theirs)
    mine = [jnp.concatenate([ba[:, own_x[v], :], ba[:, own_x[5 + v], :]], axis=0) for v in range(5)]
    theirs = [jnp.concatenate([sides[0][v], sides[1][v]], axis=0) for v in range(5)]
    low = iota((32, 128), 0) < 16
    ql = [jnp.where(low, theirs[v], mine[v]) for v in range(5)]
    qr = [jnp.where(low, mine[v], theirs[v]) for v in range(5)]
    fl, al = flux(ql, state(ql), 0)
    fr, ar = flux(qr, state(qr), 0)
    f = rusanov(ql, fl, al, qr, fr, ar)
    fx = [jnp.where(low, -t, t) for t in f]
    for v in range(5):
        for way in range(2):
            dd[:, way, 10 + v, :] = fx[v][16 * way : 16 * way + 16]
    dd[:, 0, 15, :] = jnp.zeros((16, 128), F32)
    dd[:, 1, 15, :] = jnp.zeros((16, 128), F32)

    late = []
    for d in range(1, NP):
        late.append(copy(S_G + d - 1, dd.at[peer[d]], og.at[me], (s, peer[d])))
        late[-1].start()
    own = pltpu.make_async_copy(dd.at[me], og.at[me], ls.at[6])
    own.start()

    src = iota((128, 256), 0)
    dst = iota((128, 256), 1)
    g = src // 32
    i = lax.rem(src, 32) // 2
    zz = 8 * (dst // 128) + 7 - lax.rem(dst, 128) // 16
    yy = lax.rem(dst, 16)
    far = 15 * (g & 1)
    hit = (zz == jnp.where(g < 2, i, far)) & (yy == jnp.where(g < 2, far, i))
    sign = jnp.where((g & 1) == 0, -1.0, 1.0)
    mean_of = jnp.where(hit, sign, 0.0).astype(BF16)
    src = iota((128, 128), 0)
    dst = iota((128, 128), 1)
    g = src // 32
    i = lax.rem(src, 32) // 2
    z_at = 64 * (i // 8) + 7 - lax.rem(i, 8)
    at = jnp.where(g == 0, z_at, jnp.where(g == 1, z_at + 17, jnp.where(g == 2, 96 + i, 32 + i)))
    reflux = ones_where(dst == at)
    low = ((l1 & 63) < 8) | (l1 >= 96)
    coef = jnp.where(low, -0.05, 0.05).astype(F32) * 0.25
    fix = dot3(sums, mean_of) * -0.0125
    refl = dot3(sums, reflux) * coef
    l32 = iota((32, 128), 1)
    yr = [jnp.zeros((32, 128), F32)] * 2
    zr = [jnp.zeros((32, 128), F32)] * 2
    for v in range(5):
        w = refl[32 * v : 32 * v + 32]
        for h in range(2):
            cc[:, h, v, :] = fix[32 * v : 32 * v + 32, 128 * h : 128 * h + 128]
            yr[h] = jnp.where((l32 >= 25 * v) & (l32 < 25 * v + 25), moved(w, 25 * v - 64 * h), yr[h])
            zr[h] = jnp.where(l32 // 16 == 4 - v, moved(w, 16 * (4 - v) - 64 * h - 32), zr[h])
    for h in range(2):
        cc[:, h, 5, :] = moved(yr[h], -32)
        cc[:, h, 6, :] = moved(zr[h], 48)
        cc[:, h, 7, :] = jnp.zeros((32, 128), F32)
    src = iota((128, 128), 0)
    dst = iota((128, 128), 1)
    sums = jnp.concatenate(fx, axis=0)
    for p in range(2):
        m = dot3(sums, ones_where((src // 64 == p) & ((src & 31) // 2 == (dst & 15)))) * -0.0125
        for v in range(5):
            xt[:, p, v, :] = m[32 * v : 32 * v + 32]
        for v in range(5, 8):
            xt[:, p, v, :] = jnp.zeros((32, 128), F32)
    own_av.wait()
    for c in early:
        c.wait()

    def turn(i, _):
        for p in range(2):
            gy = nbr[4, 2 * i + p]
            for h in range(2):
                k = 10 * p + 5 * h
                t = jnp.concatenate([bb[i, k : k + 5, :], jnp.zeros((3, 128), F32)], axis=0)
                tt[i, p, h] = pltpu.roll(t + cc[NP * p + i, h], (16 * gy + 32) & 127, 1)
        return 0

    lax.fori_loop(0, NP, turn, 0, unroll=4)
    lane = iota((8, 128), 1)
    sub = iota((8, 128), 0)
    block = lane // 16
    ring = (block + sub) & 7
    slope = lane + sub - 7
    def expand_to(j):
        h = lax.rem(j, 2)
        r = j // 2
        far = r - 2 + 2 * h
        acc = [jnp.zeros((8, 128), F32)] * 5
        accy = [jnp.zeros((8, 128), F32)] * 5
        accz = jnp.zeros((8, 128), F32)
        covered = jnp.zeros((8, 128), F32)
        side = [jnp.zeros((8, 128), F32)] * 2
        for gy in range(6):
            a = grid[0, gy + 8 * (r - 1) + GOFF]
            b = grid[0, gy + 8 * far + GOFF]
            a0 = jnp.maximum(a, 0)
            b0 = jnp.maximum(b, 0)
            t = tt[a0 // 2, a0 & 1, h]
            zt = tt[b0 // 2, b0 & 1, h, 6:7, :]
            for way in range(2):
                side[way] = jnp.where((block == gy + 1) & (a >= 0), xt[NP * way + a0 // 2, a0 & 1], side[way])
            covered = jnp.where((block == gy + 1) & (a >= 0), 1.0, covered)
            ina = (ring == gy + 1) & (a >= 0)
            accz = jnp.where((ring == gy + 1) & (b >= 0), zt, accz)
            for v in range(5):
                acc[v] = jnp.where(ina, t[v : v + 1], acc[v])
                off = (slope - 16 * gy - 25 * v) & 127
                accy[v] = jnp.where(((off == 0) | (off == 17)) & (a >= 0), t[5:6], accy[v])
        accz = pltpu.roll(accz, 0, 1, stride=16, stride_axis=0)
        for v in range(5):
            val = pltpu.roll(acc[v], 0, 1, stride=16, stride_axis=0)
            add = moved(pltpu.roll(accy[v], 0, 1, stride=1, stride_axis=0), 8 - 25 * v)
            add = add + jnp.where(sub == 7 * h, accz[v : v + 1], 0.0)
            ee[j, v] = jnp.where(covered > 0, val, add)
        se[j, 0] = side[0]
        se[j, 1] = side[1]

    def expanded(d):
        return copy(S_E + d - 1, ee.at[peer[d]], oe.at[me], (s, peer[d]))

    def sided(d):
        return copy(S_S + d - 1, se.at[peer[d]], so.at[lax.rem(me, 8)], (s, peer[d]))

    def takes(j):
        return (j > 0) & (j < NP - 1)

    def takes_side(j, m):
        return (j > 1) & (j < NP - 2) & (lax.rem(j, 2) == m // 8)

    order = [*range(1, NP), 0]
    for b in range(0, NP, 4):
        for d in order[b : b + 4]:
            expand_to(peer[d])
        for d in order[b : b + 4]:
            if d == 0:
                continue

            @pl.when(takes(peer[d]))
            def _():
                expanded(d).start()

            @pl.when(takes_side(peer[d], me))
            def _():
                sided(d).start()

    own_ee = pltpu.make_async_copy(ee.at[me], oe.at[me], ls.at[7])
    own_se = pltpu.make_async_copy(se.at[me], so.at[lax.rem(me, 8)], ls.at[0])

    @pl.when(takes(me))
    def _():
        own_ee.start()

    @pl.when(takes_side(me, me))
    def _():
        own_se.start()

    @pl.when(jnp.logical_not(takes(me)))
    def _():
        oe[...] = jnp.zeros((16, 5, 8, 128), F32)

    @pl.when((me < 2) | (me >= NP - 2))
    def _():
        so[...] = jnp.zeros((8, 2, 8, 128), F32)

    for c in two:
        c.wait()
    mid = provisional(s, me, cb, oz, ocx, grid, prov)
    src = iota((128, 1024), 0)
    dst = iota((128, 1024), 1)
    g = src // 32
    i = lax.rem(src, 32)
    at = jnp.where(g == 0, 32 * i, jnp.where(g == 1, 32 * i + 31, jnp.where(g == 2, i, 992 + i)))
    sign = jnp.where((g & 1) == 0, -1.0, 1.0)
    expand = jnp.where(dst == at, sign, 0.0).astype(BF16)
    own.wait()
    for c in late:
        c.wait()
    l5 = iota((5, 128), 1)
    for way in range(2):
        for j in range(8):
            e = og[2 * j, way, 10:15, :]
            o = og[2 * j + 1, way, 10:15, :]
            cut = slice(128 * j, 128 * j + 128)
            xg[:, way, cut] = jnp.where(l5 < 64, e, pltpu.roll(o, 64, 1))
            xg[:, 2 + way, cut] = jnp.where(l5 < 64, pltpu.roll(e, 64, 1), o)
    for p in range(2):
        for v in range(5):
            for xr in range(2):
                bf[pl.ds(32 * v + xr, 16, 2), :] = og[:, p, 5 * xr + v, :]
        m = dot3(bf[...], expand)
        for v in range(5):
            fs[v, p] = fs[v, p] - 0.1 * m[32 * v : 32 * v + 32]
            for way, x in ((0, 0), (1, 31)):
                fs[v, p, x : x + 1, :] = fs[v, p, x : x + 1, :] - 0.1 * xg[v, 2 * p + way : 2 * p + way + 1, :]

    @pl.when(takes(me))
    def _():
        own_ee.wait()
        for d in range(1, NP):
            expanded(d).wait_recv()

    @pl.when(takes_side(me, me))
    def _():
        own_se.wait()

    for d in range(1, NP):
        @pl.when(takes(peer[d]))
        def _():
            expanded(d).wait_send()

        @pl.when(takes_side(peer[d], me))
        def _():
            sided(d).wait_send()

        @pl.when(takes_side(me, source[d]))
        def _():
            sided(d).wait_recv()

    for x in range(16):
        for v in range(5):
            e = oe[x, v]
            if x in (0, 15):
                e = e + so[:, x // 15, v, :]
            prov[v, x] = jnp.where(mid > 0, e, prov[v, x] + e)


def copy_kernel(a, b, a_out, b_out, sems):
    n = a.shape[0]
    copies = []
    for v in range(n):
        copies.append(pltpu.make_async_copy(b.at[v, 0], b_out.at[v, 0], sems.at[n + v]))
        copies.append(pltpu.make_async_copy(b.at[v, 1], b_out.at[v, 1], sems.at[2 * n + v]))
        copies.append(pltpu.make_async_copy(a.at[v], a_out.at[v], sems.at[v]))
    for c in copies:
        c.start()
    for c in copies:
        c.wait()


def vm():
    return pl.BlockSpec(memory_space=pltpu.VMEM)


def hb():
    return pl.BlockSpec(memory_space=pltpu.HBM)


def sds(*shape, dtype=F32):
    return jax.ShapeDtypeStruct(shape, dtype)


def buf(*shape):
    return pltpu.VMEM(shape, F32)


LIMIT = 48 << 20


def pin(x):
    return pltpu.with_memory_space_constraint(x, pltpu.HBM)


def local(coarse, fine, columns, patch_ids):
    fo, co = pl.pallas_call(
        step_kernel,
        out_shape=(sds(5, 2, 32, 1024), sds(5, 16, 8, 128)),
        in_specs=[hb()] * 4,
        out_specs=(vm(), vm()),
        scratch_shapes=[
            pltpu.SMEM((1, 32), I32),
            pltpu.SMEM((2, 32), I32),
            pltpu.SMEM((7, 32), I32),
            pltpu.SMEM((1, 96), I32),
            buf(5, 2, 32, 1024),
            buf(5, 16, 8, 128),
            buf(16, 40, 128),
            buf(2, 16, 8, 128),
            buf(2, 5, 16, 128),
            buf(8, 80, 128),
            buf(320, 128),
            buf(16, 40, 128),
            buf(2, 16, 8, 128),
            buf(32, 8, 128),
            buf(16, 2, 16, 128),
            buf(16, 2, 16, 128),
            buf(2, 5, 16, 128),
            buf(2, 5, 8, 128),
            buf(160, 128),
            buf(5, 4, 1024),
            buf(16, 24, 128),
            buf(16, 24, 128),
            buf(32, 2, 8, 128),
            buf(32, 2, 8, 128),
            buf(16, 2, 2, 8, 128),
            buf(16, 5, 8, 128),
            buf(16, 5, 8, 128),
            buf(16, 2, 8, 128),
            buf(8, 2, 8, 128),
            buf(2, 160, 128),
            buf(5, 32, 1024),
            pltpu.SemaphoreType.DMA((N_SEM,)),
            pltpu.SemaphoreType.DMA((N_SEM,)),
            pltpu.SemaphoreType.DMA((8,)),
        ],
        compiler_params=pltpu.CompilerParams(collective_id=0, has_side_effects=True, vmem_limit_bytes=LIMIT),
        name="step",
    )(pin(fine), pin(coarse), pin(patch_ids), pin(columns.T))
    return pl.pallas_call(
        copy_kernel,
        out_shape=(sds(5, 16, 8, 128), sds(5, 2, 32, 1024)),
        in_specs=[pl.BlockSpec(memory_space=pl.ANY)] * 2,
        out_specs=(hb(), hb()),
        scratch_shapes=[pltpu.SemaphoreType.DMA((15,))],
        compiler_params=pltpu.CompilerParams(vmem_limit_bytes=LIMIT),
        name="copy_out",
    )(co, fo)


def solution(mesh):
    return jax.shard_map(
        local,
        mesh=mesh,
        in_specs=(
            P(None, "slab", "patch", None),
            P(None, ("slab", "patch"), None, None),
            P(),
            P("slab", None),
        ),
        out_specs=(P(None, "slab", "patch", None), P(None, ("slab", "patch"), None, None)),
        check_vma=False,
    )
```

```python
import jax
import jax.numpy as jnp
from jax import lax
from jax.experimental import pallas as pl
from jax.experimental.pallas import tpu as pltpu
from jax.sharding import PartitionSpec as P

F32 = jnp.float32
BF16 = jnp.bfloat16
I32 = jnp.int32
MESH = pl.DeviceIdType.MESH
NS = 8
NP = 16
GOFF = 16


def iota(shape, dim):
    return lax.broadcasted_iota(I32, shape, dim)


def dot3(x, m):
    hi = x.astype(BF16)
    r = x - hi.astype(F32)
    mid = r.astype(BF16)
    lo = (r - mid.astype(F32)).astype(BF16)
    n = x.shape[0]
    y = jnp.dot(jnp.concatenate([hi, mid, lo], axis=0), m, preferred_element_type=F32)
    return y[0:n] + (y[n : 2 * n] + y[2 * n : 3 * n])


def dot3_left(m, x):
    hi = x.astype(BF16)
    r = x - hi.astype(F32)
    mid = r.astype(BF16)
    lo = (r - mid.astype(F32)).astype(BF16)
    d = lambda a: jnp.dot(m, a, preferred_element_type=F32)
    return d(hi) + (d(mid) + d(lo))


def moved(x, k):
    return pltpu.roll(x, k % 128, 1) if k % 128 else x


def ones_where(c):
    return jnp.where(c, 1.0, 0.0).astype(BF16)


def state(q):
    r = 1.0 / q[0]
    p = 0.4 * (q[4] - 0.5 * ((q[1] * q[1] + q[2] * q[2] + q[3] * q[3]) * r))
    c = jnp.sqrt(1.4 * p * r)
    return r, p, c


def flux(q, s, d):
    r, p, c = s
    u = q[1 + d] * r
    f = [q[1 + d], q[1] * u, q[2] * u, q[3] * u, (q[4] + p) * u]
    f[1 + d] = f[1 + d] + p
    return f, jnp.abs(u) + c


def rusanov(ql, fl, al, qr, fr, ar):
    a = 0.5 * jnp.maximum(al, ar)
    return [0.5 * (fl[v] + fr[v]) - a * (qr[v] - ql[v]) for v in range(5)]


def provisional(s, me, coarse, oz, ocx, grid, prov):
    r = me // 2
    h = lax.rem(me, 2)
    lane = iota((8, 128), 1)
    sub = iota((8, 128), 0)
    blocks = lane // 16

    def cover(row):
        m = jnp.zeros((8, 128), F32)
        for gy in range(6):
            m = jnp.where((blocks == gy + 1) & (grid[0, gy + 8 * (row - 1) + GOFF] >= 0), 1.0, m)
        return m

    mid = cover(r)
    below = jnp.where(h == 0, cover(r - 1), mid)
    above = jnp.where(h == 1, cover(r + 1), mid)
    free = 1.0 - mid
    fup = free * (1.0 - pltpu.roll(mid, 127, 1))
    flo = free * (1.0 - pltpu.roll(mid, 1, 1))
    zlo = free * (1.0 - jnp.where(sub == 0, below, mid))
    zhi = free * (1.0 - jnp.where(sub == 7, above, mid))

    def cells(x):
        q = [coarse[v, x] for v in range(5)]
        st = state(q)
        return q, st, flux(q, st, 0)

    def face(a, b):
        return rusanov(a[0], a[2][0], a[2][1], b[0], b[2][0], b[2][1])

    first = cells(0)
    q = [jnp.where(s == 0, coarse[v, 0], ocx[0, v]) for v in range(5)]
    st = state(q)
    lower = face((q, st, flux(q, st, 0)), first)
    here = first
    for x in range(16):
        if x < 15:
            there = cells(x + 1)
        else:
            q = [jnp.where(s == NS - 1, coarse[v, 15], ocx[1, v]) for v in range(5)]
            st = state(q)
            there = (q, st, flux(q, st, 0))
        upper = face(here, there)
        q, st, _ = here
        change = [(upper[v] - lower[v]) * free for v in range(5)]
        row = slice(x, x + 1)
        zn = [jnp.where(sub == 7, jnp.where(me == NP - 1, q[v], oz[1, v, row, :]), pltpu.roll(q[v], 7, 0)) for v in range(5)]
        zb = [jnp.where(sub == 0, jnp.where(me == 0, q[v], oz[0, v, row, :]), pltpu.roll(q[v], 1, 0)) for v in range(5)]
        f, a = flux(q, st, 2)
        fn, an = flux(zn, state(zn), 2)
        fb, ab = flux(zb, state(zb), 2)
        up = rusanov(q, f, a, zn, fn, an)
        lo = rusanov(zb, fb, ab, q, f, a)
        change = [change[v] + (up[v] * zhi - lo[v] * zlo) for v in range(5)]
        f, a = flux(q, st, 1)
        nxt = lambda t: jnp.where(lane == 127, t, pltpu.roll(t, 127, 1))
        prv = lambda t: jnp.where(lane == 0, t, pltpu.roll(t, 1, 1))
        up = rusanov(q, f, a, [nxt(t) for t in q], [nxt(t) for t in f], nxt(a))
        lo = rusanov([prv(t) for t in q], [prv(t) for t in f], prv(a), q, f, a)
        for v in range(5):
            prov[v, x] = q[v] - 0.05 * (change[v] + (up[v] * fup - lo[v] * flo))
        here = there
        lower = upper
    return mid


N1 = NP - 1
OFFSETS = sorted(
    ((dx, dz) for dx in range(4) for dz in range(4)),
    key=lambda o: (o != (0, 0), -(min(o[0], 4 - o[0]) + min(o[1], 4 - o[1]))),
)
S_X = N1
S_H = S_X + 2 * NP
S_G = S_H + 4
S_A = S_G + N1
S_E = S_A + N1
S_S = S_E + N1
N_SEM = S_S + N1


def step_kernel(
    fine, coarse, ids_in, cols_in, fs, prov,
    ids, cols, nbr, grid, fb, cb, a1, x1, rz, ct, pk, ba, bx, cg, dd, og, oz, ocx,
    bf, xg, av, bb, cc, xt, tt, ee, oe, se, so, big, chg, ss, rs, ls,
):
    s = lax.axis_index("slab")
    me = lax.axis_index("patch")
    half = lax.rem(me, 2)
    up = lax.rem(s + 1, NS)
    down = lax.rem(s + NS - 1, NS)
    x, z = me // 4, lax.rem(me, 4)
    peer = [lax.rem(x + dx, 4) * 4 + lax.rem(z + dz, 4) for dx, dz in OFFSETS]
    source = [lax.rem(x + 4 - dx, 4) * 4 + lax.rem(z + 4 - dz, 4) for dx, dz in OFFSETS]
    loads = [pltpu.make_async_copy(fine.at[v], fb.at[v], ls.at[v]) for v in range(5)]
    loads.append(pltpu.make_async_copy(coarse, cb, ls.at[5]))
    loads.append(pltpu.make_async_copy(ids_in, ids, ls.at[6]))
    loads.append(pltpu.make_async_copy(cols_in, cols, ls.at[7]))
    barrier = pltpu.get_barrier_semaphore()
    for c in loads:
        c.start()
    for d in range(NP):
        if d:
            pl.semaphore_signal(barrier, inc=1, device_id=(s, peer[d]), device_id_type=MESH)
        pl.semaphore_signal(barrier, inc=1, device_id=(up, peer[d]), device_id_type=MESH)
        pl.semaphore_signal(barrier, inc=1, device_id=(down, peer[d]), device_id_type=MESH)

    def copy(k, src, dst, dev):
        return pltpu.make_async_remote_copy(
            src_ref=src, dst_ref=dst, send_sem=ss.at[k], recv_sem=rs.at[k],
            device_id=dev, device_id_type=MESH,
        )

    k = iota((1024, 128), 0)
    c = iota((1024, 128), 1)
    g = c // 32
    i = lax.rem(c, 32)
    want = jnp.where(g == 0, 32 * i + 31, jnp.where(g == 1, 32 * i, jnp.where(g == 2, 992 + i, i)))
    sel = ones_where(k == want)
    for v in range(5):
        loads[v].wait()
    pk[...] = dot3(fb[...].reshape(320, 1024), sel)
    for v in range(5):
        for p in range(2):
            for xr in range(2):
                a1[:, 16 * p + 5 * xr + v, :] = pk[pl.ds(64 * v + 32 * p + xr, 16, 2), :]
    loads[6].wait()
    loads[7].wait()
    lane = iota((5, 128), 1)
    tag = jnp.where(iota((3, 128), 1) < 64, ids[0, 2 * me], ids[0, 2 * me + 1]).astype(F32)
    for d, row in ((0, 0), (1, 31)):
        for j in range(8):
            t0 = fb[:, 0, row, 128 * j : 128 * j + 128]
            t1 = fb[:, 1, row, 128 * j : 128 * j + 128]
            for o, t in (
                (0, jnp.where(lane < 64, t0, pltpu.roll(t1, 64, 1))),
                (1, jnp.where(lane < 64, pltpu.roll(t0, 64, 1), t1)),
            ):
                x1[d, 2 * j + o, 0:5, :] = t
                if d == 0:
                    a1[2 * j + o, 32:37, :] = t
                else:
                    a1[2 * j + o, 37:40, :] = t[0:3]
                    a1[2 * j + o, 15:16, :] = t[3:4]
                    a1[2 * j + o, 31:32, :] = t[4:5]
            x1[d, 2 * j, 5:8, :] = tag
            x1[d, 2 * j + 1, 5:8, :] = tag
    loads[5].wait()
    for v in range(5):
        for z in range(8):
            ct[z, 16 * v : 16 * v + 16, :] = cb[v, :, z, :]
    y = iota((128, 128), 0)
    k = iota((128, 128), 1) // 8
    plane = jnp.where(k < 6, 16 * (k + 1) - 1, jnp.where(k < 12, 16 * (k - 4), -1))
    sel = ones_where(y == plane)
    lane8 = lax.rem(iota((80, 128), 1), 8)
    acc = jnp.zeros((80, 128), F32)
    planes = dot3(ct[...].reshape(640, 128), sel)
    for z in range(8):
        acc = jnp.where(lane8 == z, planes[80 * z : 80 * z + 80], acc)
    first = ct[0]
    last = ct[7]
    own = jnp.where(half == 0, first, last)
    for v in range(5):
        cut = slice(16 * v, 16 * v + 16)
        a1[:, 10 + v, :] = acc[cut]
        a1[:, 26 + v, :] = own[cut]
        rz[0, v] = first[cut]
        rz[1, v] = last[cut]

    pl.semaphore_wait(barrier, 3 * NP - 1)
    one = []
    two = []
    for d in [*range(1, NP), 0]:
        j = peer[d]
        if d:
            one.append(copy(d - 1, a1.at[j], ba.at[me], (s, j)))
            one[-1].start()
        for c in (
            copy(S_X + 2 * d, x1.at[0, j], bx.at[1, me], (down, j)),
            copy(S_X + 2 * d + 1, x1.at[1, j], bx.at[0, me], (up, j)),
        ):
            c.start()
            one.append(c)
    two = [
        copy(S_H, cb.at[:, 0], ocx.at[1], (down, me)),
        copy(S_H + 1, cb.at[:, 15], ocx.at[0], (up, me)),
        copy(S_H + 2, rz.at[1], oz.at[0], (s, lax.rem(me + 1, NP))),
        copy(S_H + 3, rz.at[0], oz.at[1], (s, lax.rem(me + N1, NP))),
    ]
    for c in two:
        c.start()
    own = pltpu.make_async_copy(a1.at[me], ba.at[me], ls.at[6])
    own.start()

    src = iota((1024, 256), 0)
    dst = iota((1024, 256), 1)
    zz = 8 * (dst // 128) + 7 - lax.rem(dst, 128) // 16
    pair = ones_where((src // 64 == zz) & (lax.rem(src, 32) // 2 == lax.rem(dst, 16)))

    def interior(p):
        def along_x(j, _):
            cut = pl.ds(pl.multiple_of(128 * j, 128), 128)
            q = [fb[v, p, :, cut] for v in range(5)]
            f, a = flux(q, state(q), 0)
            nxt = lambda t: pltpu.roll(t, 31, 0)
            hi = rusanov(q, f, a, [nxt(t) for t in q], [nxt(t) for t in f], nxt(a))
            inner = iota((32, 128), 0) < 31
            for v in range(5):
                t = jnp.where(inner, hi[v], 0.0)
                chg[v, :, cut] = t - pltpu.roll(t, 1, 0)
            return 0

        lax.fori_loop(0, 8, along_x, 0)

        def rows(c, _):
            cut = pl.ds(pl.multiple_of(8 * c, 8), 8)
            q = [fb[v, p, cut, :] for v in range(5)]
            st = state(q)
            l8 = iota((8, 1024), 1)
            change = [chg[v, cut, :] for v in range(5)]
            for way, shift, inner in ((2, 32, l8 < 992), (1, 1, (l8 & 31) < 31)):
                f, a = flux(q, st, way)
                nxt = lambda t: pltpu.roll(t, 1024 - shift, 1)
                hi = rusanov(q, f, a, [nxt(t) for t in q], [nxt(t) for t in f], nxt(a))
                for v in range(5):
                    t = jnp.where(inner, hi[v], 0.0)
                    change[v] = change[v] + (t - pltpu.roll(t, shift, 1))
            for v in range(5):
                fs[v, p, cut, :] = q[v] - 0.1 * change[v]
            return 0

        lax.fori_loop(0, 4, rows, 0)
        m = dot3(fs[:, p].reshape(160, 1024), pair)
        for h in range(2):
            big[h] = m[:, 128 * h : 128 * h + 128]
            for v in range(5):
                a = 32 * v
                av[:, 10 * p + 5 * h + v, :] = 0.125 * (big[h, pl.ds(a, 16, 2), :] + big[h, pl.ds(a + 1, 16, 2), :])
        for k in range(2):
            av[:, 20 + 2 * p + k, :] = jnp.zeros((16, 128), F32)

    interior(0)
    interior(1)
    early = []
    for d in range(1, NP):
        early.append(copy(S_A + d - 1, av.at[peer[d]], bb.at[me], (s, peer[d])))
        early[-1].start()
    own_av = pltpu.make_async_copy(av.at[me], bb.at[me], ls.at[7])
    own_av.start()
    def place(t, _):
        n = ids[0, t]
        gy = cols[0, n]
        gz = cols[1, n]
        nbr[4, t] = gy
        nbr[5, t] = gz
        nbr[6, t] = gy + 8 * gz + GOFF
        return 0

    lax.fori_loop(0, 32, place, 0)
    src = iota((128, 128), 0)
    dst = iota((128, 128), 1)
    g = dst // 32
    i = lax.rem(dst, 32) // 2
    base = jnp.where(g == 0, 0, jnp.where(g == 1, 48, jnp.where(g == 2, 64, 80)))
    spread = ones_where(src == base + i)
    sub = iota((32, 128), 0)
    l1 = iota((1, 128), 1)
    want = jnp.zeros((32, 128), I32)
    code = jnp.zeros((32, 128), I32)
    codes = jnp.full((1, 128), -99, I32)
    for i in range(NP):
        for p in range(2):
            k = NP * p + i
            want = jnp.where(sub == k, ids[0, 2 * i + p], want)
            code = jnp.where(sub == k, nbr[6, 2 * i + p], code)
            codes = jnp.where(l1 == k, nbr[6, 2 * i + p], codes)
    want = want.astype(F32)
    own.wait()
    for c in one:
        c.wait()

    lane = iota((8, 128), 1)

    def place_coarse(j, _):
        for p in range(2):
            gy = nbr[4, 2 * j + p]
            gz = nbr[5, 2 * j + p]
            a = 2 * (gz + 1)
            r0 = pltpu.roll(ba[a, 8:16, :], (128 - 8 * gy) & 127, 1)
            r1 = pltpu.roll(ba[a + 1, 8:16, :], (136 - 8 * gy) & 127, 1)
            r2 = pltpu.roll(ba[2 * gz + 1, 24:32, :], (176 - 16 * gy) & 127, 1)
            r3 = pltpu.roll(ba[2 * gz + 4, 24:32, :], (192 - 16 * gy) & 127, 1)
            cg[NP * p + j] = jnp.where(lane < 64, jnp.where((lane & 8) == 0, r0, r1), jnp.where(lane < 80, r2, r3))
        return 0

    lax.fori_loop(0, NP, place_coarse, 0, unroll=4)
    cg[...] = dot3(cg[...].reshape(256, 128), spread).reshape(32, 8, 128)
    packs = [
        jnp.concatenate([ba[:, k, :], ba[:, 16 + k, :]], axis=0) for k in range(10)
    ]
    data = jnp.concatenate(packs, axis=1)
    group = iota((32, 128), 1) // 32
    near = []
    absent = jnp.zeros((32, 128), F32)
    for g, step in enumerate((-1, 1, -8, 8)):
        hit = codes == code + step
        near.append(ones_where(hit)[:, 0:32])
        some = jnp.sum(jnp.where(hit, 1.0, 0.0), axis=1, keepdims=True)
        absent = jnp.where(group == g, 1.0 - some, absent)
    near = dot3_left(jnp.concatenate(near, axis=0), data)
    theirs = []
    mine = []
    low = (group & 1) == 0
    for v in range(5):
        both = []
        for xr in range(2):
            k = 128 * (5 * xr + v)
            n = [near[32 * g : 32 * g + 32, k : k + 128] for g in range(4)]
            n = jnp.where(group == 0, n[0], jnp.where(group == 1, n[1], jnp.where(group == 2, n[2], n[3])))
            both.append(jnp.where(absent > 0.5, cg[:, 2 + v, :], n))
        theirs.append(jnp.concatenate(both, axis=0))
        both = [jnp.where(low, pltpu.roll(packs[5 * xr + v], 96, 1), pltpu.roll(packs[5 * xr + v], 32, 1)) for xr in range(2)]
        mine.append(jnp.concatenate(both, axis=0))
    g1 = iota((64, 128), 1)
    low = ((g1 // 32) & 1) == 0
    isy = g1 < 64

    def face_flux(q):
        r, pr, c = state(q)
        mn = jnp.where(isy, q[2], q[3])
        u = mn * r
        py = jnp.where(isy, pr, 0.0)
        f = [mn, q[1] * u, q[2] * u + py, q[3] * u + (pr - py), (q[4] + pr) * u]
        return f, jnp.abs(u) + c

    ql = [jnp.where(low, theirs[v], mine[v]) for v in range(5)]
    qr = [jnp.where(low, mine[v], theirs[v]) for v in range(5)]
    fl, al = face_flux(ql)
    fr, ar = face_flux(qr)
    f = rusanov(ql, fl, al, qr, fr, ar)
    for v in range(5):
        for p in range(2):
            for xr in range(2):
                a = 32 * xr + 16 * p
                dd[:, p, 5 * xr + v, :] = f[v][a : a + 16]
    sums = jnp.concatenate([f[v][0:32] + f[v][32:64] for v in range(5)], axis=0)
    l16 = iota((16, 128), 1)
    diagonal = l16 == iota((16, 128), 0)
    own_x = [32 + k for k in range(8)] + [15, 31]
    sides = []
    for way in range(2):
        tag = bx[way, :, 5, :]
        data = jnp.concatenate([bx[way, :, v, :] for v in range(5)], axis=1)
        got = []
        for t in range(2):
            tt_ = pltpu.roll(tag, 64, 1) if t else tag
            row = jnp.sum(jnp.where(diagonal, tt_, 0.0), axis=0, keepdims=True)
            got.append(ones_where(want == row)[:, 0:16])
        got = dot3_left(jnp.concatenate(got, axis=0), data)
        theirs = []
        for v in range(5):
            g0 = got[0:32, 128 * v : 128 * v + 128]
            g1 = got[32:64, 128 * v : 128 * v + 128]
            a = g0[0:16] + pltpu.roll(g1[0:16], 64, 1)
            b = pltpu.roll(g0[16:32], 64, 1) + g1[16:32]
            t = jnp.where(l16 < 64, a, b)
            theirs.append(jnp.where(s == (0 if way == 0 else NS - 1), ba[:, own_x[5 * way + v], :], t))
        sides.append(theirs)
    mine = [jnp.concatenate([ba[:, own_x[v], :], ba[:, own_x[5 + v], :]], axis=0) for v in range(5)]
    theirs = [jnp.concatenate([sides[0][v], sides[1][v]], axis=0) for v in range(5)]
    low = iota((32, 128), 0) < 16
    ql = [jnp.where(low, theirs[v], mine[v]) for v in range(5)]
    qr = [jnp.where(low, mine[v], theirs[v]) for v in range(5)]
    fl, al = flux(ql, state(ql), 0)
    fr, ar = flux(qr, state(qr), 0)
    f = rusanov(ql, fl, al, qr, fr, ar)
    fx = [jnp.where(low, -t, t) for t in f]
    for v in range(5):
        for way in range(2):
            dd[:, way, 10 + v, :] = fx[v][16 * way : 16 * way + 16]
    dd[:, 0, 15, :] = jnp.zeros((16, 128), F32)
    dd[:, 1, 15, :] = jnp.zeros((16, 128), F32)

    late = []
    for d in range(1, NP):
        late.append(copy(S_G + d - 1, dd.at[peer[d]], og.at[me], (s, peer[d])))
        late[-1].start()
    own = pltpu.make_async_copy(dd.at[me], og.at[me], ls.at[6])
    own.start()

    for i in range(GOFF):
        grid[0, i] = jnp.int32(-1)

    def find(k, _):
        q = jnp.int32(-1)
        for t in range(32):
            q = jnp.where(nbr[6, t] == k, t, q)
        grid[0, k] = q
        return 0

    lax.fori_loop(GOFF, GOFF + 48, find, 0)
    for i in range(GOFF + 48, 96):
        grid[0, i] = jnp.int32(-1)

    src = iota((128, 256), 0)
    dst = iota((128, 256), 1)
    g = src // 32
    i = lax.rem(src, 32) // 2
    zz = 8 * (dst // 128) + 7 - lax.rem(dst, 128) // 16
    yy = lax.rem(dst, 16)
    far = 15 * (g & 1)
    hit = (zz == jnp.where(g < 2, i, far)) & (yy == jnp.where(g < 2, far, i))
    sign = jnp.where((g & 1) == 0, -1.0, 1.0)
    mean_of = jnp.where(hit, sign, 0.0).astype(BF16)
    src = iota((128, 128), 0)
    dst = iota((128, 128), 1)
    g = src // 32
    i = lax.rem(src, 32) // 2
    z_at = 64 * (i // 8) + 7 - lax.rem(i, 8)
    at = jnp.where(g == 0, z_at, jnp.where(g == 1, z_at + 17, jnp.where(g == 2, 96 + i, 32 + i)))
    reflux = ones_where(dst == at)
    low = ((l1 & 63) < 8) | (l1 >= 96)
    coef = jnp.where(low, -0.05, 0.05).astype(F32) * 0.25
    fix = dot3(sums, mean_of) * -0.0125
    refl = dot3(sums, reflux) * coef
    l32 = iota((32, 128), 1)
    yr = [jnp.zeros((32, 128), F32)] * 2
    zr = [jnp.zeros((32, 128), F32)] * 2
    for v in range(5):
        w = refl[32 * v : 32 * v + 32]
        for h in range(2):
            cc[:, h, v, :] = fix[32 * v : 32 * v + 32, 128 * h : 128 * h + 128]
            yr[h] = jnp.where((l32 >= 25 * v) & (l32 < 25 * v + 25), moved(w, 25 * v - 64 * h), yr[h])
            zr[h] = jnp.where(l32 // 16 == 4 - v, moved(w, 16 * (4 - v) - 64 * h - 32), zr[h])
    for h in range(2):
        cc[:, h, 5, :] = moved(yr[h], -32)
        cc[:, h, 6, :] = moved(zr[h], 48)
        cc[:, h, 7, :] = jnp.zeros((32, 128), F32)
    src = iota((128, 128), 0)
    dst = iota((128, 128), 1)
    sums = jnp.concatenate(fx, axis=0)
    for p in range(2):
        m = dot3(sums, ones_where((src // 64 == p) & ((src & 31) // 2 == (dst & 15)))) * -0.0125
        for v in range(5):
            xt[:, p, v, :] = m[32 * v : 32 * v + 32]
        for v in range(5, 8):
            xt[:, p, v, :] = jnp.zeros((32, 128), F32)
    own_av.wait()
    for c in early:
        c.wait()

    def turn(i, _):
        for p in range(2):
            gy = nbr[4, 2 * i + p]
            for h in range(2):
                k = 10 * p + 5 * h
                t = jnp.concatenate([bb[i, k : k + 5, :], jnp.zeros((3, 128), F32)], axis=0)
                tt[i, p, h] = pltpu.roll(t + cc[NP * p + i, h], (16 * gy + 32) & 127, 1)
        return 0

    lax.fori_loop(0, NP, turn, 0, unroll=4)
    lane = iota((8, 128), 1)
    sub = iota((8, 128), 0)
    block = lane // 16
    ring = (block + sub) & 7
    slope = lane + sub - 7
    def expand_to(j):
        h = lax.rem(j, 2)
        r = j // 2
        far = r - 2 + 2 * h
        acc = [jnp.zeros((8, 128), F32)] * 5
        accy = [jnp.zeros((8, 128), F32)] * 5
        accz = jnp.zeros((8, 128), F32)
        covered = jnp.zeros((8, 128), F32)
        side = [jnp.zeros((8, 128), F32)] * 2
        for gy in range(6):
            a = grid[0, gy + 8 * (r - 1) + GOFF]
            b = grid[0, gy + 8 * far + GOFF]
            a0 = jnp.maximum(a, 0)
            b0 = jnp.maximum(b, 0)
            t = tt[a0 // 2, a0 & 1, h]
            zt = tt[b0 // 2, b0 & 1, h, 6:7, :]
            for way in range(2):
                side[way] = jnp.where((block == gy + 1) & (a >= 0), xt[NP * way + a0 // 2, a0 & 1], side[way])
            covered = jnp.where((block == gy + 1) & (a >= 0), 1.0, covered)
            ina = (ring == gy + 1) & (a >= 0)
            accz = jnp.where((ring == gy + 1) & (b >= 0), zt, accz)
            for v in range(5):
                acc[v] = jnp.where(ina, t[v : v + 1], acc[v])
                off = (slope - 16 * gy - 25 * v) & 127
                accy[v] = jnp.where(((off == 0) | (off == 17)) & (a >= 0), t[5:6], accy[v])
        accz = pltpu.roll(accz, 0, 1, stride=16, stride_axis=0)
        for v in range(5):
            val = pltpu.roll(acc[v], 0, 1, stride=16, stride_axis=0)
            add = moved(pltpu.roll(accy[v], 0, 1, stride=1, stride_axis=0), 8 - 25 * v)
            add = add + jnp.where(sub == 7 * h, accz[v : v + 1], 0.0)
            ee[j, v] = jnp.where(covered > 0, val, add)
        se[j, 0] = side[0]
        se[j, 1] = side[1]

    def expanded(d):
        return copy(S_E + d - 1, ee.at[peer[d]], oe.at[me], (s, peer[d]))

    def sided(d):
        return copy(S_S + d - 1, se.at[peer[d]], so.at[lax.rem(me, 8)], (s, peer[d]))

    def takes(j):
        return (j > 0) & (j < NP - 1)

    def takes_side(j, m):
        return (j > 1) & (j < NP - 2) & (lax.rem(j, 2) == m // 8)

    order = [*range(1, NP), 0]
    for b in range(0, NP, 4):
        for d in order[b : b + 4]:
            expand_to(peer[d])
        for d in order[b : b + 4]:
            if d == 0:
                continue

            @pl.when(takes(peer[d]))
            def _():
                expanded(d).start()

            @pl.when(takes_side(peer[d], me))
            def _():
                sided(d).start()

    own_ee = pltpu.make_async_copy(ee.at[me], oe.at[me], ls.at[7])
    own_se = pltpu.make_async_copy(se.at[me], so.at[lax.rem(me, 8)], ls.at[0])

    @pl.when(takes(me))
    def _():
        own_ee.start()

    @pl.when(takes_side(me, me))
    def _():
        own_se.start()

    @pl.when(jnp.logical_not(takes(me)))
    def _():
        oe[...] = jnp.zeros((16, 5, 8, 128), F32)

    @pl.when((me < 2) | (me >= NP - 2))
    def _():
        so[...] = jnp.zeros((8, 2, 8, 128), F32)

    for c in two:
        c.wait()
    mid = provisional(s, me, cb, oz, ocx, grid, prov)
    src = iota((128, 1024), 0)
    dst = iota((128, 1024), 1)
    g = src // 32
    i = lax.rem(src, 32)
    at = jnp.where(g == 0, 32 * i, jnp.where(g == 1, 32 * i + 31, jnp.where(g == 2, i, 992 + i)))
    sign = jnp.where((g & 1) == 0, -1.0, 1.0)
    expand = jnp.where(dst == at, sign, 0.0).astype(BF16)
    own.wait()
    for c in late:
        c.wait()
    l5 = iota((5, 128), 1)
    for way in range(2):
        for j in range(8):
            e = og[2 * j, way, 10:15, :]
            o = og[2 * j + 1, way, 10:15, :]
            cut = slice(128 * j, 128 * j + 128)
            xg[:, way, cut] = jnp.where(l5 < 64, e, pltpu.roll(o, 64, 1))
            xg[:, 2 + way, cut] = jnp.where(l5 < 64, pltpu.roll(e, 64, 1), o)
    for p in range(2):
        for v in range(5):
            for xr in range(2):
                bf[pl.ds(32 * v + xr, 16, 2), :] = og[:, p, 5 * xr + v, :]
        m = dot3(bf[...], expand)
        for v in range(5):
            fs[v, p] = fs[v, p] - 0.1 * m[32 * v : 32 * v + 32]
            for way, x in ((0, 0), (1, 31)):
                fs[v, p, x : x + 1, :] = fs[v, p, x : x + 1, :] - 0.1 * xg[v, 2 * p + way : 2 * p + way + 1, :]

    @pl.when(takes(me))
    def _():
        own_ee.wait()
        for d in range(1, NP):
            expanded(d).wait_recv()

    @pl.when(takes_side(me, me))
    def _():
        own_se.wait()

    for d in range(1, NP):
        @pl.when(takes(peer[d]))
        def _():
            expanded(d).wait_send()

        @pl.when(takes_side(peer[d], me))
        def _():
            sided(d).wait_send()

        @pl.when(takes_side(me, source[d]))
        def _():
            sided(d).wait_recv()

    for x in range(16):
        for v in range(5):
            e = oe[x, v]
            if x in (0, 15):
                e = e + so[:, x // 15, v, :]
            prov[v, x] = jnp.where(mid > 0, e, prov[v, x] + e)


def copy_kernel(a, b, a_out, b_out, sems):
    n = a.shape[0]
    copies = []
    for v in range(n):
        copies.append(pltpu.make_async_copy(b.at[v, 0], b_out.at[v, 0], sems.at[n + v]))
        copies.append(pltpu.make_async_copy(b.at[v, 1], b_out.at[v, 1], sems.at[2 * n + v]))
        copies.append(pltpu.make_async_copy(a.at[v], a_out.at[v], sems.at[v]))
    for c in copies:
        c.start()
    for c in copies:
        c.wait()


def vm():
    return pl.BlockSpec(memory_space=pltpu.VMEM)


def hb():
    return pl.BlockSpec(memory_space=pltpu.HBM)


def sds(*shape, dtype=F32):
    return jax.ShapeDtypeStruct(shape, dtype)


def buf(*shape):
    return pltpu.VMEM(shape, F32)


LIMIT = 48 << 20


def pin(x):
    return pltpu.with_memory_space_constraint(x, pltpu.HBM)


def local(coarse, fine, columns, patch_ids):
    fo, co = pl.pallas_call(
        step_kernel,
        out_shape=(sds(5, 2, 32, 1024), sds(5, 16, 8, 128)),
        in_specs=[hb()] * 4,
        out_specs=(vm(), vm()),
        scratch_shapes=[
            pltpu.SMEM((1, 32), I32),
            pltpu.SMEM((2, 32), I32),
            pltpu.SMEM((7, 32), I32),
            pltpu.SMEM((1, 96), I32),
            buf(5, 2, 32, 1024),
            buf(5, 16, 8, 128),
            buf(16, 40, 128),
            buf(2, 16, 8, 128),
            buf(2, 5, 16, 128),
            buf(8, 80, 128),
            buf(320, 128),
            buf(16, 40, 128),
            buf(2, 16, 8, 128),
            buf(32, 8, 128),
            buf(16, 2, 16, 128),
            buf(16, 2, 16, 128),
            buf(2, 5, 16, 128),
            buf(2, 5, 8, 128),
            buf(160, 128),
            buf(5, 4, 1024),
            buf(16, 24, 128),
            buf(16, 24, 128),
            buf(32, 2, 8, 128),
            buf(32, 2, 8, 128),
            buf(16, 2, 2, 8, 128),
            buf(16, 5, 8, 128),
            buf(16, 5, 8, 128),
            buf(16, 2, 8, 128),
            buf(8, 2, 8, 128),
            buf(2, 160, 128),
            buf(5, 32, 1024),
            pltpu.SemaphoreType.DMA((N_SEM,)),
            pltpu.SemaphoreType.DMA((N_SEM,)),
            pltpu.SemaphoreType.DMA((8,)),
        ],
        compiler_params=pltpu.CompilerParams(collective_id=0, has_side_effects=True, vmem_limit_bytes=LIMIT),
        name="step",
    )(pin(fine), pin(coarse), pin(patch_ids), pin(columns.T))
    return pl.pallas_call(
        copy_kernel,
        out_shape=(sds(5, 16, 8, 128), sds(5, 2, 32, 1024)),
        in_specs=[pl.BlockSpec(memory_space=pl.ANY)] * 2,
        out_specs=(hb(), hb()),
        scratch_shapes=[pltpu.SemaphoreType.DMA((15,))],
        compiler_params=pltpu.CompilerParams(vmem_limit_bytes=LIMIT),
        name="copy_out",
    )(co, fo)


def solution(mesh):
    return jax.shard_map(
        local,
        mesh=mesh,
        in_specs=(
            P(None, "slab", "patch", None),
            P(None, ("slab", "patch"), None, None),
            P(),
            P("slab", None),
        ),
        out_specs=(P(None, "slab", "patch", None), P(None, ("slab", "patch"), None, None)),
        check_vma=False,
    )
```
